32 devices in a mesh: section: 2 (over core), seq: 4 (over z), head: 4 (over y, x).
Axes of the slice: x: 2, y: 2, z: 4, core: 2. Of those that a mesh axis runs over, the one named last changes fastest.
Arguments:
- tokens: bfloat16 [2, 1024, 1536], P(None, 'seq'), may hold values from -6 to 6
- cotangent: bfloat16 [2, 1024, 1536], P(None, 'seq'), may hold values from -6 to 6
- norm_gain: float32 [2, 1536], P('section'), may hold values from 0.5 to 1.5
- w_xz: bfloat16 [2, 1536, 2, 3072], P('section', None, None, 'head'), may hold values from -0.15625 to 0.15625
- w_bc: bfloat16 [2, 1536, 256], P('section'), may hold values from -0.15625 to 0.15625
- w_dt: bfloat16 [2, 1536, 48], P('section', None, 'head'), may hold values from -0.15625 to 0.15625
- conv_x: float32 [2, 5, 3072], P('section', None, 'head'), may hold values from -0.5 to 0.5
- conv_bc: float32 [2, 5, 256], P('section'), may hold values from -0.5 to 0.5
- head_params: float32 [2, 3, 48], P('section', None, 'head'), may hold values from -7 to 1.75
- out_gain: float32 [2, 3072], P('section', 'head'), may hold values from 0.5 to 1.5
- w_out: bfloat16 [2, 3072, 1536], P('section', 'head'), may hold values from -0.109375 to 0.109375
Outputs:
- section_ends: float32 [2, 2, 1024, 1536], P('section', None, ('seq', 'head'))
- g_norm_gain: float32 [2, 1536], P('section')
- g_w_xz: float32 [2, 1536, 2, 3072], P('section', 'seq', None, 'head')
- g_w_bc: float32 [2, 1536, 256], P('section', 'seq')
- g_w_dt: float32 [2, 1536, 48], P('section', 'seq', 'head')
- g_conv_x: float32 [2, 5, 3072], P('section', None, 'head')
- g_conv_bc: float32 [2, 5, 256], P('section')
- g_head_params: float32 [2, 3, 48], P('section', None, 'head')
- g_out_gain: float32 [2, 3072], P('section', 'head')
- g_w_out: float32 [2, 3072, 1536], P('section', 'head', 'seq')
The draws below stay inside these ranges and needn't reach their ends.
All inputs are finite; a program needn't handle non-finite values.
Results may differ from the reference program's by a relative error of at most 0.018.
Values may be sent and summed in bfloat16 or wider, within the bound.
A program may use at most 192 MiB of HBM per device.

```python
import jax
import jax.numpy as jnp
from jax import lax

D = 1536
HEADS = 48
STATE = 128
CONV = 4
BLOCK = 256
MB = 2
INNER = 3072
LAYERS = 2
LEN = 1024


def draw_head_params(key, part):
    key = jax.random.fold_in(key, 11)
    lower = jnp.array([-7.0, -4.0, 0.5], jnp.float32)
    upper = jnp.array([-2.0, 0.5, 1.5], jnp.float32)
    unit = jax.random.uniform(key, (LAYERS, 3, HEADS), jnp.float32)
    return lower[None, :, None] + (upper - lower)[None, :, None] * unit


def levels(own_key, dims, cuts, smallest, largest):
    gain = 1.0
    for dim, shards_of in cuts:
        heights = jax.random.uniform(jax.random.fold_in(jax.random.fold_in(own_key, 6), dim), (shards_of,), jnp.float32, smallest / len(cuts), largest / len(cuts))
        gain = gain * jnp.repeat(jnp.exp(heights), dims[dim] // shards_of).reshape((-1,) + (1,) * (len(dims) - 1 - dim))
    return gain


def bell_draw(key, dims, width, most, shards=(), kind=jnp.bfloat16):
    drawn = width * jax.random.normal(key, dims, jnp.float32)
    if shards:
        drawn = drawn * levels(key, dims, shards, -0.22, 0.18)
    return jnp.clip(drawn, -most, most).astype(kind)


def setup_inputs(seed: int = 0) -> dict:
    key_list = jax.random.split(jax.random.key(seed), 12)
    return {
        "tokens": bell_draw(key_list[0], (MB, LEN, D), 1.0, 6.0, ((1, 4),)),
        "cotangent": bell_draw(key_list[1], (MB, LEN, D), 1.0, 6.0, ((1, 4),)),
        "norm_gain": jnp.clip(1.0 + 0.1 * jax.random.normal(key_list[2], (LAYERS, D), jnp.float32), 0.5, 1.5),
        "w_xz": bell_draw(key_list[3], (LAYERS, D, 2, INNER), D ** -0.5, 0.15625, ((0, 2), (3, 4))),
        "w_bc": bell_draw(key_list[4], (LAYERS, D, 2 * STATE), D ** -0.5, 0.15625, ((0, 2),)),
        "w_dt": bell_draw(key_list[5], (LAYERS, D, HEADS), D ** -0.5, 0.15625, ((0, 2), (2, 4))),
        "conv_x": jnp.clip(jax.random.uniform(key_list[6], (LAYERS, CONV + 1, INNER), jnp.float32, -0.5, 0.5) * levels(key_list[6], (LAYERS, CONV + 1, INNER), ((0, 2), (2, 4)), -0.4, 0.0), -0.5, 0.5),
        "conv_bc": jnp.clip(jax.random.uniform(key_list[7], (LAYERS, CONV + 1, 2 * STATE), jnp.float32, -0.5, 0.5) * levels(key_list[7], (LAYERS, CONV + 1, 2 * STATE), ((0, 2),), -0.4, 0.0), -0.5, 0.5),
        "head_params": draw_head_params(jax.random.fold_in(key_list[11], 71), 0),
        "out_gain": jnp.clip(1.0 + 0.1 * jax.random.normal(key_list[9], (LAYERS, INNER), jnp.float32), 0.5, 1.5),
        "w_out": bell_draw(key_list[10], (LAYERS, INNER, D), INNER ** -0.5, 0.109375, ((0, 2), (1, 4))),
    }


EPSILON = 1e-05
PRECISE = lax.Precision.HIGHEST

@jax.custom_vjp
def low(v):
    return lax.optimization_barrier(v.astype(jnp.bfloat16)).astype(jnp.float32)

@jax.custom_vjp
def low_back(v):
    return v

def low_keep(v):
    return (low(v), None)

def low_pass(kept, grad):
    return (grad,)

def back_keep(v):
    return (v, None)

def back_low(kept, grad):
    return (low(grad),)
low.defvjp(low_keep, low_pass)
low_back.defvjp(back_keep, back_low)

def sigmoid_linear(value):
    return value * jax.nn.sigmoid(value)

def convolve(padded, tap_rows):
    kernel = tap_rows.shape[0] - 1
    length = padded.shape[0] - kernel + 1
    totals = jnp.zeros((length, tap_rows.shape[1]), jnp.float32) + tap_rows[kernel][None, :]
    for offset in range(kernel):
        totals = totals + tap_rows[offset][None, :] * padded[offset:offset + length]
    return totals

def gated_conv(padded, tap_rows):
    return sigmoid_linear(convolve(padded, tap_rows))

def block_step(carry_state, pieces):
    block_x, block_b, block_c, block_dt, block_log = pieces
    cumul_log = jnp.cumsum(block_log, axis=0)
    log_gaps = cumul_log[:, None, :] - cumul_log[None, :, :]
    later_row = lax.broadcasted_iota(jnp.int32, log_gaps.shape, 0)
    early_col = lax.broadcasted_iota(jnp.int32, log_gaps.shape, 1)
    decays = jnp.where(later_row >= early_col, jnp.exp(jnp.minimum(log_gaps, 0.0)), 0.0)
    intersection = jnp.dot(block_c, block_b.T, precision=PRECISE)
    mixing = intersection[:, :, None] * decays * block_dt[None, :, :]
    outputs = jnp.einsum('tsh,shp->thp', mixing, block_x, precision=PRECISE)
    carried = jnp.einsum('tn,hpn->thp', block_c, carry_state, precision=PRECISE)
    outputs = outputs + jnp.exp(cumul_log)[:, :, None] * carried
    tail_weight = jnp.exp(cumul_log[-1][None, :] - cumul_log) * block_dt
    fresh = jnp.einsum('sh,shp,sn->hpn', tail_weight, block_x, block_b, precision=PRECISE)
    new_state = jnp.exp(cumul_log[-1])[:, None, None] * carry_state + fresh
    return (new_state, outputs)

def local_scan(heads_x, mat_b, mat_c, step_size, log_decay):
    row_count, head_count, head_size = heads_x.shape
    blocks = row_count // BLOCK
    pieces = (heads_x.reshape(blocks, BLOCK, head_count, head_size), mat_b.reshape(blocks, BLOCK, -1), mat_c.reshape(blocks, BLOCK, -1), step_size.reshape(blocks, BLOCK, head_count), log_decay.reshape(blocks, BLOCK, head_count))
    zero_state = jnp.zeros((head_count, head_size, mat_b.shape[1]), jnp.float32)
    final_state, outputs = lax.scan(jax.checkpoint(block_step), zero_state, pieces)
    return (outputs.reshape(row_count, head_count, head_size), final_state)

def prepare(x_padded, bc_act, raw_dt, conv_x, head_params):
    inner_x = gated_conv(x_padded, conv_x)
    head_count = head_params.shape[1]
    heads_x = inner_x.reshape(inner_x.shape[0], head_count, -1)
    step_size = jax.nn.softplus(raw_dt + head_params[0][None, :])
    log_decay = -jnp.exp(head_params[1])[None, :] * step_size
    state_half = bc_act.shape[1] // 2
    mat_b = bc_act[:, :state_half]
    mat_c = bc_act[:, state_half:]
    local_out, final_state = local_scan(heads_x, mat_b, mat_c, step_size, log_decay)
    return (heads_x, mat_c, log_decay, local_out, final_state)

def layer_apply(source, norm_gain, w_xz, w_bc, w_dt, conv_x, conv_bc, head_params, out_gain, w_out):
    norm_rsqrt = lax.rsqrt(lax.optimization_barrier(jnp.mean(source * source, axis=-1, keepdims=True)) + EPSILON)
    normed = low(source * norm_rsqrt * norm_gain)
    x_proj = low_back(low(jnp.dot(normed, w_xz[:, 0], precision=PRECISE)))
    gate_raw = low_back(jnp.dot(normed, w_xz[:, 1], precision=PRECISE))
    bc_proj = low_back(low(jnp.dot(normed, w_bc, precision=PRECISE)))
    raw_dt = low_back(jnp.dot(normed, w_dt, precision=PRECISE))
    margin = conv_x.shape[0] - 2
    x_padded = jnp.pad(x_proj, ((margin, 0), (0, 0)))
    bc_padded = jnp.pad(bc_proj, ((margin, 0), (0, 0)))
    bc_act = gated_conv(bc_padded, conv_bc)
    heads_x, mat_c, log_decay, local_out, final_state = prepare(x_padded, bc_act, raw_dt, conv_x, head_params)
    mixed_out = local_out + head_params[2][None, :, None] * heads_x
    gated_out = mixed_out.reshape(mixed_out.shape[0], -1) * sigmoid_linear(gate_raw)
    out_rsqrt = lax.rsqrt(lax.optimization_barrier(jnp.mean(gated_out * gated_out, axis=-1, keepdims=True)) + EPSILON)
    branch_in = low(gated_out * out_rsqrt * out_gain)
    return source + jnp.dot(branch_in, w_out, precision=PRECISE)

def reference(tokens, cotangent, norm_gain, w_xz, w_bc, w_dt, conv_x, conv_bc, head_params, out_gain, w_out):
    params = tuple((array_item.astype(jnp.float32) for array_item in (norm_gain, w_xz, w_bc, w_dt, conv_x, conv_bc, head_params, out_gain, w_out)))
    inputs = tokens.astype(jnp.float32)

    def forward(inputs, *params):
        results = []
        for micro_index in range(MB):
            hidden = inputs[micro_index]
            for layer_index in range(LAYERS):
                hidden = layer_apply(hidden, *[array_item[layer_index] for array_item in params])
                if layer_index + 1 < LAYERS:
                    hidden = low_back(low(hidden))
                else:
                    hidden = low(hidden)
            results.append(hidden)
        return jnp.stack(results)
    outputs, pull_back = jax.vjp(forward, inputs, *params)
    grads = pull_back(cotangent.astype(jnp.float32))
    section_ends = jnp.stack([grads[0], outputs])
    return (section_ends, grads[1], grads[2], grads[3], grads[4], grads[5], grads[6], grads[7], grads[8], grads[9])
```

```python
import functools

import jax
import jax.numpy as jnp
from jax import lax
from jax.experimental import pallas as pl
from jax.experimental.pallas import tpu as pltpu
from jax.sharding import PartitionSpec as P

EPSILON = 1e-05
MESH = pl.DeviceIdType.MESH
LANES = 128
EDGE = 16
F32 = jnp.float32
BF16 = jnp.bfloat16
SEMS = 96


def dot(a, b):
    return lax.dot_general(a, b, (((1,), (0,)), ((), ())), preferred_element_type=F32)


def dot_nt(a, b):
    return lax.dot_general(a, b, (((1,), (1,)), ((), ())), preferred_element_type=F32)


def dot_tn(a, b):
    return lax.dot_general(a, b, (((0,), (0,)), ((), ())), preferred_element_type=F32)


def exact_dot(a, b):
    return lax.dot_general(
        a, b, (((1,), (0,)), ((), ())), precision=lax.Precision.HIGHEST, preferred_element_type=F32
    )


def split_dot(a, b):
    high = a.astype(BF16)
    return dot(high, b) + dot((a - high.astype(F32)).astype(BF16), b)


class Links:
    def __init__(self, local_sem, send_sem, recv_sem):
        self.local_sem, self.send_sem, self.recv_sem = local_sem, send_sem, recv_sem
        self.local_count = 0
        self.count = 0
        self.pending = []

    def local(self, src, dst):
        index = self.local_count
        self.local_count += 1
        return pltpu.make_async_copy(src, dst, self.local_sem.at[index])

    def remote(self, src, dst, peer, when=None):
        index = self.count
        self.count += 1
        copy = pltpu.make_async_remote_copy(
            src_ref=src,
            dst_ref=dst,
            send_sem=self.send_sem.at[index],
            recv_sem=self.recv_sem.at[index],
            device_id=peer,
            device_id_type=MESH,
        )
        self.pending.append((copy, when))
        return copy

    def drain(self):
        for copy, when in self.pending:
            if when is None:
                copy.wait_send()
            else:

                @pl.when(when)
                def _():
                    copy.wait_send()


def wait_if(condition, copy):
    @pl.when(condition)
    def _():
        copy.wait_recv()


def start_if(condition, copy):
    @pl.when(condition)
    def _():
        copy.start()


def lanes(i, width=LANES):
    if isinstance(i, int):
        return pl.ds(i * width, width)
    return pl.ds(pl.multiple_of(i * width, width), width)


def layer_kernel(dims, *refs):
    (n_seq, n_head, T, D, I, N, heads) = dims
    (
        tokens, cotangent, w_xz, w_bc, w_dt, w_out, prm_own,
        ends_out, nm, gp, u_out, e_out, small,
        wxz, wbc, wdt, wo, prm, hb, eb, xin, z, pre, act, dte, cume, y0, g,
        sgdt, dtv, cum, cumT, CT, BT, Bb, Cb, st_loc, s_ent, xtb, xtl, qb,
        gb, du, dy, dyb, dye, dst_loc, gin, dxt, dact, dpx, dn, dcbt,
        row_send, row_recv, rs_send, rs_recv, ch_send, ch_recv, edge_send, edge_recv, ag_send,
        end_send, ends, et, tri, local_sem, send_sem, recv_sem,
    ) = refs
    c = lax.axis_index("section")
    s = lax.axis_index("seq")
    k = lax.axis_index("head")
    links = Links(local_sem, send_sem, recv_sem)
    Q = T // n_head
    XB = I + 2 * N
    pairs = I // LANES
    is_first = s == 0
    is_last = s == n_seq - 1
    has_prev = s > 0
    has_next = s < n_seq - 1
    other = {"section": 1 - c}
    prev_dev = {"seq": jnp.maximum(s - 1, 0)}
    next_dev = {"seq": jnp.minimum(s + 1, n_seq - 1)}
    head_peers = [{"head": lax.rem(k + d, n_head)} for d in range(1, n_head)]
    own_rows = pl.ds(pl.multiple_of(k * Q, Q), Q)
    chunks = 3
    CW = I // chunks
    ntile = 256
    inner_total = I * n_head

    barrier = pltpu.get_barrier_semaphore()
    pl.semaphore_signal(barrier, inc=1, device_id=other, device_id_type=MESH)
    for peer in head_peers:
        pl.semaphore_signal(barrier, inc=1, device_id=peer, device_id_type=MESH)

    @pl.when(has_prev)
    def _():
        pl.semaphore_signal(barrier, inc=1, device_id=prev_dev, device_id_type=MESH)

    @pl.when(has_next)
    def _():
        pl.semaphore_signal(barrier, inc=1, device_id=next_dev, device_id_type=MESH)

    load_h = links.local(tokens.at[c], hb.at[0])
    load_e = links.local(cotangent.at[c], eb.at[1])
    load_h.start()
    mine = []
    for src, dst in (
        (prm_own, prm.at[c]),
        (w_xz.at[0], wxz.at[c, 0]),
        (w_bc, wbc.at[c]),
        (w_dt, wdt.at[c]),
        (w_xz.at[1], wxz.at[c, 1]),
        (w_out, wo.at[c]),
    ):
        copy = links.local(src, dst)
        copy.start()
        mine.append(copy)
    load_e.start()

    inner_seq = has_prev & has_next

    @pl.when(inner_seq)
    def _():
        pl.semaphore_wait(barrier, n_head + 2)

    @pl.when(jnp.logical_not(inner_seq))
    def _():
        pl.semaphore_wait(barrier, n_head + 1)

    theirs = []
    for src, dst in (
        (prm_own, prm.at[c]),
        (w_xz.at[0], wxz.at[c, 0]),
        (w_bc, wbc.at[c]),
        (w_dt, wdt.at[c]),
        (w_xz.at[1], wxz.at[c, 1]),
        (w_out, wo.at[c]),
    ):
        copy = links.remote(src, dst, other)
        copy.start()
        theirs.append(copy)

    def weights_ready(layer, which):
        @pl.when(c == layer)
        def _():
            for i in which:
                mine[i].wait()

        @pl.when(c != layer)
        def _():
            for i in which:
                theirs[i].wait_recv()

    row_i = lax.broadcasted_iota(jnp.int32, (T, T), 0)
    col_i = lax.broadcasted_iota(jnp.int32, (T, T), 1)
    tri[...] = jnp.where(row_i >= col_i, 1.0, 0.0)
    er = lax.broadcasted_iota(jnp.int32, (I, LANES), 0)
    ec = lax.broadcasted_iota(jnp.int32, (I, LANES), 1)
    head_size = I // heads
    et[...] = jnp.where(
        (er >= ec * head_size) & (er < (ec + 1) * head_size), 1.0, 0.0
    ).astype(BF16)

    small[...] = jnp.zeros_like(small)
    load_h.wait()

    def exchange_rows(total_cols, slot):
        summed = jnp.sum(total_cols, axis=1, keepdims=True)
        as_row = jnp.transpose(jnp.broadcast_to(summed, (T, LANES)))[:8]
        row_send[slot] = as_row
        copies = []
        for d, peer in enumerate(head_peers):
            copy = links.remote(row_send.at[slot], row_recv.at[slot, d], peer)
            copy.start()
            copies.append(copy)

        def finish():
            total = row_send[slot]
            for d, copy in enumerate(copies):
                copy.wait_recv()
                total = total + row_recv[slot, d]
            wide = jnp.broadcast_to(total[:1], (LANES, T))
            return jnp.transpose(wide)

        return finish

    def reduce_rows(slot):
        copies = []
        for d, peer in enumerate(head_peers):
            rows = pl.ds(pl.multiple_of(lax.rem(k + d + 1, n_head) * Q, Q), Q)
            copy = links.remote(rs_send.at[slot, rows], rs_recv.at[slot, d], peer)
            copy.start()
            copies.append(copy)

        def finish():
            for copy in copies:
                copy.wait_recv()

        return finish

    def rs_total(slot, rows_at):
        total = rs_send[slot, rows_at, :].astype(F32)
        for d in range(n_head - 1):
            total = total + rs_recv[slot, d, :, :].astype(F32)
        return total

    def gather_rows(slot, target, rows):
        ag_send[slot] = rows
        target[own_rows, :] = rows
        copies = []
        for peer in head_peers:
            copy = links.remote(ag_send.at[slot], target.at[own_rows], peer)
            copy.start()
            copies.append(copy)

        def finish():
            for copy in copies:
                copy.wait_recv()

        return finish

    def chain(slot, forward, local, dec_row, into):
        starts, goes_on = (is_first, has_next) if forward else (is_last, has_prev)
        receives = has_prev if forward else has_next
        peer = next_dev if forward else prev_dev
        copies = []
        for j in range(chunks):
            copies.append(
                links.remote(ch_send.at[slot, j], ch_recv.at[slot, j], peer, goes_on)
            )

        def begin():
            @pl.when(starts)
            def _():
                for j in range(chunks):
                    ch_send[slot, j] = local[:, lanes(j, CW)].astype(BF16)
                    start_if(goes_on, copies[j])

        def finish():
            @pl.when(starts)
            def _():
                into[...] = jnp.zeros_like(into)

            @pl.when(receives)
            def _():
                for j in range(chunks):
                    copies[j].wait_recv()
                    at = lanes(j, CW)
                    arrived = ch_recv[slot, j].astype(F32)
                    into[:, at] = arrived

                    @pl.when(goes_on)
                    def _():
                        ch_send[slot, j] = (
                            arrived * dec_row[:, j * CW : (j + 1) * CW] + local[:, at]
                        ).astype(BF16)
                        copies[j].start()

        return begin, finish

    lane_low = lax.broadcasted_iota(jnp.int32, (T, LANES), 1) < head_size
    later = row_i >= col_i
    earlier = col_i >= row_i

    def forward(l):
        weights_ready(l, [0])
        gain = prm[l, 0:1, :]

        def norm_rows(i, _):
            rows = pl.ds(pl.multiple_of(i * 32, 32), 32)
            v = hb[l, rows, :].astype(F32)
            rstd = lax.rsqrt(jnp.mean(v * v, axis=1, keepdims=True) + EPSILON)
            nm[l, rows, :] = (v * rstd * gain).astype(BF16)
            return 0

        lax.fori_loop(0, T // 32, norm_rows, 0)

        weights_ready(l, [1, 2, 3])

        def project_x(j, _):
            xin[l, EDGE:, lanes(j, ntile)] = dot(
                nm[l], wxz[l, 0, :, lanes(j, ntile)]
            ).astype(BF16)
            return 0

        lax.fori_loop(0, I // ntile, project_x, 0)
        xin[l, EDGE:, I:] = dot(nm[l], wbc[l]).astype(BF16)

        edge = links.remote(
            xin.at[l, pl.ds(T, EDGE)], xin.at[l, pl.ds(0, EDGE)], next_dev, has_next
        )
        start_if(has_next, edge)

        dt_raw = dot(nm[l], wdt[l])
        hp0 = prm[l, 6:7, I : I + LANES]
        hp1 = prm[l, 6:7, I + LANES : I + 2 * LANES]
        pre_dt = dt_raw + hp0
        sgdt[l] = lax.logistic(pre_dt)
        step = jnp.maximum(pre_dt, 0.0) + jnp.log1p(jnp.exp(-jnp.abs(pre_dt)))
        dtv[l] = step
        cum[l] = exact_dot(tri[...], -jnp.exp(hp1) * step)
        cumT[l] = jnp.transpose(cum[l])

        weights_ready(l, [4])

        def project_z(j, _):
            z[l, :, lanes(j, ntile)] = dot(nm[l], wxz[l, 1, :, lanes(j, ntile)])
            return 0

        lax.fori_loop(0, I // ntile, project_z, 0)

        @pl.when(is_first)
        def _():
            xin[l, :EDGE, :] = jnp.zeros((EDGE, XB), BF16)

        wait_if(has_prev, edge)

        def conv(j, _):
            at = lanes(j)
            v = xin[l, :, at].astype(F32)
            total = prm[l, 5:6, at] + prm[l, 4:5, at] * v[EDGE:]
            for shift in range(1, 4):
                total = total + prm[l, 4 - shift : 5 - shift, at] * pltpu.roll(v, shift, 0)[EDGE:]
            pre[l, :, at] = total
            act[l, :, at] = total * lax.logistic(total)
            return 0

        lax.fori_loop(0, XB // LANES, conv, 0)

        mat_b = act[l, :, I : I + N]
        mat_c = act[l, :, I + N :]
        Bb[l] = mat_b.astype(BF16)
        Cb[l] = mat_c.astype(BF16)
        BT[l] = jnp.transpose(mat_b).astype(BF16)
        CT[l] = jnp.transpose(mat_c).astype(BF16)

        for p in range(pairs):
            at = lanes(p)
            step = jnp.where(
                lane_low, dtv[l, :, 2 * p : 2 * p + 1], dtv[l, :, 2 * p + 1 : 2 * p + 2]
            )
            acc = jnp.where(
                lane_low, cum[l, :, 2 * p : 2 * p + 1], cum[l, :, 2 * p + 1 : 2 * p + 2]
            )
            tail = jnp.exp(acc[T - 1 : T] - acc)
            dte[l, :, at] = step
            cume[l, :, at] = acc
            stepped = step * act[l, :, at]
            xtb[l, :, at] = stepped.astype(BF16)
            xtl[l, :, at] = (stepped * tail).astype(BF16)

        def local_state(j, _):
            st_loc[l, :, lanes(j, ntile)] = dot(BT[l], xtl[l, :, lanes(j, ntile)])
            return 0

        lax.fori_loop(0, I // ntile, local_state, 0)
        begin, finish_chain = chain(
            l, True, st_loc.at[l], jnp.exp(cume[l, T - 1 : T, :]), s_ent.at[l]
        )
        begin()

        cb = dot_nt(Cb[l], Bb[l])

        def intra(p, _):
            at = lanes(p)
            wide = cume[l, :, at]
            values = xtb[l, :, at]
            total = jnp.zeros((T, LANES), F32)
            for half in range(2):
                column = wide[:, half * head_size : half * head_size + 1]
                row = cumT[l, pl.ds(2 * p + half, 1), :]
                decay = jnp.where(later, jnp.exp(jnp.minimum(column - row, 0.0)), 0.0)
                mix = (cb * decay).astype(BF16)
                kept = jnp.where(lane_low == (half == 0), values, jnp.zeros_like(values))
                total = total + dot(mix, kept)
            y0[l, :, at] = total
            return 0

        lax.fori_loop(0, pairs, intra, 0)
        finish_chain()

        def gate(p, ssq):
            at = lanes(p)
            carried = dot(Cb[l], s_ent[l, :, at].astype(BF16))
            y = y0[l, :, at] + jnp.exp(cume[l, :, at]) * carried
            y0[l, :, at] = y
            full = y + prm[l, 7:8, at] * act[l, :, at]
            gate_in = z[l, :, at]
            value = full * (gate_in * lax.logistic(gate_in))
            g[l, :, at] = value
            gb[:, at] = (value * prm[l, 6:7, at]).astype(BF16)
            return ssq + value * value

        ssq = lax.fori_loop(0, pairs, gate, jnp.zeros((T, LANES), F32))
        finish_rows = exchange_rows(ssq, l)
        weights_ready(l, [5])

        def project_out(j, _):
            rs_send[l, :, lanes(j, ntile)] = dot(gb[...], wo[l, :, lanes(j, ntile)]).astype(BF16)
            return 0

        lax.fori_loop(0, D // ntile, project_out, 0)
        finish_rs = reduce_rows(l)
        qb[l] = lax.rsqrt(finish_rows() / inner_total + EPSILON)

        def scaled(p, _):
            at = lanes(p)
            u_out[l, :, at] = (g[l, :, at] * qb[l] * prm[l, 6:7, at]).astype(BF16)
            return 0

        lax.fori_loop(0, pairs, scaled, 0)
        finish_rs()
        summed = rs_total(l, own_rows)
        q_own = qb[l, own_rows, :][:, :1]
        return (hb[l, own_rows, :].astype(F32) + q_own * summed).astype(BF16)

    def backward(l):
        hp1 = prm[l, 6:7, I + LANES : I + 2 * LANES]

        def start_du(j, acc):
            at = lanes(j, ntile)
            got = dot_nt(eb[l], wo[l, at, :])
            du[:, at] = got
            value = got * g[l, :, at]
            small[l, 6:7, at] = jnp.sum(value * qb[l][:, :1], axis=0, keepdims=True)
            weighted = value * prm[l, 6:7, at]
            return acc + weighted[:, :LANES] + weighted[:, LANES:]

        acc = lax.fori_loop(0, I // ntile, start_du, jnp.zeros((T, LANES), F32))
        finish_rows = exchange_rows(acc, 2 + l)
        dot_all = finish_rows()

        def through_gate(p, _):
            at = lanes(p)
            q = qb[l]
            gate_in = z[l, :, at]
            sig = lax.logistic(gate_in)
            silu = gate_in * sig
            value = g[l, :, at]
            dg = q * (du[:, at] * prm[l, 6:7, at]) - value * (q * q * q) * (
                dot_all / inner_total
            )
            x_now = act[l, :, at]
            full = y0[l, :, at] + prm[l, 7:8, at] * x_now
            d_y = dg * silu
            gp[l, :, lanes(p + pairs)] = (
                dg * full * sig * (1.0 + gate_in * (1.0 - sig))
            ).astype(BF16)
            small[l, 7:8, at] = jnp.sum(d_y * x_now, axis=0, keepdims=True)
            dy[:, at] = d_y
            dyb[:, at] = d_y.astype(BF16)
            dye[:, at] = (d_y * jnp.exp(cume[l, :, at])).astype(BF16)
            return 0

        lax.fori_loop(0, pairs, through_gate, 0)

        def local_state(j, _):
            dst_loc[:, lanes(j, ntile)] = dot(CT[l], dye[:, lanes(j, ntile)])
            return 0

        lax.fori_loop(0, I // ntile, local_state, 0)
        begin, finish_chain = chain(
            2 + l, False, dst_loc, jnp.exp(cume[l, T - 1 : T, :]), gin
        )
        begin()

        def normed_z(j, _):
            dn[:, lanes(j, ntile)] = dot_nt(
                gp[l, :, I : 2 * I], wxz[l, 1, lanes(j, ntile), :]
            )
            return 0

        lax.fori_loop(0, D // ntile, normed_z, 0)

        cbt = dot_nt(Bb[l], Cb[l])
        dcbt[...] = jnp.zeros_like(dcbt)

        def intra(p, _):
            at = lanes(p)
            wide = cume[l, :, at]
            values = xtb[l, :, at]
            grads = dyb[:, at]
            total = jnp.zeros((T, LANES), F32)
            for half in range(2):
                column = wide[:, half * head_size : half * head_size + 1]
                row = cumT[l, pl.ds(2 * p + half, 1), :]
                decay = jnp.where(earlier, jnp.exp(jnp.minimum(row - column, 0.0)), 0.0)
                mix = (cbt * decay).astype(BF16)
                kept = jnp.where(lane_low == (half == 0), grads, jnp.zeros_like(grads))
                total = total + dot(mix, kept)
                dcbt[...] += dot_nt(values, kept) * decay
            dxt[:, at] = total
            return 0

        lax.fori_loop(0, pairs, intra, 0)
        finish_chain()

        def join(p, carry):
            sum_v, sum_w = carry
            at = lanes(p)
            into = gin[:, at]
            acc = cume[l, :, at]
            end = acc[T - 1 : T]
            got = dxt[:, at] + jnp.exp(end - acc) * dot(Bb[l], into.astype(BF16))
            x_now = act[l, :, at]
            d_y = dy[:, at]
            leaving = s_ent[l, :, at] * jnp.exp(end) + st_loc[l, :, at]
            final = jnp.sum(into * leaving, axis=0, keepdims=True)
            v = dyb[:, at].astype(F32) * y0[l, :, at] - xtb[l, :, at].astype(F32) * got
            is_end = lax.broadcasted_iota(jnp.int32, (T, LANES), 0) == T - 1
            v = v + jnp.where(is_end, final, 0.0)
            dact[:, at] = dte[l, :, at] * got + prm[l, 7:8, at] * d_y
            picks = et[at, :]
            return (sum_v + split_dot(v, picks), sum_w + split_dot(x_now * got, picks))

        zero = jnp.zeros((T, LANES), F32)
        sum_v, sum_w = lax.fori_loop(0, pairs, join, (zero, zero))

        dcb_low = dcbt[...].astype(BF16)
        gin_low = gin[...].astype(BF16)
        ent_low = s_ent[l].astype(BF16)
        dact[:, I : I + N] = dot(dcb_low, Cb[l]) + dot_nt(xtl[l], gin_low)
        dact[:, I + N :] = dot_tn(dcb_low, Bb[l]) + dot_nt(dye[...], ent_low)

        def conv_pre(j, _):
            at = lanes(j)
            v = pre[l, :, at]
            sig = lax.logistic(v)
            got = dact[:, at] * (sig * (1.0 + v * (1.0 - sig)))
            dpx[:T, at] = got
            edge_send[l, :, at] = got[:EDGE].astype(BF16)
            return 0

        lax.fori_loop(0, XB // LANES, conv_pre, 0)
        edge = links.remote(edge_send.at[l], edge_recv.at[l], prev_dev, has_prev)
        start_if(has_prev, edge)

        d_log = lax.dot_general(
            tri[...], sum_v, (((0,), (0,)), ((), ())),
            precision=lax.Precision.HIGHEST, preferred_element_type=F32,
        )
        rate = -jnp.exp(hp1)
        d_raw = (sum_w + d_log * rate) * sgdt[l]
        small[l, 6:7, I : I + LANES] = jnp.sum(d_raw, axis=0, keepdims=True)
        small[l, 6:7, I + LANES : I + 2 * LANES] = jnp.sum(
            d_log * rate * dtv[l], axis=0, keepdims=True
        )
        gp[l, :, 2 * I + 2 * N :] = jnp.where(
            lax.broadcasted_iota(jnp.int32, (T, LANES), 1) < heads, d_raw, 0.0
        ).astype(BF16)

        def conv_taps(j, _):
            at = lanes(j)
            v = xin[l, :, at].astype(F32)
            got = dpx[:T, at]
            small[l, 5:6, at] = jnp.sum(got, axis=0, keepdims=True)
            for shift in range(4):
                moved = v if shift == 0 else pltpu.roll(v, shift, 0)
                small[l, 4 - shift : 5 - shift, at] = jnp.sum(
                    got * moved[EDGE:], axis=0, keepdims=True
                )
            return 0

        lax.fori_loop(0, XB // LANES, conv_taps, 0)

        @pl.when(is_last)
        def _():
            dpx[T:, :] = jnp.zeros((EDGE, XB), F32)

        @pl.when(has_next)
        def _():
            edge.wait_recv()
            dpx[T:, :] = edge_recv[l].astype(F32)

        def conv_in(j, _):
            at = lanes(j)
            v = dpx[:, at]
            total = prm[l, 4:5, at] * v[:T]
            for shift in range(1, 4):
                moved = pltpu.roll(v, T + EDGE - shift, 0)
                total = total + prm[l, 4 - shift : 5 - shift, at] * moved[:T]
            dact[:, at] = total
            return 0

        lax.fori_loop(0, XB // LANES, conv_in, 0)
        gp[l, :, :I] = dact[:, :I].astype(BF16)
        gp[l, :, 2 * I : 2 * I + 2 * N] = dact[:, I:].astype(BF16)

        def normed_rest(j, _):
            at = lanes(j, ntile)
            total = dn[:, at] + dot_nt(gp[l, :, :I], wxz[l, 0, at, :])
            total = total + dot_nt(gp[l, :, 2 * I : 2 * I + 2 * N], wbc[l, at, :])
            total = total + dot_nt(gp[l, :, 2 * I + 2 * N :], wdt[l, at, :])
            rs_send[2 + l, :, at] = total.astype(BF16)
            return 0

        lax.fori_loop(0, D // ntile, normed_rest, 0)
        finish_rs = reduce_rows(2 + l)
        finish_rs()
        got = rs_total(2 + l, own_rows)
        v = hb[l, own_rows, :].astype(F32)
        rstd = lax.rsqrt(jnp.mean(v * v, axis=1, keepdims=True) + EPSILON)
        small[l, 0:1, :] = jnp.sum(got * v * rstd, axis=0, keepdims=True)
        hat = got * prm[l, 0:1, :]
        inner = jnp.sum(hat * v, axis=1, keepdims=True)
        return (
            rstd * hat - v * (rstd * rstd * rstd) * inner / D
            + eb[l, own_rows, :].astype(F32)
        )

    def deliver(kind, rows):
        copy = links.remote(end_send.at[kind], ends.at[c], other, c != kind)

        @pl.when(c == kind)
        def _():
            ends[c] = rows

        @pl.when(c != kind)
        def _():
            end_send[kind] = rows
            copy.start()

        def finish():
            wait_if(c == kind, copy)

        return finish

    rows = forward(0)
    finish_gather = gather_rows(0, hb.at[1], rows)
    finish_gather()
    rows = forward(1)
    finish_out = deliver(1, rows.astype(F32))
    load_e.wait()
    rows = backward(1)
    finish_gather = gather_rows(1, eb.at[0], rows.astype(BF16))
    finish_gather()
    rows = backward(0)
    finish_in = deliver(0, rows)
    e_out[...] = eb[...]
    finish_out()
    finish_in()
    ends_out[...] = ends[...]
    links.drain()


def run_layers(tokens, cotangent, w_xz, w_bc, w_dt, w_out, prm, heads):
    n_seq, n_head = lax.axis_size("seq"), lax.axis_size("head")
    _, T, D = tokens.shape
    I = w_xz.shape[2]
    N = w_bc.shape[1] // 2
    XB = I + 2 * N
    G = 2 * I + 2 * N + LANES
    Q = T // n_head
    S = jax.ShapeDtypeStruct
    V = pltpu.VMEM
    vm = pl.BlockSpec(memory_space=pltpu.VMEM)
    hbm = pl.BlockSpec(memory_space=pl.ANY)
    scratch = [
        V((2, 2, D, I), BF16), V((2, D, 2 * N), BF16), V((2, D, LANES), BF16), V((2, I, D), BF16),
        V((2, 8, D), F32), V((2, T, D), BF16), V((2, T, D), BF16), V((2, T + EDGE, XB), BF16),
        V((2, T, I), F32), V((2, T, XB), F32), V((2, T, XB), F32),
        V((2, T, I), F32), V((2, T, I), F32), V((2, T, I), F32), V((2, T, I), F32),
        V((2, T, LANES), F32), V((2, T, LANES), F32), V((2, T, LANES), F32), V((2, LANES, T), F32),
        V((2, N, T), BF16), V((2, N, T), BF16), V((2, T, N), BF16), V((2, T, N), BF16),
        V((2, N, I), F32), V((2, N, I), F32), V((2, T, I), BF16), V((2, T, I), BF16),
        V((2, T, LANES), F32),
        V((T, I), BF16), V((T, I), F32), V((T, I), F32), V((T, I), BF16), V((T, I), BF16),
        V((N, I), F32), V((N, I), F32), V((T, I), F32), V((T, XB), F32), V((T + EDGE, XB), F32),
        V((T, D), F32), V((T, T), F32),
        V((4, 8, T), F32), V((4, n_head - 1, 8, T), F32),
        V((4, T, D), BF16), V((4, n_head - 1, Q, D), BF16),
        V((4, 3, N, I // 3), BF16), V((4, 3, N, I // 3), BF16),
        V((2, EDGE, XB), BF16), V((2, EDGE, XB), BF16), V((2, Q, D), BF16),
        V((2, Q, D), F32), V((2, Q, D), F32), V((I, LANES), BF16), V((T, T), F32),
        pltpu.SemaphoreType.DMA((SEMS,)), pltpu.SemaphoreType.DMA((SEMS,)),
        pltpu.SemaphoreType.DMA((SEMS,)),
    ]
    dims = (n_seq, n_head, T, D, I, N, heads)
    return pl.pallas_call(
        functools.partial(layer_kernel, dims),
        out_shape=(
            S((2, Q, D), F32), S((2, T, D), BF16), S((2, T, G), BF16), S((2, T, I), BF16),
            S((2, T, D), BF16), S((2, 8, D), F32),
        ),
        in_specs=[hbm] * 7,
        out_specs=(vm,) * 6,
        scratch_shapes=scratch,
        compiler_params=pltpu.CompilerParams(
            collective_id=0, has_side_effects=True, vmem_limit_bytes=62 * 2**20
        ),
        name="layers",
    )(tokens, cotangent, w_xz, w_bc, w_dt, w_out, prm)


def body(
    tokens, cotangent, norm_gain, w_xz, w_bc, w_dt, conv_x, conv_bc, head_params, out_gain, w_out
):
    n_seq = lax.axis_size("seq")
    D = tokens.shape[2]
    I = w_xz.shape[3]
    N2 = w_bc.shape[2]
    heads = w_dt.shape[2]
    lane_pad = LANES - heads

    def wide(a):
        return jnp.pad(a, ((0, 0), (0, D - a.shape[1])))

    params = jnp.concatenate(
        [
            norm_gain,
            wide(jnp.concatenate([conv_x[0], conv_bc[0]], axis=1)),
            wide(
                jnp.concatenate(
                    [
                        out_gain,
                        jnp.pad(head_params[0, 0:1], ((0, 0), (0, lane_pad))),
                        jnp.pad(head_params[0, 1:2], ((0, 0), (0, lane_pad))),
                    ],
                    axis=1,
                )
            ),
            wide(jnp.repeat(head_params[0, 2:3], I // heads, axis=1)),
        ],
        axis=0,
    )
    w_xz2 = jnp.swapaxes(w_xz[0], 0, 1)
    w_dt2 = jnp.pad(w_dt[0], ((0, 0), (0, lane_pad)))
    ends, normed, gproj, u, e, small = run_layers(
        tokens, cotangent, w_xz2, w_bc[0], w_dt2, w_out[0], params, heads
    )
    G = gproj.shape[2]
    contract = (((1,), (1,)), ((0,), (0,)))
    dbc = lax.psum(gproj[:, :, 2 * I : 2 * I + N2].astype(F32), "head").astype(BF16)
    g_xz = lax.dot_general(normed, gproj[:, :, : 2 * I], contract, preferred_element_type=F32)
    g_bc = lax.dot_general(normed, dbc, contract, preferred_element_type=F32)
    g_dt = lax.dot_general(
        normed, gproj[:, :, 2 * I + N2 :], contract, preferred_element_type=F32
    )
    g_out = lax.dot_general(u, e, contract, preferred_element_type=F32)

    def scatter(a):
        layers, rows, cols = a.shape
        return lax.psum_scatter(
            a.astype(BF16).reshape(layers * rows, cols), ("section", "seq"), scatter_dimension=0, tiled=True
        ).astype(F32)

    g_xz = scatter(g_xz)
    g_small = scatter(jnp.concatenate([g_bc, g_dt], axis=2))
    layers, rows, cols = g_out.shape
    g_out = g_out.reshape(layers, rows, n_seq, cols // n_seq).swapaxes(1, 2)
    g_out = scatter(g_out.reshape(layers, n_seq * rows, cols // n_seq))
    shared = jnp.concatenate([small[:, 0], small[:, 1:6, I : I + N2].reshape(2, -1)], axis=1)
    shared = lax.psum(shared, ("section", "seq", "head"))
    own = lax.psum(small[:, 1:8], ("section", "seq"))
    c = lax.axis_index("section")
    shared = lax.dynamic_index_in_dim(shared, c, 0, False)
    own = lax.dynamic_index_in_dim(own, c, 0, False)
    g_conv_x = own[0:5, :I]
    g_conv_bc = shared[D:].reshape(5, N2)
    g_skip = jnp.sum(own[6, :I].reshape(heads, -1), axis=1)
    g_head = jnp.stack([own[5, I : I + heads], own[5, I + LANES : I + LANES + heads], g_skip])
    return (
        ends[None],
        shared[None, :D],
        g_xz.reshape(1, D // n_seq, 2, I),
        g_small[None, :, :N2],
        g_small[None, :, N2 : N2 + heads],
        g_conv_x[None],
        g_conv_bc[None],
        g_head[None],
        own[None, 5, :I],
        g_out[None],
    )


def solution(mesh):
    placed = (
        P(None, "seq", None),
        P(None, "seq", None),
        P("section", None),
        P("section", None, None, "head"),
        P("section", None, None),
        P("section", None, "head"),
        P("section", None, "head"),
        P("section", None, None),
        P("section", None, "head"),
        P("section", "head"),
        P("section", "head", None),
    )
    return jax.shard_map(
        body,
        mesh=mesh,
        in_specs=placed,
        out_specs=(
            P("section", None, ("seq", "head"), None),
            P("section", None),
            P("section", "seq", None, "head"),
            P("section", "seq", None),
            P("section", "seq", "head"),
            P("section", None, "head"),
            P("section", None, None),
            P("section", None, "head"),
            P("section", "head"),
            P("section", "head", "seq"),
        ),
        check_vma=False,
    )
```

```python
import functools

import jax
import jax.numpy as jnp
from jax import lax
from jax.experimental import pallas as pl
from jax.experimental.pallas import tpu as pltpu
from jax.sharding import PartitionSpec as P

EPSILON = 1e-05
MESH = pl.DeviceIdType.MESH
LANES = 128
EDGE = 16
F32 = jnp.float32
BF16 = jnp.bfloat16


def dot(a, b):
    return lax.dot_general(a, b, (((1,), (0,)), ((), ())), preferred_element_type=F32)


def dot_nt(a, b):
    return lax.dot_general(a, b, (((1,), (1,)), ((), ())), preferred_element_type=F32)


def dot_tn(a, b):
    return lax.dot_general(a, b, (((0,), (0,)), ((), ())), preferred_element_type=F32)


def exact_dot(a, b):
    return lax.dot_general(
        a, b, (((1,), (0,)), ((), ())), precision=lax.Precision.HIGHEST, preferred_element_type=F32
    )


def split_dot(a, b):
    high = a.astype(BF16)
    return dot(high, b) + dot((a - high.astype(F32)).astype(BF16), b)


class Links:
    def __init__(self, local_sem, send_sem, recv_sem):
        self.local_sem, self.send_sem, self.recv_sem = local_sem, send_sem, recv_sem
        self.local_count = 0
        self.count = 0
        self.pending = []

    def local(self, src, dst):
        index = self.local_count
        assert index < self.local_sem.shape[0]
        self.local_count += 1
        return pltpu.make_async_copy(src, dst, self.local_sem.at[index])

    def remote(self, src, dst, peer, when=None):
        index = self.count
        assert index < self.send_sem.shape[0]
        self.count += 1
        copy = pltpu.make_async_remote_copy(
            src_ref=src,
            dst_ref=dst,
            send_sem=self.send_sem.at[index],
            recv_sem=self.recv_sem.at[index],
            device_id=peer,
            device_id_type=MESH,
        )
        self.pending.append((copy, when))
        return copy

    def drain(self):
        for copy, when in self.pending:
            if when is None:
                copy.wait_send()
            else:

                @pl.when(when)
                def _():
                    copy.wait_send()


def wait_if(condition, copy):
    @pl.when(condition)
    def _():
        copy.wait_recv()


def start_if(condition, copy):
    @pl.when(condition)
    def _():
        copy.start()


def lanes(i, width=LANES):
    if isinstance(i, int):
        return pl.ds(i * width, width)
    return pl.ds(pl.multiple_of(i * width, width), width)


def layer_kernel(dims, *refs):
    (n_seq, n_head, T, D, I, N, heads) = dims
    (
        tokens, cotangent, w_xz, w_bc, w_dt, w_out, prm_own,
        ends_out, z_out, bc_out, small_out, z_land,
        wxz, wbc, wdt, wo, prm, hb, eb, nm, xin, z, act, dte, cume, y0,
        sgdt, dtv, cum, cumT, CT, BT, Bb, Cb, st_loc, s_ent, xtb, xtl, qb,
        du, dy, dyb, dye, dst_loc, gin, dact, dpx, dcbt, gp, us, small,
        row_send, row_recv, rs_send, rs_recv, ch_send, ch_recv, edge_send, edge_recv,
        end_send, ends, et, tri,
        lt, lt_send, rhs, z_send, z_in, z_acc, bc_recv, bc_t, bc_rows, bc_rhs, bc_send, bc_land, bc_all,
        sm_o, sm_t, sm_h, sm_u, sm_z,
        local_sem, send_sem, recv_sem, zs_sem, zr_sem, zi_sem,
    ) = refs
    c = lax.axis_index("section")
    s = lax.axis_index("seq")
    k = lax.axis_index("head")
    links = Links(local_sem, send_sem, recv_sem)
    Q = T // n_head
    XB = I + 2 * N
    DB = D // n_seq
    pairs = I // LANES
    head_size = I // heads
    is_first = s == 0
    is_last = s == n_seq - 1
    has_prev = s > 0
    has_next = s < n_seq - 1
    other = {"section": 1 - c}
    prev_dev = {"seq": jnp.maximum(s - 1, 0)}
    next_dev = {"seq": jnp.minimum(s + 1, n_seq - 1)}
    head_peers = [{"head": lax.rem(k + d, n_head)} for d in range(1, n_head)]
    seq_peers = [{"seq": lax.rem(s + d, n_seq)} for d in range(1, n_seq)]
    own_rows = pl.ds(pl.multiple_of(k * Q, Q), Q)
    chunks = 3
    CW = I // chunks
    ntile = 256
    inner_total = I * n_head
    Q2 = 2 * N // n_head
    rs_copies = {}

    barrier = pltpu.get_barrier_semaphore()
    for peer in [other] + head_peers + seq_peers:
        pl.semaphore_signal(barrier, inc=1, device_id=peer, device_id_type=MESH)

    load_h = links.local(tokens.at[c], hb.at[0])
    load_e = links.local(cotangent.at[c], eb.at[1])
    load_h.start()
    parts = (
        (prm_own, prm.at[c]),
        (w_xz.at[0], wxz.at[c, 0]),
        (w_bc, wbc.at[c]),
        (w_dt, wdt.at[c]),
        (w_xz.at[1], wxz.at[c, 1]),
        (w_out, wo.at[c]),
    )
    mine = [links.local(src, dst) for src, dst in parts]
    for copy in mine:
        copy.start()
    load_e.start()
    pl.semaphore_wait(barrier, n_head + n_seq - 1)
    theirs = [links.remote(src, dst, other) for src, dst in parts]
    for copy in theirs:
        copy.start()

    def weights_ready(layer, which):
        @pl.when(c == layer)
        def _():
            for i in which:
                mine[i].wait()

        @pl.when(c != layer)
        def _():
            for i in which:
                theirs[i].wait_recv()

    row_i = lax.broadcasted_iota(jnp.int32, (T, T), 0)
    col_i = lax.broadcasted_iota(jnp.int32, (T, T), 1)
    tri[...] = jnp.where(row_i >= col_i, 1.0, 0.0)
    er = lax.broadcasted_iota(jnp.int32, (I, LANES), 0)
    ec = lax.broadcasted_iota(jnp.int32, (I, LANES), 1)
    et[...] = jnp.where(
        (er >= ec * head_size) & (er < (ec + 1) * head_size), 1.0, 0.0
    ).astype(BF16)
    small[...] = jnp.zeros_like(small)
    load_h.wait()

    def exchange_rows(total_cols, slot):
        summed = jnp.sum(total_cols, axis=1, keepdims=True)
        as_row = jnp.transpose(jnp.broadcast_to(summed, (T, LANES)))[:8]
        row_send[slot] = as_row
        copies = []
        for d, peer in enumerate(head_peers):
            copy = links.remote(row_send.at[slot], row_recv.at[slot, d], peer)
            copy.start()
            copies.append(copy)

        def finish():
            total = row_send[slot]
            for d, copy in enumerate(copies):
                copy.wait_recv()
                total = total + row_recv[slot, d]
            wide = jnp.broadcast_to(total[:1], (LANES, T))
            return jnp.transpose(wide)

        return finish

    def reduce_rows(slot):
        copies = []
        for d, peer in enumerate(head_peers):
            rows = pl.ds(pl.multiple_of(lax.rem(k + d + 1, n_head) * Q, Q), Q)
            copy = links.remote(rs_send.at[slot, rows], rs_recv.at[slot, d], peer)
            copy.start()
            links.pending.pop()
            copies.append(copy)
        rs_copies[slot] = copies

        def finish():
            for copy in copies:
                copy.wait_recv()

        return finish

    def rs_total(slot, rows_at):
        total = rs_send[slot, rows_at, :].astype(F32)
        for d in range(n_head - 1):
            total = total + rs_recv[slot, d, :, :].astype(F32)
        return total

    def gather_rows(target, rows):
        target[own_rows, :] = rows
        copies = []
        for peer in head_peers:
            copy = links.remote(target.at[own_rows], target.at[own_rows], peer)
            copy.start()
            copies.append(copy)

        def finish():
            for copy in copies:
                copy.wait_recv()

        return finish

    def chain(slot, forward, local, dec_row, into):
        starts, goes_on = (is_first, has_next) if forward else (is_last, has_prev)
        receives = has_prev if forward else has_next
        peer = next_dev if forward else prev_dev
        copies = []
        for j in range(chunks):
            copies.append(
                links.remote(ch_send.at[slot, j], ch_recv.at[slot, j], peer, goes_on)
            )

        def begin():
            @pl.when(starts)
            def _():
                for j in range(chunks):
                    ch_send[slot, j] = local[:, lanes(j, CW)].astype(BF16)
                    start_if(goes_on, copies[j])

        def finish():
            @pl.when(starts)
            def _():
                into[...] = jnp.zeros_like(into)

            @pl.when(receives)
            def _():
                for j in range(chunks):
                    copies[j].wait_recv()
                    at = lanes(j, CW)
                    arrived = ch_recv[slot, j].astype(F32)
                    into[:, at] = arrived

                    @pl.when(goes_on)
                    def _():
                        ch_send[slot, j] = (
                            arrived * dec_row[:, j * CW : (j + 1) * CW] + local[:, at]
                        ).astype(BF16)
                        copies[j].start()

        return begin, finish

    def collect(l, src, dst):
        near = links.local(src, dst)
        far = links.remote(src, dst, other, c != l)

        @pl.when(c == l)
        def _():
            near.start()

        @pl.when(c != l)
        def _():
            far.start()

        def ready():
            near.wait()
            far.wait_recv()

        return ready

    lt_sends = []

    def collect_transposed(l, kind, src):
        far = links.remote(lt_send, lt.at[kind, c], other, c != l)
        links.pending.pop()

        @pl.when(c == l)
        def _():
            def turn(t, _):
                lt[kind, c, lanes(t), :] = jnp.transpose(src[:, lanes(t)].astype(F32)).astype(BF16)
                return 0

            lax.fori_loop(0, D // LANES, turn, 0)

        @pl.when(c != l)
        def _():
            for l_then, copy in lt_sends:
                if l_then == l:
                    copy.wait_send()

            def turn(t, _):
                lt_send[lanes(t), :] = jnp.transpose(src[:, lanes(t)].astype(F32)).astype(BF16)
                return 0

            lax.fori_loop(0, D // LANES, turn, 0)
            far.start()

        for item in [i for i in lt_sends if i[0] == l]:
            lt_sends.remove(item)
        lt_sends.append((l, far))

        def ready():
            far.wait_recv()

        return ready

    def z_copy(piece, j, up):
        if up:
            slot, peer = j, next_dev
        else:
            slot, peer = jnp.where(j == s - 1, n_seq, j), prev_dev
        index = jnp.where(j < s, j, j - 1)
        return pltpu.make_async_remote_copy(
            src_ref=z_send.at[piece % 2, index],
            dst_ref=z_land.at[piece, slot],
            send_sem=zs_sem.at[piece * (n_seq - 1) + index],
            recv_sem=zr_sem.at[piece * (n_seq + 1) + slot],
            device_id=peer,
            device_id_type=MESH,
        )

    def z_arrived(piece, slot, into):
        pltpu.make_async_remote_copy(
            src_ref=z_send.at[piece % 2, 0],
            dst_ref=z_land.at[piece, slot],
            send_sem=zs_sem.at[piece * (n_seq - 1)],
            recv_sem=zr_sem.at[piece * (n_seq + 1) + slot],
            device_id=prev_dev,
            device_id_type=MESH,
        ).wait_recv()
        return pltpu.make_async_copy(z_land.at[piece, slot], z_in.at[into], zi_sem.at[into])

    def z_block(piece, j, store):
        kind = 0 if piece == 0 else 1
        rows = pl.ds(pl.multiple_of(j * DB, DB), DB)

        def tile(t, _):
            at = lanes(t, ntile)
            store(
                at,
                dot(lt[kind, 0, rows, :], rhs[piece, 0, :, at])
                + dot(lt[kind, 1, rows, :], rhs[piece, 1, :, at]),
            )
            return 0

        lax.fori_loop(0, I // ntile, tile, 0)

    def z_sent(piece):
        for i in range(n_seq - 1):
            pltpu.make_async_remote_copy(
                src_ref=z_send.at[piece % 2, i],
                dst_ref=z_land.at[piece, i],
                send_sem=zs_sem.at[piece * (n_seq - 1) + i],
                recv_sem=zr_sem.at[piece * (n_seq + 1)],
                device_id=next_dev,
                device_id_type=MESH,
            ).wait_send()

    def z_post(piece):
        def one(j, up):
            index = jnp.where(j < s, j, j - 1)

            def store(at, value):
                z_send[piece % 2, index, :, at] = value.astype(BF16)

            z_block(piece, j, store)
            z_copy(piece, j, up).start()
            return 0

        @pl.when(is_first)
        def _():
            if piece == 2:
                z_sent(0)
            lax.fori_loop(0, n_seq - 1, lambda i, _: one(n_seq - 1 - i, True), 0)

        @pl.when(is_last)
        def _():
            if piece == 2:
                z_sent(0)
            lax.fori_loop(0, n_seq - 1, lambda i, _: one(i, False), 0)

    inside = has_prev & has_next
    low_half = s < n_seq // 2

    def z_forward(piece, first):
        def one(j, up):
            index = jnp.where(j < s, j, j - 1)
            load = z_arrived(piece, j, 0)
            load.start()

            def hold(at, value):
                z_acc[:, at] = value

            z_block(piece, j, hold)
            load.wait()
            z_send[piece % 2, index] = (z_acc[...] + z_in[0].astype(F32)).astype(BF16)
            z_copy(piece, j, up).start()
            return 0

        go_up = low_half if first else jnp.logical_not(low_half)
        if piece == 2 and first:

            @pl.when(inside)
            def _():
                z_sent(0)

        @pl.when(inside & go_up)
        def _():
            lax.fori_loop(0, n_seq - 1 - s, lambda i, _: one(n_seq - 1 - i, True), 0)

        @pl.when(inside & jnp.logical_not(go_up))
        def _():
            lax.fori_loop(0, s, lambda i, _: one(i, False), 0)

    def z_final(piece):
        @pl.when(has_prev)
        def _():
            z_arrived(piece, s, 0).start()

        @pl.when(has_next)
        def _():
            z_arrived(piece, n_seq, 1).start()

        def hold(at, value):
            z_acc[:, at] = value

        z_block(piece, s, hold)

        @pl.when(has_prev)
        def _():
            pltpu.make_async_copy(z_land.at[piece, s], z_in.at[0], zi_sem.at[0]).wait()
            z_acc[...] += z_in[0].astype(F32)

        @pl.when(has_next)
        def _():
            pltpu.make_async_copy(z_land.at[piece, n_seq], z_in.at[1], zi_sem.at[1]).wait()
            z_acc[...] += z_in[1].astype(F32)

        save = pltpu.make_async_copy(z_acc, z_out.at[piece], zi_sem.at[0])
        save.start()
        save.wait()

    lane_low = lax.broadcasted_iota(jnp.int32, (T, LANES), 1) < head_size
    later = row_i >= col_i
    earlier = col_i >= row_i

    def spread_heads(l):
        for p in range(pairs):
            at = lanes(p)
            dte[:, at] = jnp.where(
                lane_low, dtv[l, :, 2 * p : 2 * p + 1], dtv[l, :, 2 * p + 1 : 2 * p + 2]
            )
            cume[:, at] = jnp.where(
                lane_low, cum[l, :, 2 * p : 2 * p + 1], cum[l, :, 2 * p + 1 : 2 * p + 2]
            )

    def steps(l):
        def one(p, _):
            at = lanes(p)
            acc = cume[:, at]
            stepped = dte[:, at] * act[l, :, at]
            xtb[:, at] = stepped.astype(BF16)
            xtl[:, at] = (stepped * jnp.exp(acc[T - 1 : T] - acc)).astype(BF16)
            return 0

        lax.fori_loop(0, pairs, one, 0)

    def conv_sum(l, at, v):
        total = prm[l, 5:6, at] + prm[l, 4:5, at] * v[EDGE:]
        moved = []
        for shift in range(1, 4):
            moved.append(pltpu.roll(v, shift, 0)[EDGE:])
            total = total + prm[l, 4 - shift : 5 - shift, at] * moved[-1]
        return total, [v[EDGE:]] + moved

    def forward(l, gap_chain):
        weights_ready(l, [0])
        gain = prm[l, 0:1, :]

        def norm_rows(i, _):
            rows = pl.ds(pl.multiple_of(i * 32, 32), 32)
            v = hb[l, rows, :].astype(F32)
            rstd = lax.rsqrt(jnp.mean(v * v, axis=1, keepdims=True) + EPSILON)
            nm[rows, :] = (v * rstd * gain).astype(BF16)
            return 0

        lax.fori_loop(0, T // 32, norm_rows, 0)

        weights_ready(l, [1, 2, 3])

        def project_x(j, _):
            xin[l, EDGE:, lanes(j, ntile)] = dot(
                nm[...], wxz[l, 0, :, lanes(j, ntile)]
            ).astype(BF16)
            return 0

        lax.fori_loop(0, I // ntile, project_x, 0)
        xin[l, EDGE:, I:] = dot(nm[...], wbc[l]).astype(BF16)

        edge = links.remote(
            xin.at[l, pl.ds(T, EDGE)], xin.at[l, pl.ds(0, EDGE)], next_dev, has_next
        )
        start_if(has_next, edge)

        dt_raw = dot(nm[...], wdt[l])
        hp0 = prm[l, 6:7, I : I + LANES]
        hp1 = prm[l, 6:7, I + LANES : I + 2 * LANES]
        pre_dt = dt_raw + hp0
        sgdt[l] = lax.logistic(pre_dt)
        step = jnp.maximum(pre_dt, 0.0) + jnp.log1p(jnp.exp(-jnp.abs(pre_dt)))
        dtv[l] = step
        cum[l] = exact_dot(tri[...], -jnp.exp(hp1) * step)
        cumT[l] = jnp.transpose(cum[l])

        weights_ready(l, [4])

        def project_z(j, _):
            z[l, :, lanes(j, ntile)] = dot(nm[...], wxz[l, 1, :, lanes(j, ntile)])
            return 0

        lax.fori_loop(0, I // ntile, project_z, 0)

        @pl.when(is_first)
        def _():
            xin[l, :EDGE, :] = jnp.zeros((EDGE, XB), BF16)

        wait_if(has_prev, edge)

        def conv(j, _):
            at = lanes(j)
            total, _ = conv_sum(l, at, xin[l, :, at].astype(F32))
            act[l, :, at] = total * lax.logistic(total)
            return 0

        lax.fori_loop(0, XB // LANES, conv, 0)

        mat_b = act[l, :, I : I + N]
        mat_c = act[l, :, I + N :]
        Bb[l] = mat_b.astype(BF16)
        Cb[l] = mat_c.astype(BF16)
        BT[l] = jnp.transpose(mat_b).astype(BF16)
        CT[l] = jnp.transpose(mat_c).astype(BF16)
        spread_heads(l)
        steps(l)

        def local_state(j, _):
            st_loc[l, :, lanes(j, ntile)] = dot(BT[l], xtl[:, lanes(j, ntile)])
            return 0

        lax.fori_loop(0, I // ntile, local_state, 0)
        begin, finish_chain = chain(
            l, True, st_loc.at[l], jnp.exp(cume[T - 1 : T, :]), s_ent.at[l]
        )
        begin()

        cb = dot_nt(Cb[l], Bb[l])

        def intra(p, _):
            at = lanes(p)
            wide = cume[:, at]
            values = xtb[:, at]
            total = jnp.zeros((T, LANES), F32)
            for half in range(2):
                column = wide[:, half * head_size : half * head_size + 1]
                row = cumT[l, pl.ds(2 * p + half, 1), :]
                decay = jnp.where(later, jnp.exp(jnp.minimum(column - row, 0.0)), 0.0)
                mix = (cb * decay).astype(BF16)
                kept = jnp.where(lane_low == (half == 0), values, jnp.zeros_like(values))
                total = total + dot(mix, kept)
            y0[l, :, at] = total
            return 0

        lax.fori_loop(0, pairs, intra, 0)
        gap_chain()
        finish_chain()

        def gate(p, ssq):
            at = lanes(p)
            carried = dot(Cb[l], s_ent[l, :, at].astype(BF16))
            y = y0[l, :, at] + jnp.exp(cume[:, at]) * carried
            y0[l, :, at] = y
            full = y + prm[l, 7:8, at] * act[l, :, at]
            gate_in = z[l, :, at]
            value = full * (gate_in * lax.logistic(gate_in))
            du[:, at] = value
            dye[:, at] = (value * prm[l, 6:7, at]).astype(BF16)
            return ssq + value * value

        ssq = lax.fori_loop(0, pairs, gate, jnp.zeros((T, LANES), F32))
        finish_rows = exchange_rows(ssq, l)
        weights_ready(l, [5])

        def project_out(j, _):
            rs_send[l, :, lanes(j, ntile)] = dot(dye[...], wo[l, :, lanes(j, ntile)]).astype(BF16)
            return 0

        lax.fori_loop(0, D // ntile, project_out, 0)
        finish_rs = reduce_rows(l)
        qb[l] = lax.rsqrt(finish_rows() / inner_total + EPSILON)

        def scaled(p, _):
            at = lanes(p)
            us[l, :, at] = (du[:, at] * qb[l] * prm[l, 6:7, at]).astype(BF16)
            return 0

        lax.fori_loop(0, pairs, scaled, 0)
        ready_u = collect(l, us.at[l], rhs.at[0, c])
        finish_rs()
        summed = rs_total(l, own_rows)
        q_own = qb[l, own_rows, :][:, :1]
        return (hb[l, own_rows, :].astype(F32) + q_own * summed).astype(BF16), ready_u

    def backward(l, gap_dot, gap_chain, gap_join, gap_rs):
        hp1 = prm[l, 6:7, I + LANES : I + 2 * LANES]

        def start_du(j, acc):
            at = lanes(j, ntile)
            got = dot_nt(eb[l], wo[l, at, :])
            du[:, at] = got
            gate_in = z[l, :, at]
            value = (y0[l, :, at] + prm[l, 7:8, at] * act[l, :, at]) * (
                gate_in * lax.logistic(gate_in)
            )
            value = got * value
            small[l, 6:7, at] = jnp.sum(value * qb[l][:, :1], axis=0, keepdims=True)
            weighted = value * prm[l, 6:7, at]
            return acc + weighted[:, :LANES] + weighted[:, LANES:]

        acc = lax.fori_loop(0, I // ntile, start_du, jnp.zeros((T, LANES), F32))
        finish_rows = exchange_rows(acc, 2 + l)
        spread_heads(l)
        steps(l)
        gap_dot()
        dot_all = finish_rows()

        def through_gate(p, _):
            at = lanes(p)
            q = qb[l]
            gate_in = z[l, :, at]
            sig = lax.logistic(gate_in)
            silu = gate_in * sig
            x_now = act[l, :, at]
            full = y0[l, :, at] + prm[l, 7:8, at] * x_now
            dg = q * (du[:, at] * prm[l, 6:7, at]) - full * silu * (q * q * q) * (
                dot_all / inner_total
            )
            d_y = dg * silu
            gp[l, :, lanes(p + pairs)] = (
                dg * full * sig * (1.0 + gate_in * (1.0 - sig))
            ).astype(BF16)
            small[l, 7:8, at] = jnp.sum(d_y * x_now, axis=0, keepdims=True)
            dy[:, at] = d_y
            dyb[:, at] = d_y.astype(BF16)
            dye[:, at] = (d_y * jnp.exp(cume[:, at])).astype(BF16)
            return 0

        lax.fori_loop(0, pairs, through_gate, 0)

        def local_state(j, _):
            dst_loc[:, lanes(j, ntile)] = dot(CT[l], dye[:, lanes(j, ntile)])
            return 0

        lax.fori_loop(0, I // ntile, local_state, 0)
        begin, finish_chain = chain(
            2 + l, False, dst_loc, jnp.exp(cume[T - 1 : T, :]), gin
        )
        begin()
        ready_z = collect(l, gp.at[l, :, pl.ds(I, I)], rhs.at[1, c])

        cbt = dot_nt(Bb[l], Cb[l])
        dcbt[...] = jnp.zeros_like(dcbt)

        def intra(p, _):
            at = lanes(p)
            wide = cume[:, at]
            values = xtb[:, at]
            grads = dyb[:, at]
            total = jnp.zeros((T, LANES), F32)
            for half in range(2):
                column = wide[:, half * head_size : half * head_size + 1]
                row = cumT[l, pl.ds(2 * p + half, 1), :]
                decay = jnp.where(earlier, jnp.exp(jnp.minimum(row - column, 0.0)), 0.0)
                mix = (cbt * decay).astype(BF16)
                kept = jnp.where(lane_low == (half == 0), grads, jnp.zeros_like(grads))
                total = total + dot(mix, kept)
                dcbt[...] += dot_nt(values, kept) * decay
            du[:, at] = total
            return 0

        lax.fori_loop(0, pairs, intra, 0)
        gap_chain(ready_z)
        finish_chain()

        def join(p, carry):
            sum_v, sum_w = carry
            at = lanes(p)
            into = gin[:, at]
            acc = cume[:, at]
            end = acc[T - 1 : T]
            got = du[:, at] + jnp.exp(end - acc) * dot(Bb[l], into.astype(BF16))
            x_now = act[l, :, at]
            d_y = dy[:, at]
            leaving = s_ent[l, :, at] * jnp.exp(end) + st_loc[l, :, at]
            final = jnp.sum(into * leaving, axis=0, keepdims=True)
            v = dyb[:, at].astype(F32) * y0[l, :, at] - xtb[:, at].astype(F32) * got
            is_end = lax.broadcasted_iota(jnp.int32, (T, LANES), 0) == T - 1
            v = v + jnp.where(is_end, final, 0.0)
            dact[:, at] = dte[:, at] * got + prm[l, 7:8, at] * d_y
            picks = et[at, :]
            return (sum_v + split_dot(v, picks), sum_w + split_dot(x_now * got, picks))

        zero = jnp.zeros((T, LANES), F32)
        sum_v, sum_w = lax.fori_loop(0, pairs, join, (zero, zero))

        dcb_low = dcbt[...].astype(BF16)
        gin_low = gin[...].astype(BF16)
        ent_low = s_ent[l].astype(BF16)
        dact[:, I : I + N] = dot(dcb_low, Cb[l]) + dot_nt(xtl[...], gin_low)
        dact[:, I + N :] = dot_tn(dcb_low, Bb[l]) + dot_nt(dye[...], ent_low)

        def conv_pre(j, _):
            at = lanes(j)
            total, moved = conv_sum(l, at, xin[l, :, at].astype(F32))
            sig = lax.logistic(total)
            got = dact[:, at] * (sig * (1.0 + total * (1.0 - sig)))
            dpx[:T, at] = got
            edge_send[l, :, at] = got[:EDGE].astype(BF16)
            small[l, 5:6, at] = jnp.sum(got, axis=0, keepdims=True)
            for shift in range(4):
                small[l, 4 - shift : 5 - shift, at] = jnp.sum(
                    got * moved[shift], axis=0, keepdims=True
                )
            return 0

        lax.fori_loop(0, XB // LANES, conv_pre, 0)
        edge = links.remote(edge_send.at[l], edge_recv.at[l], prev_dev, has_prev)
        start_if(has_prev, edge)

        d_log = lax.dot_general(
            tri[...], sum_v, (((0,), (0,)), ((), ())),
            precision=lax.Precision.HIGHEST, preferred_element_type=F32,
        )
        rate = -jnp.exp(hp1)
        d_raw = (sum_w + d_log * rate) * sgdt[l]
        small[l, 6:7, I : I + LANES] = jnp.sum(d_raw, axis=0, keepdims=True)
        small[l, 6:7, I + LANES : I + 2 * LANES] = jnp.sum(
            d_log * rate * dtv[l], axis=0, keepdims=True
        )
        d_raw = jnp.where(lax.broadcasted_iota(jnp.int32, (T, LANES), 1) < heads, d_raw, 0.0)
        gp[l, :, 2 * I + 2 * N :] = d_raw.astype(BF16)
        dt_rows = bc_rows.shape[1] - Q2
        bc_rows[l, Q2:, :] = jnp.transpose(d_raw)[:dt_rows].astype(BF16)
        gap_join()

        @pl.when(is_last)
        def _():
            dpx[T:, :] = jnp.zeros((EDGE, XB), F32)

        @pl.when(has_next)
        def _():
            edge.wait_recv()
            dpx[T:, :] = edge_recv[l].astype(F32)

        def conv_in(j, _):
            at = lanes(j)
            v = dpx[:, at]
            total = prm[l, 4:5, at] * v[:T]
            for shift in range(1, 4):
                moved = pltpu.roll(v, T + EDGE - shift, 0)
                total = total + prm[l, 4 - shift : 5 - shift, at] * moved[:T]
            dact[:, at] = total
            return 0

        lax.fori_loop(0, XB // LANES, conv_in, 0)
        gp[l, :, :I] = dact[:, :I].astype(BF16)
        gp[l, :, 2 * I : 2 * I + 2 * N] = dact[:, I:].astype(BF16)

        def normed_all(j, _):
            at = lanes(j, ntile)
            total = dot_nt(gp[l, :, I : 2 * I], wxz[l, 1, at, :])
            total = total + dot_nt(gp[l, :, :I], wxz[l, 0, at, :])
            total = total + dot_nt(gp[l, :, 2 * I : 2 * I + 2 * N], wbc[l, at, :])
            total = total + dot_nt(gp[l, :, 2 * I + 2 * N :], wdt[l, at, :])
            rs_send[1 - l, :, at] = total.astype(BF16)
            return 0

        for copy in rs_copies[1 - l]:
            copy.wait_send()
        lax.fori_loop(0, D // ntile, normed_all, 0)
        finish_rs = reduce_rows(1 - l)
        ready_x = collect(l, gp.at[l, :, pl.ds(0, I)], rhs.at[2, c])
        gap_rs(ready_x)
        finish_rs()
        got = rs_total(1 - l, own_rows)
        v = hb[l, own_rows, :].astype(F32)
        rstd = lax.rsqrt(jnp.mean(v * v, axis=1, keepdims=True) + EPSILON)
        small[l, 0:1, :] = jnp.sum(got * v * rstd, axis=0, keepdims=True)
        hat = got * prm[l, 0:1, :]
        inner = jnp.sum(hat * v, axis=1, keepdims=True)
        return (
            rstd * hat - v * (rstd * rstd * rstd) * inner / D
            + eb[l, own_rows, :].astype(F32)
        )

    def bc_start(l):
        copies = []
        for d, peer in enumerate(head_peers):
            copy = links.remote(
                gp.at[l, :, pl.ds(2 * I, 2 * N)], bc_recv.at[l, d], peer
            )
            copy.start()
            copies.append(copy)
        return copies

    def bc_mid(l, copies):
        total = gp[l, :, 2 * I : 2 * I + 2 * N].astype(F32)
        for d, copy in enumerate(copies):
            copy.wait_recv()
            total = total + bc_recv[l, d].astype(F32)
        bc_t[...] = jnp.transpose(total).astype(BF16)
        bc_rows[l, :Q2, :] = bc_t[pl.ds(pl.multiple_of(k * Q2, Q2), Q2), :]
        return collect(l, bc_rows.at[l], bc_rhs.at[c])

    def bc_block(j):
        rows = pl.ds(pl.multiple_of(j * DB, DB), DB)
        return dot_nt(bc_rhs[0], lt[1, 0, rows, :]) + dot_nt(bc_rhs[1], lt[1, 1, rows, :])

    def bc_copies(l):
        return [
            links.remote(bc_send.at[d], bc_land.at[d], peer, c == l)
            for d, peer in enumerate(seq_peers)
        ]

    def bc_out_start(ready, copies):
        ready()
        for d, copy in enumerate(copies):
            bc_send[d] = bc_block(lax.rem(s + d + 1, n_seq)).astype(BF16)
            copy.start()

    def bc_gather_copies(l):
        return [
            links.remote(bc_all.at[k], bc_all.at[k], peer, c == l) for peer in head_peers
        ]

    def bc_sum(copies, gathers):
        total = bc_block(s)
        for d, copy in enumerate(copies):
            copy.wait_recv()
            total = total + bc_land[d].astype(F32)
        bc_all[k] = total[:Q2]
        bc_out[2 * N :, :] = total[Q2:]
        for copy in gathers:
            copy.start()

    def bc_finish(gathers):
        for copy in gathers:
            copy.wait_recv()
        for i in range(n_head):
            bc_out[i * Q2 : (i + 1) * Q2, :] = bc_all[i]

    def small_start(l):
        copy = links.remote(small.at[l], sm_o, other, c != l)
        start_if(c != l, copy)
        heads_to = [
            links.remote(sm_t, sm_h.at[d], peer, c == l) for d, peer in enumerate(head_peers)
        ]
        seqs_to = [
            links.remote(sm_u, sm_z.at[d], peer, c == l) for d, peer in enumerate(seq_peers)
        ]
        return copy, heads_to, seqs_to

    def small_heads(l, copies):
        copies[0].wait_recv()
        sm_t[...] = small[l] + sm_o[...]
        for copy in copies[1]:
            copy.start()

    def small_seqs(copies):
        sm_u[...] = sm_t[...]
        for d, copy in enumerate(copies[1]):
            copy.wait_recv()
            sm_u[0:1, :] += sm_h[d, 0:1, :]
            sm_u[1:6, I : I + 2 * N] += sm_h[d, 1:6, I : I + 2 * N]
        for copy in copies[2]:
            copy.start()

    def small_finish(copies):
        total = sm_u[...]
        for d, copy in enumerate(copies[2]):
            copy.wait_recv()
            total = total + sm_z[d]
        small_out[...] = total
        small_out[7:8, I : I + LANES] = split_dot(total[:, :I], et[...])[7:8]

    def deliver(kind, rows):
        copy = links.remote(end_send.at[kind], ends.at[c], other, c != kind)

        @pl.when(c == kind)
        def _():
            ends[c] = rows

        @pl.when(c != kind)
        def _():
            end_send[kind] = rows
            copy.start()

        def finish():
            wait_if(c == kind, copy)

        return finish

    on0, on1 = pl.when(c == 0), pl.when(c == 1)
    got = {}

    def gap():
        got["n0"] = collect_transposed(0, 1, nm)

    rows, ready_u0 = forward(0, gap)
    finish_gather = gather_rows(hb.at[1], rows)
    load_e.wait()
    ready_e1 = collect_transposed(1, 0, eb.at[1])
    finish_gather()

    def gap():
        got["n1"] = collect_transposed(1, 1, nm)

    rows, ready_u1 = forward(1, gap)
    finish_out = deliver(1, rows.astype(F32))

    def gap_dot():
        @on1
        def _():
            ready_u1()
            ready_e1()
            z_post(0)

    def gap_chain(ready):
        @on1
        def _():
            got["n1"]()
            ready()
            z_post(1)

    def gap_join():
        @on1
        def _():
            z_forward(0, True)

    def gap_rs(ready):
        got["bc1"] = bc_start(1)

        @on1
        def _():
            ready()
            z_forward(0, False)
            z_post(2)
            z_forward(1, True)

    rows = backward(1, gap_dot, gap_chain, gap_join, gap_rs)
    finish_gather = gather_rows(eb.at[0], rows.astype(BF16))
    small1 = small_start(1)
    ready_bc1 = bc_mid(1, got["bc1"])
    bc_to1, bc_g1 = bc_copies(1), bc_gather_copies(1)
    finish_gather()

    def gap_dot():
        got["e0"] = collect_transposed(0, 0, eb.at[0])

        @on1
        def _():
            z_forward(1, False)
            bc_out_start(ready_bc1, bc_to1)
            small_heads(1, small1)

        @on0
        def _():
            ready_u0()
            got["e0"]()
            z_post(0)

    def gap_chain(ready):
        @on1
        def _():
            z_forward(2, True)
            small_seqs(small1)

        @on0
        def _():
            got["n0"]()
            ready()
            z_post(1)

    def gap_join():
        @on1
        def _():
            z_forward(2, False)

        @on0
        def _():
            z_forward(0, True)

    def gap_rs(ready):
        got["bc0"] = bc_start(0)

        @on1
        def _():
            z_final(0)
            bc_sum(bc_to1, bc_g1)

        @on0
        def _():
            ready()
            z_forward(0, False)
            z_post(2)
            z_forward(1, True)

    rows = backward(0, gap_dot, gap_chain, gap_join, gap_rs)
    finish_in = deliver(0, rows)
    small0 = small_start(0)
    ready_bc0 = bc_mid(0, got["bc0"])
    bc_to0, bc_g0 = bc_copies(0), bc_gather_copies(0)

    @on1
    def _():
        small_finish(small1)
        z_final(1)
        z_final(2)
        bc_finish(bc_g1)

    @on0
    def _():
        z_forward(1, False)
        bc_out_start(ready_bc0, bc_to0)
        small_heads(0, small0)
        z_forward(2, True)
        small_seqs(small0)
        z_forward(2, False)
        bc_sum(bc_to0, bc_g0)
        z_final(0)
        z_final(1)
        small_finish(small0)
        bc_finish(bc_g0)
        z_final(2)

    finish_out()
    finish_in()
    save = links.local(ends, ends_out)
    save.start()
    save.wait()
    z_sent(1)
    z_sent(2)
    for l, copy in lt_sends:

        @pl.when(c != l)
        def _():
            copy.wait_send()

    for slot in range(2):
        for copy in rs_copies[slot]:
            copy.wait_send()
    links.drain()


def run_layers(tokens, cotangent, w_xz, w_bc, w_dt, w_out, prm, heads):
    n_seq, n_head = lax.axis_size("seq"), lax.axis_size("head")
    _, T, D = tokens.shape
    I = w_xz.shape[2]
    N = w_bc.shape[1] // 2
    XB = I + 2 * N
    G = 2 * I + 2 * N + LANES
    Q = T // n_head
    DB = D // n_seq
    BR = 2 * N // n_head + (heads + 15) // 16 * 16
    sems = 88 + 4 * (n_seq + n_head)
    S = jax.ShapeDtypeStruct
    V = pltpu.VMEM
    dma = pltpu.SemaphoreType.DMA
    vm = pl.BlockSpec(memory_space=pltpu.VMEM)
    hbm = pl.BlockSpec(memory_space=pl.ANY)
    scratch = [
        V((2, 2, D, I), BF16), V((2, D, 2 * N), BF16), V((2, D, LANES), BF16), V((2, I, D), BF16),
        V((2, 8, D), F32), V((2, T, D), BF16), V((2, T, D), BF16), V((T, D), BF16),
        V((2, T + EDGE, XB), BF16), V((2, T, I), F32), V((2, T, XB), F32),
        V((T, I), F32), V((T, I), F32), V((2, T, I), F32),
        V((2, T, LANES), F32), V((2, T, LANES), F32), V((2, T, LANES), F32), V((2, LANES, T), F32),
        V((2, N, T), BF16), V((2, N, T), BF16), V((2, T, N), BF16), V((2, T, N), BF16),
        V((2, N, I), F32), V((2, N, I), F32), V((T, I), BF16), V((T, I), BF16),
        V((2, T, LANES), F32),
        V((T, I), F32), V((T, I), F32), V((T, I), BF16), V((T, I), BF16),
        V((N, I), F32), V((N, I), F32), V((T, XB), F32), V((T + EDGE, XB), F32),
        V((T, T), F32), V((2, T, G), BF16), V((2, T, I), BF16), V((2, 8, D), F32),
        V((4, 8, T), F32), V((4, n_head - 1, 8, T), F32),
        V((2, T, D), BF16), V((2, n_head - 1, Q, D), BF16),
        V((4, 3, N, I // 3), BF16), V((4, 3, N, I // 3), BF16),
        V((2, EDGE, XB), BF16), V((2, EDGE, XB), BF16),
        V((2, Q, D), F32), V((2, Q, D), F32), V((I, LANES), BF16), V((T, T), F32),
        V((2, 2, D, T), BF16), V((D, T), BF16), V((3, 2, T, I), BF16),
        V((2, n_seq - 1, DB, I), BF16), V((2, DB, I), BF16), V((DB, I), F32),
        V((2, n_head - 1, T, 2 * N), BF16), V((2 * N, T), BF16), V((2, BR, T), BF16),
        V((2, BR, T), BF16), V((n_seq - 1, BR, DB), BF16), V((n_seq - 1, BR, DB), BF16),
        V((n_head, 2 * N // n_head, DB), F32),
        V((8, D), F32), V((8, D), F32), V((n_head - 1, 8, D), F32), V((8, D), F32),
        V((n_seq - 1, 8, D), F32),
        dma((24,)), dma((sems,)), dma((sems,)),
        dma((3 * (n_seq - 1),)), dma((3 * (n_seq + 1),)), dma((2,)),
    ]
    dims = (n_seq, n_head, T, D, I, N, heads)
    return pl.pallas_call(
        functools.partial(layer_kernel, dims),
        out_shape=(
            S((2, Q, D), F32), S((3, DB, I), F32),
            S((2 * N + BR - 2 * N // n_head, DB), F32), S((8, D), F32),
            S((3, n_seq + 1, DB, I), BF16),
        ),
        in_specs=[hbm] * 7,
        out_specs=(hbm, hbm, vm, vm, hbm),
        scratch_shapes=scratch,
        compiler_params=pltpu.CompilerParams(
            collective_id=0, has_side_effects=True, vmem_limit_bytes=63 * 2**20
        ),
        name="layers",
    )(tokens, cotangent, w_xz, w_bc, w_dt, w_out, prm)


def body(
    tokens, cotangent, norm_gain, w_xz, w_bc, w_dt, conv_x, conv_bc, head_params, out_gain, w_out
):
    D = tokens.shape[2]
    I = w_xz.shape[3]
    N2 = w_bc.shape[2]
    heads = w_dt.shape[2]
    lane_pad = LANES - heads

    def wide(a):
        return jnp.pad(a, ((0, 0), (0, D - a.shape[1])))

    params = jnp.concatenate(
        [
            norm_gain,
            wide(jnp.concatenate([conv_x[0], conv_bc[0]], axis=1)),
            wide(
                jnp.concatenate(
                    [
                        out_gain,
                        jnp.pad(head_params[0, 0:1], ((0, 0), (0, lane_pad))),
                        jnp.pad(head_params[0, 1:2], ((0, 0), (0, lane_pad))),
                    ],
                    axis=1,
                )
            ),
            wide(jnp.repeat(head_params[0, 2:3], I // heads, axis=1)),
        ],
        axis=0,
    )
    w_xz2 = jnp.swapaxes(w_xz[0], 0, 1)
    w_dt2 = jnp.pad(w_dt[0], ((0, 0), (0, lane_pad)))
    ends, z_out, bc_out, small, _ = run_layers(
        tokens, cotangent, w_xz2, w_bc[0], w_dt2, w_out[0], params, heads
    )
    g_skip = small[7, I : I + heads]
    g_head = jnp.stack([small[6, I : I + heads], small[6, I + LANES : I + LANES + heads], g_skip])
    return (
        ends[None],
        small[None, 0],
        jnp.stack([z_out[2], z_out[1]], axis=1)[None],
        bc_out[:N2].T[None],
        bc_out[N2 : N2 + heads].T[None],
        small[None, 1:6, :I],
        small[None, 1:6, I : I + N2],
        g_head[None],
        small[None, 6, :I],
        z_out[0].T[None],
    )


def solution(mesh):
    placed = (
        P(None, "seq", None),
        P(None, "seq", None),
        P("section", None),
        P("section", None, None, "head"),
        P("section", None, None),
        P("section", None, "head"),
        P("section", None, "head"),
        P("section", None, None),
        P("section", None, "head"),
        P("section", "head"),
        P("section", "head", None),
    )
    return jax.shard_map(
        body,
        mesh=mesh,
        in_specs=placed,
        out_specs=(
            P("section", None, ("seq", "head"), None),
            P("section", None),
            P("section", "seq", None, "head"),
            P("section", "seq", None),
            P("section", "seq", "head"),
            P("section", None, "head"),
            P("section", None, None),
            P("section", None, "head"),
            P("section", "head"),
            P("section", "head", "seq"),
        ),
        check_vma=False,
    )
```

```python
import functools

import jax
import jax.numpy as jnp
from jax import lax
from jax.experimental import pallas as pl
from jax.experimental.pallas import tpu as pltpu
from jax.sharding import PartitionSpec as P

EPSILON = 1e-05
MESH = pl.DeviceIdType.MESH
LANES = 128
EDGE = 16
F32 = jnp.float32
BF16 = jnp.bfloat16


def dot(a, b):
    return lax.dot_general(a, b, (((1,), (0,)), ((), ())), preferred_element_type=F32)


def dot_nt(a, b):
    return lax.dot_general(a, b, (((1,), (1,)), ((), ())), preferred_element_type=F32)


def dot_tn(a, b):
    return lax.dot_general(a, b, (((0,), (0,)), ((), ())), preferred_element_type=F32)


def exact_dot(a, b):
    return lax.dot_general(
        a, b, (((1,), (0,)), ((), ())), precision=lax.Precision.HIGHEST, preferred_element_type=F32
    )


def split_dot(a, b):
    high = a.astype(BF16)
    return dot(high, b) + dot((a - high.astype(F32)).astype(BF16), b)


class Links:
    def __init__(self, local_sem, send_sem, recv_sem):
        self.local_sem, self.send_sem, self.recv_sem = local_sem, send_sem, recv_sem
        self.local_count = 0
        self.count = 0
        self.pending = []

    def local(self, src, dst):
        index = self.local_count
        assert index < self.local_sem.shape[0]
        self.local_count += 1
        return pltpu.make_async_copy(src, dst, self.local_sem.at[index])

    def remote(self, src, dst, peer, when=None):
        index = self.count
        assert index < self.send_sem.shape[0]
        self.count += 1
        copy = pltpu.make_async_remote_copy(
            src_ref=src,
            dst_ref=dst,
            send_sem=self.send_sem.at[index],
            recv_sem=self.recv_sem.at[index],
            device_id=peer,
            device_id_type=MESH,
        )
        self.pending.append((copy, when))
        return copy

    def drain(self):
        for copy, when in self.pending:
            if when is None:
                copy.wait_send()
            else:

                @pl.when(when)
                def _():
                    copy.wait_send()


def wait_if(condition, copy):
    @pl.when(condition)
    def _():
        copy.wait_recv()


def start_if(condition, copy):
    @pl.when(condition)
    def _():
        copy.start()


def lanes(i, width=LANES):
    if isinstance(i, int):
        return pl.ds(i * width, width)
    return pl.ds(pl.multiple_of(i * width, width), width)


def layer_kernel(dims, *refs):
    (n_seq, n_head, T, D, I, N, heads) = dims
    (
        tokens, cotangent, w_xz, w_bc, w_dt, w_out, in_gain, in_conv_x, in_conv_bc, in_head, in_out,
        ends_out, gw_out, gw_xz, gw_bc, gw_dt, g_gain, g_conv_x, g_conv_bc, g_head, g_out, z_land, far_lt, far_rhs,
        wxz, wbc, wdt, wo, prm, hb, eb, nm, xin, z, act, dte, cume, y0,
        sgdt, dtv, cum, cumT, CT, BT, Bb, Cb, st_loc, s_ent, xtb, xtl, qb,
        du, dy, dyb, dye, dst_loc, gin, dact, dcbt, gp, us, small,
        row_send, row_recv, rs_send, rs_recv, ch_send, ch_recv, edge_send, edge_recv,
        end_send, ends, et, tri,
        lt, lt_send, rhs, z_send, z_in, z_acc, far_l, far_r, bc_recv, bc_t, bc_rows, bc_rhs, bc_send, bc_land, bc_all,
        sm_o, sm_t, sm_h, sm_u, sm_z,
        local_sem, send_sem, recv_sem, zs_sem, zr_sem, zi_sem,
    ) = refs
    c = lax.axis_index("section")
    s = lax.axis_index("seq")
    k = lax.axis_index("head")
    links = Links(local_sem, send_sem, recv_sem)
    Q = T // n_head
    XB = I + 2 * N
    DB = D // n_seq
    pairs = I // LANES
    head_size = I // heads
    is_first = s == 0
    is_last = s == n_seq - 1
    has_prev = s > 0
    has_next = s < n_seq - 1
    other = {"section": 1 - c}
    prev_dev = {"seq": jnp.maximum(s - 1, 0)}
    next_dev = {"seq": jnp.minimum(s + 1, n_seq - 1)}
    head_peers = [{"head": lax.rem(k + d, n_head)} for d in range(1, n_head)]
    seq_peers = [{"seq": lax.rem(s + d, n_seq)} for d in range(1, n_seq)]
    own_rows = pl.ds(pl.multiple_of(k * Q, Q), Q)
    chunks = 3
    CW = I // chunks
    ntile = 256
    inner_total = I * n_head
    Q2 = 2 * N // n_head
    rs_copies = {}

    barrier = pltpu.get_barrier_semaphore()
    for peer in [other] + head_peers + seq_peers:
        pl.semaphore_signal(barrier, inc=1, device_id=peer, device_id_type=MESH)

    load_h = links.local(tokens.at[c], hb.at[0])
    load_e = links.local(cotangent.at[c], eb.at[1])
    load_h.start()
    parts = (
        (w_xz.at[0], wxz.at[c, 0]),
        (w_bc, wbc.at[c]),
        (w_dt, wdt.at[c]),
        (w_xz.at[1], wxz.at[c, 1]),
        (w_out, wo.at[c]),
    )
    mine = [links.local(src, dst) for src, dst in parts]
    for copy in mine:
        copy.start()
    load_e.start()
    pl.semaphore_wait(barrier, n_head + n_seq - 1)
    low_row = lax.broadcasted_iota(jnp.int32, (1, LANES), 1) < head_size
    prm[c] = jnp.zeros((8, D), F32)
    prm[c, 0:1, :] = in_gain[...]
    for r in range(5):
        prm[c, 1 + r : 2 + r, :I] = in_conv_x[r]
        prm[c, 1 + r : 2 + r, I : I + 2 * N] = in_conv_bc[r]
    prm[c, 6:7, :I] = in_out[...]
    prm[c, 6:7, I : I + heads] = in_head[0]
    prm[c, 6:7, I + LANES : I + LANES + heads] = in_head[1]
    skips = in_head[2]
    for p in range(pairs):
        prm[c, 7:8, lanes(p)] = jnp.where(
            low_row, skips[:, 2 * p : 2 * p + 1], skips[:, 2 * p + 1 : 2 * p + 2]
        )
    theirs = [links.remote(prm.at[c], prm.at[c], other)]
    theirs += [links.remote(src, dst, other) for src, dst in parts]
    for copy in theirs:
        copy.start()

    def weights_ready(layer, which):
        @pl.when(c == layer)
        def _():
            for i in which:
                if i:
                    mine[i - 1].wait()

        @pl.when(c != layer)
        def _():
            for i in which:
                theirs[i].wait_recv()

    row_i = lax.broadcasted_iota(jnp.int32, (T, T), 0)
    col_i = lax.broadcasted_iota(jnp.int32, (T, T), 1)
    tri[...] = jnp.where(row_i >= col_i, 1.0, 0.0)
    er = lax.broadcasted_iota(jnp.int32, (I, LANES), 0)
    ec = lax.broadcasted_iota(jnp.int32, (I, LANES), 1)
    et[...] = jnp.where(
        (er >= ec * head_size) & (er < (ec + 1) * head_size), 1.0, 0.0
    ).astype(BF16)
    small[...] = jnp.zeros_like(small)
    load_h.wait()

    def exchange_rows(total_cols, slot):
        summed = jnp.sum(total_cols, axis=1, keepdims=True)
        as_row = jnp.transpose(jnp.broadcast_to(summed, (T, LANES)))[:8]
        row_send[slot] = as_row
        copies = []
        for d, peer in enumerate(head_peers):
            copy = links.remote(row_send.at[slot], row_recv.at[slot, d], peer)
            copy.start()
            copies.append(copy)

        def finish():
            total = row_send[slot]
            for d, copy in enumerate(copies):
                copy.wait_recv()
                total = total + row_recv[slot, d]
            wide = jnp.broadcast_to(total[:1], (LANES, T))
            return jnp.transpose(wide)

        return finish

    def reduce_rows(slot):
        copies = []
        for d, peer in enumerate(head_peers):
            rows = pl.ds(pl.multiple_of(lax.rem(k + d + 1, n_head) * Q, Q), Q)
            copy = links.remote(rs_send.at[slot, rows], rs_recv.at[slot, d], peer)
            copy.start()
            links.pending.pop()
            copies.append(copy)
        rs_copies[slot] = copies

        def finish():
            for copy in copies:
                copy.wait_recv()

        return finish

    def rs_total(slot, rows_at):
        total = rs_send[slot, rows_at, :].astype(F32)
        for d in range(n_head - 1):
            total = total + rs_recv[slot, d, :, :].astype(F32)
        return total

    def gather_rows(target, rows):
        target[own_rows, :] = rows
        copies = []
        for peer in head_peers:
            copy = links.remote(target.at[own_rows], target.at[own_rows], peer)
            copy.start()
            copies.append(copy)

        def finish():
            for copy in copies:
                copy.wait_recv()

        return finish

    def chain(slot, forward, local, dec_row, into):
        starts, goes_on = (is_first, has_next) if forward else (is_last, has_prev)
        receives = has_prev if forward else has_next
        peer = next_dev if forward else prev_dev
        copies = []
        for j in range(chunks):
            copies.append(
                links.remote(ch_send.at[slot, j], ch_recv.at[slot, j], peer, goes_on)
            )

        def begin():
            @pl.when(starts)
            def _():
                for j in range(chunks):
                    ch_send[slot, j] = local[:, lanes(j, CW)].astype(BF16)
                    start_if(goes_on, copies[j])

        def finish():
            @pl.when(starts)
            def _():
                into[...] = jnp.zeros_like(into)

            @pl.when(receives)
            def _():
                for j in range(chunks):
                    copies[j].wait_recv()
                    at = lanes(j, CW)
                    arrived = ch_recv[slot, j].astype(F32)
                    into[:, at] = arrived

                    @pl.when(goes_on)
                    def _():
                        ch_send[slot, j] = (
                            arrived * dec_row[:, j * CW : (j + 1) * CW] + local[:, at]
                        ).astype(BF16)
                        copies[j].start()

        return begin, finish

    def collect(l, src, dst):
        near = links.local(src, dst)
        far = links.remote(src, dst, other, c != l)

        @pl.when(c == l)
        def _():
            near.start()

        @pl.when(c != l)
        def _():
            far.start()

        def ready():
            near.wait()
            far.wait_recv()

        return ready

    lt_sends = []

    def collect_transposed(l, kind, src):
        far = links.remote(lt_send, lt.at[kind, c], other, c != l)
        links.pending.pop()

        @pl.when(c == l)
        def _():
            def turn(t, _):
                lt[kind, c, lanes(t), :] = jnp.transpose(src[:, lanes(t)].astype(F32)).astype(BF16)
                return 0

            lax.fori_loop(0, D // LANES, turn, 0)

        @pl.when(c != l)
        def _():
            for l_then, copy in lt_sends:
                if l_then == l:
                    copy.wait_send()

            def turn(t, _):
                lt_send[lanes(t), :] = jnp.transpose(src[:, lanes(t)].astype(F32)).astype(BF16)
                return 0

            lax.fori_loop(0, D // LANES, turn, 0)
            far.start()

        for item in [i for i in lt_sends if i[0] == l]:
            lt_sends.remove(item)
        lt_sends.append((l, far))

        def ready():
            far.wait_recv()

        return ready

    low_half = s < n_seq // 2
    is_end = is_first | is_last
    inside = has_prev & has_next
    near = (s == 1) | (s == n_seq - 2)
    inward = {"seq": jnp.where(is_first, 1, jnp.where(is_last, n_seq - 2, s))}

    def far_copies(l):
        when = is_end & (c == l)
        return (
            [links.remote(lt.at[i], far_lt.at[i], inward, when) for i in range(2)],
            [links.remote(rhs.at[i], far_rhs.at[i], inward, when) for i in range(3)],
        )

    def z_copy(piece, j, up):
        if up:
            slot, peer = j, next_dev
        else:
            slot, peer = jnp.where(j == s - 1, n_seq, j), prev_dev
        index = jnp.where(j < s, j, j - 1)
        return pltpu.make_async_remote_copy(
            src_ref=z_send.at[piece % 2, index],
            dst_ref=z_land.at[piece, slot],
            send_sem=zs_sem.at[piece * (n_seq - 1) + index],
            recv_sem=zr_sem.at[piece * (n_seq + 1) + slot],
            device_id=peer,
            device_id_type=MESH,
        )

    def z_arrived(piece, slot, into):
        pltpu.make_async_remote_copy(
            src_ref=z_send.at[piece % 2, 0],
            dst_ref=z_land.at[piece, slot],
            send_sem=zs_sem.at[piece * (n_seq - 1)],
            recv_sem=zr_sem.at[piece * (n_seq + 1) + slot],
            device_id=prev_dev,
            device_id_type=MESH,
        ).wait_recv()
        return pltpu.make_async_copy(z_land.at[piece, slot], z_in.at[into], zi_sem.at[into])

    def z_block(piece, j, store, far):
        kind = 0 if piece == 0 else 1
        rows = pl.ds(pl.multiple_of(j * DB, DB), DB)
        if far:
            load = pltpu.make_async_copy(far_lt.at[kind, :, rows], far_l, zi_sem.at[2])
            load.start()
            load.wait()

        def tile(t, _):
            at = lanes(t, ntile)
            value = dot(lt[kind, 0, rows, :], rhs[piece, 0, :, at]) + dot(
                lt[kind, 1, rows, :], rhs[piece, 1, :, at]
            )
            if far:
                value = value + dot(far_l[0], far_r[0, :, at]) + dot(far_l[1], far_r[1, :, at])
            store(at, value)
            return 0

        lax.fori_loop(0, I // ntile, tile, 0)

    def z_one(piece, j, up):
        index = jnp.where(j < s, j, j - 1)
        if piece == 2:
            z_sent(0, index)

        def store(at, value):
            z_send[piece % 2, index, :, at] = value.astype(BF16)

        z_block(piece, j, store, False)
        z_copy(piece, j, up).start()
        return 0

    def z_first(piece):
        @pl.when(is_first)
        def _():
            lax.fori_loop(0, n_seq - 1, lambda i, _: z_one(piece, n_seq - 1 - i, True), 0)

    def z_last(piece):
        @pl.when(is_last)
        def _():
            lax.fori_loop(0, n_seq - 1, lambda i, _: z_one(piece, i, False), 0)

    def far_load(piece):
        load = pltpu.make_async_copy(far_rhs.at[piece], far_r, zi_sem.at[3])
        load.start()
        load.wait()

    def z_sent(piece, index):
        pltpu.make_async_remote_copy(
            src_ref=z_send.at[piece % 2, index],
            dst_ref=z_land.at[piece, 0],
            send_sem=zs_sem.at[piece * (n_seq - 1) + index],
            recv_sem=zr_sem.at[piece * (n_seq + 1)],
            device_id=next_dev,
            device_id_type=MESH,
        ).wait_send()

    def z_forward(copies, piece, up, first, use_far):
        mine = inside & (low_half if up == first else jnp.logical_not(low_half))
        count = n_seq - 1 - s if up else s

        def one(i, _, far):
            j = n_seq - 1 - i if up else i
            index = jnp.where(j < s, j, j - 1)
            if piece == 2:
                z_sent(0, index)
            if not far:
                load = z_arrived(piece, j, 0)
                load.start()
                load.wait()

            def store(at, value):
                if not far:
                    value = value + z_in[0, :, at].astype(F32)
                z_send[piece % 2, index, :, at] = value.astype(BF16)

            z_block(piece, j, store, far)
            z_copy(piece, j, up).start()
            return 0

        if first and use_far:

            @pl.when(mine & near)
            def _():
                if piece == 0:
                    copies[0][0].wait_recv()
                if piece == 1:
                    copies[0][1].wait_recv()
                copies[1][piece].wait_recv()
                far_load(piece)
                lax.fori_loop(0, count, functools.partial(one, far=True), 0)

            if n_seq > 4:

                @pl.when(mine & jnp.logical_not(near))
                def _():
                    lax.fori_loop(0, count, functools.partial(one, far=False), 0)

        else:

            @pl.when(mine)
            def _():
                lax.fori_loop(0, count, functools.partial(one, far=False), 0)

    def z_final(piece, use_far):
        from_low = s >= (2 if use_far else 1)
        from_high = s < n_seq - (2 if use_far else 1)

        @pl.when(from_low)
        def _():
            z_arrived(piece, s, 0).start()

        @pl.when(from_high)
        def _():
            z_arrived(piece, n_seq, 1).start()

        def hold(at, value):
            z_acc[:, at] = value

        if use_far:

            @pl.when(near)
            def _():
                far_load(piece)
                z_block(piece, s, hold, True)

            @pl.when(jnp.logical_not(near))
            def _():
                z_block(piece, s, hold, False)

        else:
            z_block(piece, s, hold, False)

        @pl.when(from_low)
        def _():
            pltpu.make_async_copy(z_land.at[piece, s], z_in.at[0], zi_sem.at[0]).wait()
            z_acc[...] += z_in[0].astype(F32)

        @pl.when(from_high)
        def _():
            pltpu.make_async_copy(z_land.at[piece, n_seq], z_in.at[1], zi_sem.at[1]).wait()
            z_acc[...] += z_in[1].astype(F32)

        target = gw_out if piece == 0 else gw_xz.at[2 - piece]
        save = pltpu.make_async_copy(z_acc, target, zi_sem.at[0])
        save.start()
        save.wait()

    lane_low = lax.broadcasted_iota(jnp.int32, (T, LANES), 1) < head_size
    later = row_i >= col_i
    earlier = col_i >= row_i

    def spread_heads(l):
        for p in range(pairs):
            at = lanes(p)
            dte[:, at] = jnp.where(
                lane_low, dtv[l, :, 2 * p : 2 * p + 1], dtv[l, :, 2 * p + 1 : 2 * p + 2]
            )
            cume[:, at] = jnp.where(
                lane_low, cum[l, :, 2 * p : 2 * p + 1], cum[l, :, 2 * p + 1 : 2 * p + 2]
            )

    def steps(l):
        def one(p, _):
            at = lanes(p)
            acc = cume[:, at]
            stepped = dte[:, at] * act[l, :, at]
            xtb[:, at] = stepped.astype(BF16)
            xtl[:, at] = (stepped * jnp.exp(acc[T - 1 : T] - acc)).astype(BF16)
            return 0

        lax.fori_loop(0, pairs, one, 0)

    def conv_sum(l, at, v):
        total = prm[l, 5:6, at] + prm[l, 4:5, at] * v[EDGE:]
        moved = []
        for shift in range(1, 4):
            moved.append(pltpu.roll(v, shift, 0)[EDGE:])
            total = total + prm[l, 4 - shift : 5 - shift, at] * moved[-1]
        return total, [v[EDGE:]] + moved

    def forward(l, gap_norm, gap_chain, gap_rs):
        weights_ready(l, [0])
        gain = prm[l, 0:1, :]

        def norm_rows(i, _):
            rows = pl.ds(pl.multiple_of(i * 32, 32), 32)
            v = hb[l, rows, :].astype(F32)
            rstd = lax.rsqrt(jnp.mean(v * v, axis=1, keepdims=True) + EPSILON)
            nm[rows, :] = (v * rstd * gain).astype(BF16)
            return 0

        lax.fori_loop(0, T // 32, norm_rows, 0)

        gap_norm()
        weights_ready(l, [1, 2, 3])

        def project_x(j, _):
            xin[l, EDGE:, lanes(j, ntile)] = dot(
                nm[...], wxz[l, 0, :, lanes(j, ntile)]
            ).astype(BF16)
            return 0

        lax.fori_loop(0, I // ntile, project_x, 0)
        xin[l, EDGE:, I:] = dot(nm[...], wbc[l]).astype(BF16)

        edge = links.remote(
            xin.at[l, pl.ds(T, EDGE)], xin.at[l, pl.ds(0, EDGE)], next_dev, has_next
        )
        start_if(has_next, edge)

        dt_raw = dot_nt(nm[...], wdt[l])
        hp0 = prm[l, 6:7, I : I + LANES]
        hp1 = prm[l, 6:7, I + LANES : I + 2 * LANES]
        pre_dt = dt_raw + hp0
        sgdt[l] = lax.logistic(pre_dt)
        step = jnp.maximum(pre_dt, 0.0) + jnp.log1p(jnp.exp(-jnp.abs(pre_dt)))
        dtv[l] = step
        cum[l] = exact_dot(tri[...], -jnp.exp(hp1) * step)
        cumT[l] = jnp.transpose(cum[l])

        weights_ready(l, [4])

        def project_z(j, _):
            z[l, :, lanes(j, ntile)] = dot(nm[...], wxz[l, 1, :, lanes(j, ntile)])
            return 0

        lax.fori_loop(0, I // ntile, project_z, 0)

        @pl.when(is_first)
        def _():
            xin[l, :EDGE, :] = jnp.zeros((EDGE, XB), BF16)

        wait_if(has_prev, edge)

        def conv(j, _):
            at = lanes(j)
            total, _ = conv_sum(l, at, xin[l, :, at].astype(F32))
            act[l, :, at] = total * lax.logistic(total)
            return 0

        lax.fori_loop(0, XB // LANES, conv, 0)

        mat_b = act[l, :, I : I + N]
        mat_c = act[l, :, I + N :]
        Bb[l] = mat_b.astype(BF16)
        Cb[l] = mat_c.astype(BF16)
        BT[l] = jnp.transpose(mat_b).astype(BF16)
        CT[l] = jnp.transpose(mat_c).astype(BF16)
        spread_heads(l)
        steps(l)

        def local_state(j, _):
            st_loc[l, :, lanes(j, ntile)] = dot(BT[l], xtl[:, lanes(j, ntile)])
            return 0

        lax.fori_loop(0, I // ntile, local_state, 0)
        begin, finish_chain = chain(
            l, True, st_loc.at[l], jnp.exp(cume[T - 1 : T, :]), s_ent.at[l]
        )
        begin()

        cb = dot_nt(Cb[l], Bb[l])

        def intra(p, _):
            at = lanes(p)
            wide = cume[:, at]
            values = xtb[:, at]
            total = jnp.zeros((T, LANES), F32)
            for half in range(2):
                column = wide[:, half * head_size : half * head_size + 1]
                row = cumT[l, pl.ds(2 * p + half, 1), :]
                decay = jnp.where(later, jnp.exp(jnp.minimum(column - row, 0.0)), 0.0)
                mix = (cb * decay).astype(BF16)
                kept = jnp.where(lane_low == (half == 0), values, jnp.zeros_like(values))
                total = total + dot(mix, kept)
            y0[l, :, at] = total
            return 0

        lax.fori_loop(0, pairs, intra, 0)
        gap_chain()
        finish_chain()

        def gate(p, ssq):
            at = lanes(p)
            carried = dot(Cb[l], s_ent[l, :, at].astype(BF16))
            y = y0[l, :, at] + jnp.exp(cume[:, at]) * carried
            y0[l, :, at] = y
            full = y + prm[l, 7:8, at] * act[l, :, at]
            gate_in = z[l, :, at]
            value = full * (gate_in * lax.logistic(gate_in))
            du[:, at] = value
            dye[:, at] = (value * prm[l, 6:7, at]).astype(BF16)
            return ssq + value * value

        ssq = lax.fori_loop(0, pairs, gate, jnp.zeros((T, LANES), F32))
        finish_rows = exchange_rows(ssq, l)
        weights_ready(l, [5])

        def project_out(j, _):
            rs_send[l, :, lanes(j, ntile)] = dot(dye[...], wo[l, :, lanes(j, ntile)]).astype(BF16)
            return 0

        lax.fori_loop(0, D // ntile, project_out, 0)
        finish_rs = reduce_rows(l)
        qb[l] = lax.rsqrt(finish_rows() / inner_total + EPSILON)

        def scaled(p, _):
            at = lanes(p)
            us[l, :, at] = (du[:, at] * qb[l] * prm[l, 6:7, at]).astype(BF16)
            return 0

        lax.fori_loop(0, pairs, scaled, 0)
        ready_u = collect(l, us.at[l], rhs.at[0, c])
        gap_rs()
        finish_rs()
        summed = rs_total(l, own_rows)
        q_own = qb[l, own_rows, :][:, :1]
        return (hb[l, own_rows, :].astype(F32) + q_own * summed).astype(BF16), ready_u

    def backward(l, gap_dot, gap_chain, gap_join, gap_rs):
        hp1 = prm[l, 6:7, I + LANES : I + 2 * LANES]

        def start_du(j, acc):
            at = lanes(j, ntile)
            got = dot_nt(eb[l], wo[l, at, :])
            du[:, at] = got
            gate_in = z[l, :, at]
            value = (y0[l, :, at] + prm[l, 7:8, at] * act[l, :, at]) * (
                gate_in * lax.logistic(gate_in)
            )
            value = got * value
            small[l, 6:7, at] = jnp.sum(value * qb[l][:, :1], axis=0, keepdims=True)
            weighted = value * prm[l, 6:7, at]
            return acc + weighted[:, :LANES] + weighted[:, LANES:]

        acc = lax.fori_loop(0, I // ntile, start_du, jnp.zeros((T, LANES), F32))
        finish_rows = exchange_rows(acc, 2 + l)
        spread_heads(l)
        steps(l)
        gap_dot()
        dot_all = finish_rows()

        def through_gate(p, _):
            at = lanes(p)
            q = qb[l]
            gate_in = z[l, :, at]
            sig = lax.logistic(gate_in)
            silu = gate_in * sig
            x_now = act[l, :, at]
            full = y0[l, :, at] + prm[l, 7:8, at] * x_now
            dg = q * (du[:, at] * prm[l, 6:7, at]) - full * silu * (q * q * q) * (
                dot_all / inner_total
            )
            d_y = dg * silu
            gp[l, :, lanes(p + pairs)] = (
                dg * full * sig * (1.0 + gate_in * (1.0 - sig))
            ).astype(BF16)
            small[l, 7:8, at] = jnp.sum(d_y * x_now, axis=0, keepdims=True)
            dy[:, at] = d_y
            dyb[:, at] = d_y.astype(BF16)
            dye[:, at] = (d_y * jnp.exp(cume[:, at])).astype(BF16)
            return 0

        lax.fori_loop(0, pairs, through_gate, 0)

        def local_state(j, _):
            dst_loc[:, lanes(j, ntile)] = dot(CT[l], dye[:, lanes(j, ntile)])
            return 0

        lax.fori_loop(0, I // ntile, local_state, 0)
        begin, finish_chain = chain(
            2 + l, False, dst_loc, jnp.exp(cume[T - 1 : T, :]), gin
        )
        begin()
        ready_z = collect(l, gp.at[l, :, pl.ds(I, I)], rhs.at[1, c])

        cbt = dot_nt(Bb[l], Cb[l])
        dcbt[...] = jnp.zeros_like(dcbt)

        def intra(p, _):
            at = lanes(p)
            wide = cume[:, at]
            values = xtb[:, at]
            grads = dyb[:, at]
            total = jnp.zeros((T, LANES), F32)
            for half in range(2):
                column = wide[:, half * head_size : half * head_size + 1]
                row = cumT[l, pl.ds(2 * p + half, 1), :]
                decay = jnp.where(earlier, jnp.exp(jnp.minimum(row - column, 0.0)), 0.0)
                mix = (cbt * decay).astype(BF16)
                kept = jnp.where(lane_low == (half == 0), grads, jnp.zeros_like(grads))
                total = total + dot(mix, kept)
                dcbt[...] += dot_nt(values, kept) * decay
            du[:, at] = total
            return 0

        lax.fori_loop(0, pairs, intra, 0)
        gap_chain(ready_z)
        finish_chain()

        def join(p, carry):
            sum_v, sum_w = carry
            at = lanes(p)
            into = gin[:, at]
            acc = cume[:, at]
            end = acc[T - 1 : T]
            got = du[:, at] + jnp.exp(end - acc) * dot(Bb[l], into.astype(BF16))
            x_now = act[l, :, at]
            d_y = dy[:, at]
            leaving = s_ent[l, :, at] * jnp.exp(end) + st_loc[l, :, at]
            final = jnp.sum(into * leaving, axis=0, keepdims=True)
            v = dyb[:, at].astype(F32) * y0[l, :, at] - xtb[:, at].astype(F32) * got
            is_end = lax.broadcasted_iota(jnp.int32, (T, LANES), 0) == T - 1
            v = v + jnp.where(is_end, final, 0.0)
            dact[:T, at] = dte[:, at] * got + prm[l, 7:8, at] * d_y
            picks = et[at, :]
            return (sum_v + split_dot(v, picks), sum_w + split_dot(x_now * got, picks))

        zero = jnp.zeros((T, LANES), F32)
        sum_v, sum_w = lax.fori_loop(0, pairs, join, (zero, zero))

        dcb_low = dcbt[...].astype(BF16)
        gin_low = gin[...].astype(BF16)
        ent_low = s_ent[l].astype(BF16)
        dact[:T, I : I + N] = dot(dcb_low, Cb[l]) + dot_nt(xtl[...], gin_low)
        dact[:T, I + N :] = dot_tn(dcb_low, Bb[l]) + dot_nt(dye[...], ent_low)

        def conv_pre(j, _):
            at = lanes(j)
            total, moved = conv_sum(l, at, xin[l, :, at].astype(F32))
            sig = lax.logistic(total)
            got = dact[:T, at] * (sig * (1.0 + total * (1.0 - sig)))
            dact[:T, at] = got
            edge_send[l, :, at] = got[:EDGE].astype(BF16)
            small[l, 5:6, at] = jnp.sum(got, axis=0, keepdims=True)
            for shift in range(4):
                small[l, 4 - shift : 5 - shift, at] = jnp.sum(
                    got * moved[shift], axis=0, keepdims=True
                )
            return 0

        lax.fori_loop(0, XB // LANES, conv_pre, 0)
        edge = links.remote(edge_send.at[l], edge_recv.at[l], prev_dev, has_prev)
        start_if(has_prev, edge)

        d_log = lax.dot_general(
            tri[...], sum_v, (((0,), (0,)), ((), ())),
            precision=lax.Precision.HIGHEST, preferred_element_type=F32,
        )
        rate = -jnp.exp(hp1)
        d_raw = (sum_w + d_log * rate) * sgdt[l]
        small[l, 6:7, I : I + LANES] = jnp.sum(d_raw, axis=0, keepdims=True)
        small[l, 6:7, I + LANES : I + 2 * LANES] = jnp.sum(
            d_log * rate * dtv[l], axis=0, keepdims=True
        )
        d_raw = jnp.where(lax.broadcasted_iota(jnp.int32, (T, LANES), 1) < heads, d_raw, 0.0)
        gp[l, :, 2 * I + 2 * N :] = d_raw.astype(BF16)
        dt_rows = bc_rows.shape[1] - Q2
        bc_rows[l, Q2:, :] = jnp.transpose(d_raw)[:dt_rows].astype(BF16)
        gap_join()

        @pl.when(is_last)
        def _():
            dact[T:, :] = jnp.zeros((EDGE, XB), F32)

        @pl.when(has_next)
        def _():
            edge.wait_recv()
            dact[T:, :] = edge_recv[l].astype(F32)

        def conv_in(j, _):
            at = lanes(j)
            v = dact[:, at]
            total = prm[l, 4:5, at] * v[:T]
            for shift in range(1, 4):
                moved = pltpu.roll(v, T + EDGE - shift, 0)
                total = total + prm[l, 4 - shift : 5 - shift, at] * moved[:T]
            dact[:T, at] = total
            return 0

        lax.fori_loop(0, XB // LANES, conv_in, 0)
        gp[l, :, :I] = dact[:T, :I].astype(BF16)
        gp[l, :, 2 * I : 2 * I + 2 * N] = dact[:T, I:].astype(BF16)

        def normed_all(j, _):
            at = lanes(j, ntile)
            total = dot_nt(gp[l, :, I : 2 * I], wxz[l, 1, at, :])
            total = total + dot_nt(gp[l, :, :I], wxz[l, 0, at, :])
            total = total + dot_nt(gp[l, :, 2 * I : 2 * I + 2 * N], wbc[l, at, :])
            total = total + dot(gp[l, :, 2 * I + 2 * N :], wdt[l, :, at])
            rs_send[1 - l, :, at] = total.astype(BF16)
            return 0

        for copy in rs_copies[1 - l]:
            copy.wait_send()
        lax.fori_loop(0, D // ntile, normed_all, 0)
        finish_rs = reduce_rows(1 - l)
        ready_x = collect(l, gp.at[l, :, pl.ds(0, I)], rhs.at[2, c])
        gap_rs(ready_x)
        finish_rs()
        got = rs_total(1 - l, own_rows)
        v = hb[l, own_rows, :].astype(F32)
        rstd = lax.rsqrt(jnp.mean(v * v, axis=1, keepdims=True) + EPSILON)
        small[l, 0:1, :] = jnp.sum(got * v * rstd, axis=0, keepdims=True)
        hat = got * prm[l, 0:1, :]
        inner = jnp.sum(hat * v, axis=1, keepdims=True)
        return (
            rstd * hat - v * (rstd * rstd * rstd) * inner / D
            + eb[l, own_rows, :].astype(F32)
        )

    def bc_start(l):
        copies = []
        bc_t[l] = jnp.transpose(dact[:T, I:]).astype(BF16)
        for d, peer in enumerate(head_peers):
            rows = pl.ds(pl.multiple_of(lax.rem(k + d + 1, n_head) * Q2, Q2), Q2)
            copy = links.remote(bc_t.at[l, rows], bc_recv.at[l, d], peer)
            copy.start()
            copies.append(copy)
        return copies

    def bc_mid(l, copies):
        total = bc_t[l, pl.ds(pl.multiple_of(k * Q2, Q2), Q2), :].astype(F32)
        for d, copy in enumerate(copies):
            copy.wait_recv()
            total = total + bc_recv[l, d].astype(F32)
        bc_rows[l, :Q2, :] = total.astype(BF16)
        return collect(l, bc_rows.at[l], bc_rhs.at[c])

    def bc_block(j):
        rows = pl.ds(pl.multiple_of(j * DB, DB), DB)
        return dot_nt(bc_rhs[0], lt[1, 0, rows, :]) + dot_nt(bc_rhs[1], lt[1, 1, rows, :])

    def bc_copies(l):
        return [
            links.remote(bc_send.at[d], bc_land.at[d], peer, c == l)
            for d, peer in enumerate(seq_peers)
        ]

    def bc_out_start(ready, copies):
        ready()
        for d, copy in enumerate(copies):
            bc_send[d] = bc_block(lax.rem(s + d + 1, n_seq)).astype(BF16)
            copy.start()

    def bc_gather_copies(l):
        return [
            links.remote(bc_all.at[k], bc_all.at[k], peer, c == l) for peer in head_peers
        ]

    def bc_sum(copies, gathers):
        total = bc_block(s)
        for d, copy in enumerate(copies):
            copy.wait_recv()
            total = total + bc_land[d].astype(F32)
        bc_all[k] = total[:Q2]
        for h in range(heads):
            gw_dt[h] = total[Q2 + h : Q2 + h + 1]
        for copy in gathers:
            copy.start()

    def bc_finish(gathers):
        for copy in gathers:
            copy.wait_recv()
        whole = jnp.concatenate([bc_all[i] for i in range(n_head)], axis=0)
        gw_bc[...] = jnp.transpose(whole) if DB % LANES == 0 else whole

    def small_start(l):
        copy = links.remote(small.at[l], sm_o, other, c != l)
        start_if(c != l, copy)
        heads_to = [
            links.remote(sm_t, sm_h.at[d], peer, c == l) for d, peer in enumerate(head_peers)
        ]
        seqs_to = [
            links.remote(sm_u, sm_z.at[d], peer, c == l) for d, peer in enumerate(seq_peers)
        ]
        return copy, heads_to, seqs_to

    def small_heads(l, copies):
        copies[0].wait_recv()
        sm_t[...] = small[l] + sm_o[...]
        for copy in copies[1]:
            copy.start()

    def small_seqs(copies):
        sm_u[...] = sm_t[...]
        for d, copy in enumerate(copies[1]):
            copy.wait_recv()
            sm_u[0:1, :] += sm_h[d, 0:1, :]
            sm_u[1:6, I : I + 2 * N] += sm_h[d, 1:6, I : I + 2 * N]
        for copy in copies[2]:
            copy.start()

    def small_finish(copies):
        total = sm_u[...]
        for d, copy in enumerate(copies[2]):
            copy.wait_recv()
            total = total + sm_z[d]
        g_gain[...] = total[0:1]
        for r in range(5):
            g_conv_x[r] = total[1 + r : 2 + r, :I]
            g_conv_bc[r] = total[1 + r : 2 + r, I : I + 2 * N]
        g_out[...] = total[6:7, :I]
        g_head[0] = total[6:7, I : I + heads]
        g_head[1] = total[6:7, I + LANES : I + LANES + heads]
        g_head[2] = split_dot(total[:, :I], et[...])[7:8, :heads]

    def deliver(kind, rows):
        copy = links.remote(end_send.at[kind], ends.at[c], other, c != kind)

        @pl.when(c == kind)
        def _():
            ends[c] = rows

        @pl.when(c != kind)
        def _():
            end_send[kind] = rows
            copy.start()

        def finish():
            wait_if(c == kind, copy)

        return finish

    on0, on1 = pl.when(c == 0), pl.when(c == 1)
    end1 = pl.when(is_end & (c == 1))
    first1, last1 = pl.when(is_first & (c == 1)), pl.when(is_last & (c == 1))
    far = far_copies(1)
    got = {}

    def up1(l, piece):
        z_forward(far, piece, True, True, l == 1)

    def up2(l, piece):
        z_forward(far, piece, True, False, l == 1)

    def down1(l, piece):
        z_forward(far, piece, False, True, l == 1)

    def down2(l, piece):
        z_forward(far, piece, False, False, l == 1)

    def nothing():
        pass

    def gap():
        got["n0"] = collect_transposed(0, 1, nm)
        load_e.wait()
        got["e1"] = collect_transposed(1, 0, eb.at[1])

    rows, ready_u0 = forward(0, nothing, gap, nothing)
    finish_gather = gather_rows(hb.at[1], rows)

    @on1
    def _():
        got["e1"]()

    @end1
    def _():
        far[0][0].start()

    finish_gather()

    def gap_norm():
        got["n1"] = collect_transposed(1, 1, nm)

    def gap():
        @on1
        def _():
            got["n1"]()

        @end1
        def _():
            far[0][1].start()

    rows, ready_u1 = forward(1, gap_norm, gap, nothing)
    finish_out = deliver(1, rows.astype(F32))

    def gap_dot():
        @on1
        def _():
            ready_u1()

        @first1
        def _():
            far[1][0].start()

    def gap_chain(ready):
        @on1
        def _():
            ready()

        @first1
        def _():
            far[1][1].start()

    def gap_join():
        @last1
        def _():
            far[1][0].start()
            far[1][1].start()

        @on1
        def _():
            up1(1, 0)

    def gap_rs(ready):
        got["bc1"] = bc_start(1)

        @on1
        def _():
            ready()

        @end1
        def _():
            far[1][2].start()

        @on1
        def _():
            up1(1, 1)

    rows = backward(1, gap_dot, gap_chain, gap_join, gap_rs)
    finish_gather = gather_rows(eb.at[0], rows.astype(BF16))
    small1 = small_start(1)
    ready_bc1 = bc_mid(1, got["bc1"])
    bc_to1, bc_g1 = bc_copies(1), bc_gather_copies(1)

    @on1
    def _():
        up2(1, 0)
        down1(1, 0)

    finish_gather()

    def gap_dot():
        got["e0"] = collect_transposed(0, 0, eb.at[0])

        @on1
        def _():
            up1(1, 2)
            small_heads(1, small1)

        @on0
        def _():
            ready_u0()
            got["e0"]()
            z_first(0)

    def gap_chain(ready):
        @on1
        def _():
            up2(1, 1)
            small_seqs(small1)

        @on0
        def _():
            got["n0"]()
            ready()
            z_first(1)

    def gap_join():
        @on0
        def _():
            z_last(0)
            z_last(1)

        @on1
        def _():
            down1(1, 1)
            down2(1, 0)

    def gap_rs(ready):
        got["bc0"] = bc_start(0)

        @on0
        def _():
            ready()
            z_first(2)
            z_last(2)
            up1(0, 0)

        @on1
        def _():
            down1(1, 2)
            up2(1, 2)
            bc_out_start(ready_bc1, bc_to1)
            z_final(0, True)

    rows = backward(0, gap_dot, gap_chain, gap_join, gap_rs)
    finish_in = deliver(0, rows)
    small0 = small_start(0)
    ready_bc0 = bc_mid(0, got["bc0"])
    bc_to0, bc_g0 = bc_copies(0), bc_gather_copies(0)

    @on1
    def _():
        down2(1, 1)
        small_finish(small1)
        bc_sum(bc_to1, bc_g1)
        z_final(1, True)
        down2(1, 2)
        bc_finish(bc_g1)
        z_final(2, True)

    @on0
    def _():
        up1(0, 1)
        down1(0, 0)
        bc_out_start(ready_bc0, bc_to0)
        small_heads(0, small0)
        up1(0, 2)
        down1(0, 1)
        up2(0, 0)
        down2(0, 0)
        small_seqs(small0)
        z_final(0, False)
        up2(0, 1)
        down1(0, 2)
        down2(0, 1)
        bc_sum(bc_to0, bc_g0)
        z_final(1, False)
        small_finish(small0)
        bc_finish(bc_g0)
        up2(0, 2)
        down2(0, 2)
        z_final(2, False)

    finish_out()
    finish_in()
    save = links.local(ends, ends_out)
    save.start()
    save.wait()

    @pl.when(inside | (c == 0))
    def _():
        for i in range(n_seq - 1):
            z_sent(1, i)
            z_sent(2, i)

    for l, copy in lt_sends:

        @pl.when(c != l)
        def _():
            copy.wait_send()

    for slot in range(2):
        for copy in rs_copies[slot]:
            copy.wait_send()
    links.drain()


def run_layers(tokens, cotangent, w_xz, w_bc, w_dt, w_out, in_gain, in_conv_x, in_conv_bc, in_head, in_out):
    n_seq, n_head = lax.axis_size("seq"), lax.axis_size("head")
    _, T, D = tokens.shape
    I = w_xz.shape[2]
    N = w_bc.shape[1] // 2
    heads = in_head.shape[2]
    XB = I + 2 * N
    G = 2 * I + 2 * N + LANES
    Q = T // n_head
    DB = D // n_seq
    BR = 2 * N // n_head + (heads + 15) // 16 * 16
    sems = 104 + 4 * (n_seq + n_head)
    S = jax.ShapeDtypeStruct
    V = pltpu.VMEM
    dma = pltpu.SemaphoreType.DMA
    vm = pl.BlockSpec(memory_space=pltpu.VMEM)
    hbm = pl.BlockSpec(memory_space=pl.ANY)
    scratch = [
        V((2, 2, D, I), BF16), V((2, D, 2 * N), BF16), V((2, LANES, D), BF16), V((2, I, D), BF16),
        V((2, 8, D), F32), V((2, T, D), BF16), V((2, T, D), BF16), V((T, D), BF16),
        V((2, T + EDGE, XB), BF16), V((2, T, I), F32), V((2, T, XB), F32),
        V((T, I), F32), V((T, I), F32), V((2, T, I), F32),
        V((2, T, LANES), F32), V((2, T, LANES), F32), V((2, T, LANES), F32), V((2, LANES, T), F32),
        V((2, N, T), BF16), V((2, N, T), BF16), V((2, T, N), BF16), V((2, T, N), BF16),
        V((2, N, I), F32), V((2, N, I), F32), V((T, I), BF16), V((T, I), BF16),
        V((2, T, LANES), F32),
        V((T, I), F32), V((T, I), F32), V((T, I), BF16), V((T, I), BF16),
        V((N, I), F32), V((N, I), F32), V((T + EDGE, XB), F32),
        V((T, T), F32), V((2, T, G), BF16), V((2, T, I), BF16), V((2, 8, D), F32),
        V((4, 8, T), F32), V((4, n_head - 1, 8, T), F32),
        V((2, T, D), BF16), V((2, n_head - 1, Q, D), BF16),
        V((4, 3, N, I // 3), BF16), V((4, 3, N, I // 3), BF16),
        V((2, EDGE, XB), BF16), V((2, EDGE, XB), BF16),
        V((2, Q, D), F32), V((2, Q, D), F32), V((I, LANES), BF16), V((T, T), F32),
        V((2, 2, D, T), BF16), V((D, T), BF16), V((3, 2, T, I), BF16),
        V((2, n_seq - 1, DB, I), BF16), V((2, DB, I), BF16), V((DB, I), F32),
        V((2, DB, T), BF16), V((2, T, I), BF16),
        V((2, n_head - 1, 2 * N // n_head, T), BF16), V((2, 2 * N, T), BF16), V((2, BR, T), BF16),
        V((2, BR, T), BF16), V((n_seq - 1, BR, DB), BF16), V((n_seq - 1, BR, DB), BF16),
        V((n_head, 2 * N // n_head, DB), F32),
        V((8, D), F32), V((8, D), F32), V((n_head - 1, 8, D), F32), V((8, D), F32),
        V((n_seq - 1, 8, D), F32),
        dma((24,)), dma((sems,)), dma((sems,)),
        dma((3 * (n_seq - 1),)), dma((3 * (n_seq + 1),)), dma((4,)),
    ]
    dims = (n_seq, n_head, T, D, I, N, heads)
    return pl.pallas_call(
        functools.partial(layer_kernel, dims),
        out_shape=(
            S((2, Q, D), F32), S((DB, I), F32), S((2, DB, I), F32),
            S((DB, 2 * N) if DB % LANES == 0 else (2 * N, DB), F32), S((heads, 1, DB), F32),
            S((1, D), F32), S((5, 1, I), F32), S((5, 1, 2 * N), F32), S((3, 1, heads), F32),
            S((1, I), F32),
            S((3, n_seq + 1, DB, I), BF16), S((2, 2, D, T), BF16), S((3, 2, T, I), BF16),
        ),
        in_specs=[hbm] * 6 + [vm] * 5,
        out_specs=(hbm, hbm, hbm, vm, vm, vm, vm, vm, vm, vm, hbm, hbm, hbm),
        scratch_shapes=scratch,
        compiler_params=pltpu.CompilerParams(
            collective_id=0, has_side_effects=True, vmem_limit_bytes=63 * 2**20
        ),
        name="layers",
    )(
        tokens, cotangent, w_xz, w_bc, w_dt, w_out, in_gain, in_conv_x, in_conv_bc, in_head, in_out
    )[:10]


def body(
    tokens, cotangent, norm_gain, w_xz, w_bc, w_dt, conv_x, conv_bc, head_params, out_gain, w_out
):
    heads = w_dt.shape[2]
    dt_rows = jnp.pad(w_dt[0].T, ((0, LANES - heads), (0, 0)))
    ends, gw_out, gw_xz, gw_bc, gw_dt, g_gain, g_conv_x, g_conv_bc, g_head, g_out = run_layers(
        tokens,
        cotangent,
        jnp.swapaxes(w_xz[0], 0, 1),
        w_bc[0],
        dt_rows,
        w_out[0],
        norm_gain,
        jnp.swapaxes(conv_x, 0, 1),
        jnp.swapaxes(conv_bc, 0, 1),
        jnp.swapaxes(head_params, 0, 1),
        out_gain,
    )
    if gw_bc.shape[1] != w_bc.shape[2]:
        gw_bc = gw_bc.T
    return (
        ends[None],
        g_gain,
        jnp.swapaxes(gw_xz, 0, 1)[None],
        gw_bc[None],
        jnp.transpose(gw_dt, (1, 2, 0)),
        jnp.swapaxes(g_conv_x, 0, 1),
        jnp.swapaxes(g_conv_bc, 0, 1),
        jnp.swapaxes(g_head, 0, 1),
        g_out,
        gw_out.T[None],
    )


def solution(mesh):
    placed = (
        P(None, "seq", None),
        P(None, "seq", None),
        P("section", None),
        P("section", None, None, "head"),
        P("section", None, None),
        P("section", None, "head"),
        P("section", None, "head"),
        P("section", None, None),
        P("section", None, "head"),
        P("section", "head"),
        P("section", "head", None),
    )
    return jax.shard_map(
        body,
        mesh=mesh,
        in_specs=placed,
        out_specs=(
            P("section", None, ("seq", "head"), None),
            P("section", None),
            P("section", "seq", None, "head"),
            P("section", "seq", None),
            P("section", "seq", "head"),
            P("section", None, "head"),
            P("section", None, None),
            P("section", None, "head"),
            P("section", "head"),
            P("section", "head", "seq"),
        ),
        check_vma=False,
    )
```

```python
import functools

import jax
import jax.numpy as jnp
from jax import lax
from jax.experimental import pallas as pl
from jax.experimental.pallas import tpu as pltpu
from jax.sharding import PartitionSpec as P

EPSILON = 1e-05
MESH = pl.DeviceIdType.MESH
LANES = 128
EDGE = 16
F32 = jnp.float32
BF16 = jnp.bfloat16


def dot(a, b):
    return lax.dot_general(a, b, (((1,), (0,)), ((), ())), preferred_element_type=F32)


def dot_nt(a, b):
    return lax.dot_general(a, b, (((1,), (1,)), ((), ())), preferred_element_type=F32)


def dot_tn(a, b):
    return lax.dot_general(a, b, (((0,), (0,)), ((), ())), preferred_element_type=F32)


def exact_dot(a, b):
    return lax.dot_general(
        a, b, (((1,), (0,)), ((), ())), precision=lax.Precision.HIGHEST, preferred_element_type=F32
    )


def split_dot(a, b):
    high = a.astype(BF16)
    return dot(high, b) + dot((a - high.astype(F32)).astype(BF16), b)


class Links:
    def __init__(self, local_sem, send_sem, recv_sem):
        self.local_sem, self.send_sem, self.recv_sem = local_sem, send_sem, recv_sem
        self.local_count = 0
        self.count = 0
        self.pending = []

    def local(self, src, dst):
        index = self.local_count
        assert index < self.local_sem.shape[0]
        self.local_count += 1
        return pltpu.make_async_copy(src, dst, self.local_sem.at[index])

    def remote(self, src, dst, peer, when=None):
        index = self.count
        assert index < self.send_sem.shape[0]
        self.count += 1
        copy = pltpu.make_async_remote_copy(
            src_ref=src,
            dst_ref=dst,
            send_sem=self.send_sem.at[index],
            recv_sem=self.recv_sem.at[index],
            device_id=peer,
            device_id_type=MESH,
        )
        self.pending.append((copy, when))
        return copy

    def drain(self):
        for copy, when in self.pending:
            if when is None:
                copy.wait_send()
            else:

                @pl.when(when)
                def _():
                    copy.wait_send()


def wait_if(condition, copy):
    @pl.when(condition)
    def _():
        copy.wait_recv()


def start_if(condition, copy):
    @pl.when(condition)
    def _():
        copy.start()


def lanes(i, width=LANES):
    if isinstance(i, int):
        return pl.ds(i * width, width)
    return pl.ds(pl.multiple_of(i * width, width), width)


def layer_kernel(dims, *refs):
    (n_seq, n_head, T, D, I, N, heads) = dims
    (
        tokens, cotangent, w_xz, w_bc, w_dt, w_out, in_gain, in_conv_x, in_conv_bc, in_head, in_out,
        ends_out, gw_out, gw_xz, gw_bc, gw_dt, g_gain, g_conv_x, g_conv_bc, g_head, g_out, z_land, far_lt, far_rhs,
        wxz, wbc, wdt, wo, prm, hb, eb, nm, xin, z, act, dte, cume, y0,
        sgdt, dtv, cum, cumT, CT, BT, Bb, Cb, st_loc, s_ent, xtb, xtl, qb,
        du, dy, dyb, dye, dst_loc, gin, dact, dcbt, gp, us, small,
        row_send, row_recv, rs_send, rs_recv, ch_send, ch_recv, edge_send, edge_recv,
        end_send, ends, et, tri,
        lt, lt_send, rhs, z_send, z_in, z_acc, z_turn, far_l, far_r, bc_recv, bc_t, bc_rows, bc_rhs, bc_send, bc_land, bc_all,
        sm_o, sm_t, sm_h, sm_u, sm_z,
        local_sem, send_sem, recv_sem, zs_sem, zr_sem, zi_sem,
    ) = refs
    c = lax.axis_index("section")
    s = lax.axis_index("seq")
    k = lax.axis_index("head")
    links = Links(local_sem, send_sem, recv_sem)
    Q = T // n_head
    XB = I + 2 * N
    DB = D // n_seq
    pairs = I // LANES
    head_size = I // heads
    is_first = s == 0
    is_last = s == n_seq - 1
    has_prev = s > 0
    has_next = s < n_seq - 1
    other = {"section": 1 - c}
    prev_dev = {"seq": jnp.maximum(s - 1, 0)}
    next_dev = {"seq": jnp.minimum(s + 1, n_seq - 1)}
    head_peers = [{"head": lax.rem(k + d, n_head)} for d in range(1, n_head)]
    seq_peers = [{"seq": lax.rem(s + d, n_seq)} for d in range(1, n_seq)]
    own_rows = pl.ds(pl.multiple_of(k * Q, Q), Q)
    chunks = 3
    CW = I // chunks
    ntile = 256
    inner_total = I * n_head
    Q2 = 2 * N // n_head
    rs_copies = {}
    parts_rs = 3
    RW = D // parts_rs

    barrier = pltpu.get_barrier_semaphore()
    for peer in [other] + head_peers + seq_peers:
        pl.semaphore_signal(barrier, inc=1, device_id=peer, device_id_type=MESH)

    load_h = links.local(tokens.at[c], hb.at[0])
    load_e = links.local(cotangent.at[c], eb.at[1])
    load_h.start()
    parts = (
        (w_xz.at[0], wxz.at[c, 0]),
        (w_bc, wbc.at[c]),
        (w_dt, wdt.at[c]),
        (w_xz.at[1], wxz.at[c, 1]),
        (w_out, wo.at[c]),
    )
    mine = [links.local(src, dst) for src, dst in parts]
    for copy in mine:
        copy.start()
    load_e.start()
    pl.semaphore_wait(barrier, n_head + n_seq - 1)
    low_row = lax.broadcasted_iota(jnp.int32, (1, LANES), 1) < head_size
    prm[c] = jnp.zeros((8, D), F32)
    prm[c, 0:1, :] = in_gain[...]
    for r in range(5):
        prm[c, 1 + r : 2 + r, :I] = in_conv_x[r]
        prm[c, 1 + r : 2 + r, I : I + 2 * N] = in_conv_bc[r]
    prm[c, 6:7, :I] = in_out[...]
    prm[c, 6:7, I : I + heads] = in_head[0]
    prm[c, 6:7, I + LANES : I + LANES + heads] = in_head[1]
    skips = in_head[2]
    for p in range(pairs):
        prm[c, 7:8, lanes(p)] = jnp.where(
            low_row, skips[:, 2 * p : 2 * p + 1], skips[:, 2 * p + 1 : 2 * p + 2]
        )
    theirs = [links.remote(prm.at[c], prm.at[c], other)]
    theirs += [links.remote(src, dst, other) for src, dst in parts]
    for copy in theirs:
        copy.start()

    def weights_ready(layer, which):
        @pl.when(c == layer)
        def _():
            for i in which:
                if i:
                    mine[i - 1].wait()

        @pl.when(c != layer)
        def _():
            for i in which:
                theirs[i].wait_recv()

    row_i = lax.broadcasted_iota(jnp.int32, (T, T), 0)
    col_i = lax.broadcasted_iota(jnp.int32, (T, T), 1)
    tri[...] = jnp.where(row_i >= col_i, 1.0, 0.0)
    er = lax.broadcasted_iota(jnp.int32, (I, LANES), 0)
    ec = lax.broadcasted_iota(jnp.int32, (I, LANES), 1)
    et[...] = jnp.where(
        (er >= ec * head_size) & (er < (ec + 1) * head_size), 1.0, 0.0
    ).astype(BF16)
    small[...] = jnp.zeros_like(small)
    load_h.wait()

    def exchange_rows(total_cols, slot):
        summed = jnp.sum(total_cols, axis=1, keepdims=True)
        as_row = jnp.transpose(jnp.broadcast_to(summed, (T, LANES)))[:8]
        row_send[slot] = as_row
        copies = []
        for d, peer in enumerate(head_peers):
            copy = links.remote(row_send.at[slot], row_recv.at[slot, d], peer)
            copy.start()
            copies.append(copy)

        def finish():
            total = row_send[slot]
            for d, copy in enumerate(copies):
                copy.wait_recv()
                total = total + row_recv[slot, d]
            wide = jnp.broadcast_to(total[:1], (LANES, T))
            return jnp.transpose(wide)

        return finish

    def reduce_rows(slot):
        copies = []
        for q in range(parts_rs):
            at = pl.ds(q * RW, RW)
            row = []
            for d, peer in enumerate(head_peers):
                rows = pl.ds(pl.multiple_of(lax.rem(k + d + 1, n_head) * Q, Q), Q)
                row.append(
                    links.remote(rs_send.at[slot, rows, at], rs_recv.at[slot, d, :, at], peer)
                )
                links.pending.pop()
            copies.append(row)
        rs_copies[slot] = [copy for row in copies for copy in row]

        def send(q):
            for copy in copies[q]:
                copy.start()

        def part(q):
            at = pl.ds(q * RW, RW)
            total = rs_send[slot, own_rows, at].astype(F32)
            for d, copy in enumerate(copies[q]):
                copy.wait_recv()
                total = total + rs_recv[slot, d, :, at].astype(F32)
            return total

        return send, part

    def gather_rows(target):
        copies = []
        for q in range(parts_rs):
            at = target.at[own_rows, pl.ds(q * RW, RW)]
            copies.append([links.remote(at, at, peer) for peer in head_peers])

        def send(q, rows):
            target[own_rows, pl.ds(q * RW, RW)] = rows
            for copy in copies[q]:
                copy.start()

        def finish():
            for row in copies:
                for copy in row:
                    copy.wait_recv()

        return send, finish

    def chain(slot, forward, local, dec_row, into):
        starts, goes_on = (is_first, has_next) if forward else (is_last, has_prev)
        receives = has_prev if forward else has_next
        peer = next_dev if forward else prev_dev
        copies = []
        for j in range(chunks):
            copies.append(
                links.remote(ch_send.at[slot, j], ch_recv.at[slot, j], peer, goes_on)
            )

        def begin():
            @pl.when(starts)
            def _():
                for j in range(chunks):
                    ch_send[slot, j] = local[:, lanes(j, CW)].astype(BF16)
                    start_if(goes_on, copies[j])

        def finish():
            @pl.when(starts)
            def _():
                into[...] = jnp.zeros_like(into)

            @pl.when(receives)
            def _():
                for j in range(chunks):
                    copies[j].wait_recv()
                    at = lanes(j, CW)
                    arrived = ch_recv[slot, j].astype(F32)
                    into[:, at] = arrived

                    @pl.when(goes_on)
                    def _():
                        ch_send[slot, j] = (
                            arrived * dec_row[:, j * CW : (j + 1) * CW] + local[:, at]
                        ).astype(BF16)
                        copies[j].start()

        return begin, finish

    def collect(l, src, dst):
        near = links.local(src, dst)
        far = links.remote(src, dst, other, c != l)

        @pl.when(c == l)
        def _():
            near.start()

        @pl.when(c != l)
        def _():
            far.start()

        def ready():
            near.wait()
            far.wait_recv()

        return ready

    lt_sends = []

    def collect_transposed(l, kind, src):
        far = links.remote(lt_send, lt.at[kind, c], other, c != l)
        links.pending.pop()
        before = [copy for layer, copy in lt_sends if layer == l]
        lt_sends[:] = [item for item in lt_sends if item[0] != l] + [(l, far)]

        def run():
            @pl.when(c == l)
            def _():
                def turn(t, _):
                    lt[kind, c, lanes(t), :] = jnp.transpose(src[:, lanes(t)].astype(F32)).astype(BF16)
                    return 0

                lax.fori_loop(0, D // LANES, turn, 0)

            @pl.when(c != l)
            def _():
                for copy in before:
                    copy.wait_send()

                def turn(t, _):
                    lt_send[lanes(t), :] = jnp.transpose(src[:, lanes(t)].astype(F32)).astype(BF16)
                    return 0

                lax.fori_loop(0, D // LANES, turn, 0)
                far.start()

        def ready():
            far.wait_recv()

        return run, ready

    low_half = s < n_seq // 2
    is_end = is_first | is_last
    inside = has_prev & has_next
    inward = {"seq": jnp.where(is_first, 1, jnp.where(is_last, n_seq - 2, s))}

    def far_copies(l, kinds, pieces):
        def one(a, there, i):
            ends = is_end if far_up(l, i) else is_last
            return links.remote(a.at[i], there.at[i], inward, ends & (c == l))

        return (
            {i: one(lt, far_lt, i) for i in kinds},
            {i: one(rhs, far_rhs, i) for i in pieces},
        )

    def far_up(l, piece):
        return piece > 0

    def far_down(l, piece):
        return l == 1 or piece > 0

    def z_copy(piece, j, up):
        if up:
            slot, peer = j, next_dev
        else:
            slot, peer = jnp.where(j == s - 1, n_seq, j), prev_dev
        index = jnp.where(j < s, j, j - 1)
        return pltpu.make_async_remote_copy(
            src_ref=z_send.at[piece % 2, index],
            dst_ref=z_land.at[piece, slot],
            send_sem=zs_sem.at[piece * (n_seq - 1) + index],
            recv_sem=zr_sem.at[piece * (n_seq + 1) + slot],
            device_id=peer,
            device_id_type=MESH,
        )

    def z_arrived(piece, slot, into):
        pltpu.make_async_remote_copy(
            src_ref=z_send.at[piece % 2, 0],
            dst_ref=z_land.at[piece, slot],
            send_sem=zs_sem.at[piece * (n_seq - 1)],
            recv_sem=zr_sem.at[piece * (n_seq + 1) + slot],
            device_id=prev_dev,
            device_id_type=MESH,
        ).wait_recv()
        return pltpu.make_async_copy(z_land.at[piece, slot], z_in.at[into], zi_sem.at[into])

    def z_block(piece, j, store, far):
        kind = 0 if piece == 0 else 1
        rows = pl.ds(pl.multiple_of(j * DB, DB), DB)
        if far:
            load = pltpu.make_async_copy(far_lt.at[kind, :, rows], far_l, zi_sem.at[2])
            load.start()
            load.wait()

        def tile(t, _):
            at = lanes(t, ntile)
            value = dot(lt[kind, 0, rows, :], rhs[piece, 0, :, at]) + dot(
                lt[kind, 1, rows, :], rhs[piece, 1, :, at]
            )
            if far:
                value = value + dot(far_l[0], far_r[0, :, at]) + dot(far_l[1], far_r[1, :, at])
            store(at, value)
            return 0

        lax.fori_loop(0, I // ntile, tile, 0)

    def z_one(piece, j, up):
        index = jnp.where(j < s, j, j - 1)
        def store(at, value):
            z_send[piece % 2, index, :, at] = value.astype(BF16)

        z_block(piece, j, store, False)
        z_copy(piece, j, up).start()
        return 0

    def z_first(piece):
        @pl.when(is_first)
        def _():
            lax.fori_loop(0, n_seq - 1, lambda i, _: z_one(piece, n_seq - 1 - i, True), 0)

    def z_last(piece, part):
        low, high = (n_seq - 1) * part // 3, (n_seq - 1) * (part + 1) // 3

        @pl.when(is_last)
        def _():
            lax.fori_loop(low, high, lambda i, _: z_one(piece, i, False), 0)

    def far_load(piece):
        load = pltpu.make_async_copy(far_rhs.at[piece], far_r, zi_sem.at[3])
        load.start()
        load.wait()

    def z_sent(piece, index):
        pltpu.make_async_remote_copy(
            src_ref=z_send.at[piece % 2, index],
            dst_ref=z_land.at[piece, 0],
            send_sem=zs_sem.at[piece * (n_seq - 1) + index],
            recv_sem=zr_sem.at[piece * (n_seq + 1)],
            device_id=next_dev,
            device_id_type=MESH,
        ).wait_send()

    def z_forward(l, piece, up, first, part=None):
        mine = inside & (low_half if up == first else jnp.logical_not(low_half))
        count = n_seq - 1 - s if up else s
        begin, end = 0, count
        if part is not None:
            begin, end = (0, count // 2) if part == 0 else (count // 2, count)

        def one(i, _, far):
            j = n_seq - 1 - i if up else i
            index = jnp.where(j < s, j, j - 1)
            if piece == 2:
                z_sent(0, index)
            if not far:
                load = z_arrived(piece, j, 0)
                load.start()
                load.wait()

            def store(at, value):
                if not far:
                    value = value + z_in[0, :, at].astype(F32)
                z_send[piece % 2, index, :, at] = value.astype(BF16)

            z_block(piece, j, store, far)
            z_copy(piece, j, up).start()
            return 0

        use_far = far_up(l, piece) if up else far_down(l, piece)
        near = s == 1 if up else s == n_seq - 2
        if first and use_far:

            @pl.when(mine & near)
            def _():
                if not part:
                    if piece < 2:
                        far[l][0][piece].wait_recv()
                    far[l][1][piece].wait_recv()
                far_load(piece)
                lax.fori_loop(begin, end, functools.partial(one, far=True), 0)

            if n_seq > 4:

                @pl.when(mine & jnp.logical_not(near))
                def _():
                    lax.fori_loop(begin, end, functools.partial(one, far=False), 0)

        else:

            @pl.when(mine)
            def _():
                lax.fori_loop(begin, end, functools.partial(one, far=False), 0)

    def z_final(l, piece):
        by_low, by_high = far_up(l, piece), far_down(l, piece)
        from_low = s >= (2 if by_low else 1)
        from_high = s < n_seq - (2 if by_high else 1)
        near = ((s == 1) & by_low) | ((s == n_seq - 2) & by_high)

        @pl.when(from_low)
        def _():
            z_arrived(piece, s, 0).start()

        @pl.when(from_high)
        def _():
            z_arrived(piece, n_seq, 1).start()

        def hold(at, value):
            z_acc[:, at] = value

        if by_low or by_high:

            @pl.when(near)
            def _():
                far_load(piece)
                z_block(piece, s, hold, True)

            @pl.when(jnp.logical_not(near))
            def _():
                z_block(piece, s, hold, False)

        else:
            z_block(piece, s, hold, False)

        @pl.when(from_low)
        def _():
            pltpu.make_async_copy(z_land.at[piece, s], z_in.at[0], zi_sem.at[0]).wait()
            z_acc[...] += z_in[0].astype(F32)

        @pl.when(from_high)
        def _():
            pltpu.make_async_copy(z_land.at[piece, n_seq], z_in.at[1], zi_sem.at[1]).wait()
            z_acc[...] += z_in[1].astype(F32)

        if piece == 0 and DB % LANES == 0:
            for t in range(I // ntile):
                z_turn[t * ntile : (t + 1) * ntile, :] = jnp.transpose(z_acc[:, t * ntile : (t + 1) * ntile])
            save = pltpu.make_async_copy(z_turn, gw_out, zi_sem.at[0])
        else:
            target = gw_out if piece == 0 else gw_xz.at[2 - piece]
            save = pltpu.make_async_copy(z_acc, target, zi_sem.at[0])
        save.start()
        save.wait()

    lane_low = lax.broadcasted_iota(jnp.int32, (T, LANES), 1) < head_size
    later = row_i >= col_i
    earlier = col_i >= row_i

    def spread_heads(l):
        for p in range(pairs):
            at = lanes(p)
            dte[:, at] = jnp.where(
                lane_low, dtv[l, :, 2 * p : 2 * p + 1], dtv[l, :, 2 * p + 1 : 2 * p + 2]
            )
            cume[:, at] = jnp.where(
                lane_low, cum[l, :, 2 * p : 2 * p + 1], cum[l, :, 2 * p + 1 : 2 * p + 2]
            )

    def steps(l):
        def one(p, _):
            at = lanes(p)
            acc = cume[:, at]
            stepped = dte[:, at] * act[l, :, at]
            xtb[:, at] = stepped.astype(BF16)
            xtl[:, at] = (stepped * jnp.exp(acc[T - 1 : T] - acc)).astype(BF16)
            return 0

        lax.fori_loop(0, pairs, one, 0)

    def conv_sum(l, at, v):
        total = prm[l, 5:6, at] + prm[l, 4:5, at] * v[EDGE:]
        moved = []
        for shift in range(1, 4):
            moved.append(pltpu.roll(v, shift, 0)[EDGE:])
            total = total + prm[l, 4 - shift : 5 - shift, at] * moved[-1]
        return total, [v[EDGE:]] + moved

    def forward(l, gap_norm, gap_chain, gap_rs, put):
        weights_ready(l, [0])
        gain = prm[l, 0:1, :]

        def norm_rows(i, _):
            rows = pl.ds(pl.multiple_of(i * 32, 32), 32)
            v = hb[l, rows, :].astype(F32)
            rstd = lax.rsqrt(jnp.mean(v * v, axis=1, keepdims=True) + EPSILON)
            nm[rows, :] = (v * rstd * gain).astype(BF16)
            return 0

        lax.fori_loop(0, T // 32, norm_rows, 0)

        gap_norm()
        weights_ready(l, [1, 2, 3])

        def project_x(j, _):
            xin[l, EDGE:, lanes(j, ntile)] = dot(
                nm[...], wxz[l, 0, :, lanes(j, ntile)]
            ).astype(BF16)
            return 0

        lax.fori_loop(0, I // ntile, project_x, 0)
        xin[l, EDGE:, I:] = dot(nm[...], wbc[l]).astype(BF16)

        edge = links.remote(
            xin.at[l, pl.ds(T, EDGE)], xin.at[l, pl.ds(0, EDGE)], next_dev, has_next
        )
        start_if(has_next, edge)

        dt_raw = dot_nt(nm[...], wdt[l])
        hp0 = prm[l, 6:7, I : I + LANES]
        hp1 = prm[l, 6:7, I + LANES : I + 2 * LANES]
        pre_dt = dt_raw + hp0
        sgdt[l] = lax.logistic(pre_dt)
        step = jnp.maximum(pre_dt, 0.0) + jnp.log1p(jnp.exp(-jnp.abs(pre_dt)))
        dtv[l] = step
        cum[l] = exact_dot(tri[...], -jnp.exp(hp1) * step)
        cumT[l] = jnp.transpose(cum[l])

        weights_ready(l, [4])

        def project_z(j, _):
            z[l, :, lanes(j, ntile)] = dot(nm[...], wxz[l, 1, :, lanes(j, ntile)])
            return 0

        lax.fori_loop(0, I // ntile, project_z, 0)

        @pl.when(is_first)
        def _():
            xin[l, :EDGE, :] = jnp.zeros((EDGE, XB), BF16)

        wait_if(has_prev, edge)

        def conv(j, _):
            at = lanes(j)
            total, _ = conv_sum(l, at, xin[l, :, at].astype(F32))
            act[l, :, at] = total * lax.logistic(total)
            return 0

        lax.fori_loop(0, XB // LANES, conv, 0)

        mat_b = act[l, :, I : I + N]
        mat_c = act[l, :, I + N :]
        Bb[l] = mat_b.astype(BF16)
        Cb[l] = mat_c.astype(BF16)
        BT[l] = jnp.transpose(mat_b).astype(BF16)
        CT[l] = jnp.transpose(mat_c).astype(BF16)
        spread_heads(l)
        steps(l)

        def local_state(j, _):
            st_loc[l, :, lanes(j, ntile)] = dot(BT[l], xtl[:, lanes(j, ntile)])
            return 0

        lax.fori_loop(0, I // ntile, local_state, 0)
        begin, finish_chain = chain(
            l, True, st_loc.at[l], jnp.exp(cume[T - 1 : T, :]), s_ent.at[l]
        )
        begin()

        cb = dot_nt(Cb[l], Bb[l])

        def intra(p, _):
            at = lanes(p)
            wide = cume[:, at]
            values = xtb[:, at]
            total = jnp.zeros((T, LANES), F32)
            for half in range(2):
                column = wide[:, half * head_size : half * head_size + 1]
                row = cumT[l, pl.ds(2 * p + half, 1), :]
                decay = jnp.where(later, jnp.exp(jnp.minimum(column - row, 0.0)), 0.0)
                mix = (cb * decay).astype(BF16)
                kept = jnp.where(lane_low == (half == 0), values, jnp.zeros_like(values))
                total = total + dot(mix, kept)
            y0[l, :, at] = total
            return 0

        lax.fori_loop(0, pairs, intra, 0)
        gap_chain()
        finish_chain()

        def gate(p, ssq):
            at = lanes(p)
            carried = dot(Cb[l], s_ent[l, :, at].astype(BF16))
            y = y0[l, :, at] + jnp.exp(cume[:, at]) * carried
            y0[l, :, at] = y
            full = y + prm[l, 7:8, at] * act[l, :, at]
            gate_in = z[l, :, at]
            value = full * (gate_in * lax.logistic(gate_in))
            du[:, at] = value
            dye[:, at] = (value * prm[l, 6:7, at]).astype(BF16)
            return ssq + value * value

        ssq = lax.fori_loop(0, pairs, gate, jnp.zeros((T, LANES), F32))
        finish_rows = exchange_rows(ssq, l)
        weights_ready(l, [5])

        rs_start, rs_part = reduce_rows(l)

        def project_out(j, _):
            rs_send[l, :, lanes(j, ntile)] = dot(dye[...], wo[l, :, lanes(j, ntile)]).astype(BF16)
            return 0

        for q in range(parts_rs):
            lax.fori_loop(q * RW // ntile, (q + 1) * RW // ntile, project_out, 0)
            rs_start(q)
        qb[l] = lax.rsqrt(finish_rows() / inner_total + EPSILON)

        def scaled(p, _):
            at = lanes(p)
            us[l, :, at] = (du[:, at] * qb[l] * prm[l, 6:7, at]).astype(BF16)
            return 0

        lax.fori_loop(0, pairs, scaled, 0)
        ready_u = collect(l, us.at[l], rhs.at[0, c])
        gap_rs()
        q_own = qb[l, own_rows, :][:, :1]
        for q in range(parts_rs):
            at = pl.ds(q * RW, RW)
            rows = hb[l, own_rows, at].astype(F32) + q_own * rs_part(q)
            put(q, rows.astype(BF16))
        return ready_u

    def backward(l, gap_dot, gap_chain, gap_after, gap_join, gap_rs):
        hp1 = prm[l, 6:7, I + LANES : I + 2 * LANES]

        def start_du(j, acc):
            at = lanes(j, ntile)
            got = dot_nt(eb[l], wo[l, at, :])
            du[:, at] = got
            gate_in = z[l, :, at]
            value = (y0[l, :, at] + prm[l, 7:8, at] * act[l, :, at]) * (
                gate_in * lax.logistic(gate_in)
            )
            value = got * value
            small[l, 6:7, at] = jnp.sum(value * qb[l][:, :1], axis=0, keepdims=True)
            weighted = value * prm[l, 6:7, at]
            return acc + weighted[:, :LANES] + weighted[:, LANES:]

        acc = lax.fori_loop(0, I // ntile, start_du, jnp.zeros((T, LANES), F32))
        finish_rows = exchange_rows(acc, 2 + l)
        spread_heads(l)
        steps(l)
        gap_dot()
        dot_all = finish_rows()

        def through_gate(p, _):
            at = lanes(p)
            q = qb[l]
            gate_in = z[l, :, at]
            sig = lax.logistic(gate_in)
            silu = gate_in * sig
            x_now = act[l, :, at]
            full = y0[l, :, at] + prm[l, 7:8, at] * x_now
            dg = q * (du[:, at] * prm[l, 6:7, at]) - full * silu * (q * q * q) * (
                dot_all / inner_total
            )
            d_y = dg * silu
            gp[l, :, lanes(p + pairs)] = (
                dg * full * sig * (1.0 + gate_in * (1.0 - sig))
            ).astype(BF16)
            small[l, 7:8, at] = jnp.sum(d_y * x_now, axis=0, keepdims=True)
            dy[:, at] = d_y
            dyb[:, at] = d_y.astype(BF16)
            dye[:, at] = (d_y * jnp.exp(cume[:, at])).astype(BF16)
            return 0

        lax.fori_loop(0, pairs, through_gate, 0)

        def local_state(j, _):
            dst_loc[:, lanes(j, ntile)] = dot(CT[l], dye[:, lanes(j, ntile)])
            return 0

        lax.fori_loop(0, I // ntile, local_state, 0)
        begin, finish_chain = chain(
            2 + l, False, dst_loc, jnp.exp(cume[T - 1 : T, :]), gin
        )
        begin()
        ready_z = collect(l, gp.at[l, :, pl.ds(I, I)], rhs.at[1, c])

        cbt = dot_nt(Bb[l], Cb[l])
        dcbt[...] = jnp.zeros_like(dcbt)

        def intra(p, _):
            at = lanes(p)
            wide = cume[:, at]
            values = xtb[:, at]
            grads = dyb[:, at]
            total = jnp.zeros((T, LANES), F32)
            for half in range(2):
                column = wide[:, half * head_size : half * head_size + 1]
                row = cumT[l, pl.ds(2 * p + half, 1), :]
                decay = jnp.where(earlier, jnp.exp(jnp.minimum(row - column, 0.0)), 0.0)
                mix = (cbt * decay).astype(BF16)
                kept = jnp.where(lane_low == (half == 0), grads, jnp.zeros_like(grads))
                total = total + dot(mix, kept)
                dcbt[...] += dot_nt(values, kept) * decay
            du[:, at] = total
            return 0

        lax.fori_loop(0, pairs, intra, 0)
        gap_chain(ready_z)
        finish_chain()
        gap_after()

        def join(p, carry):
            sum_v, sum_w = carry
            at = lanes(p)
            into = gin[:, at]
            acc = cume[:, at]
            end = acc[T - 1 : T]
            got = du[:, at] + jnp.exp(end - acc) * dot(Bb[l], into.astype(BF16))
            x_now = act[l, :, at]
            d_y = dy[:, at]
            leaving = s_ent[l, :, at] * jnp.exp(end) + st_loc[l, :, at]
            final = jnp.sum(into * leaving, axis=0, keepdims=True)
            v = dyb[:, at].astype(F32) * y0[l, :, at] - xtb[:, at].astype(F32) * got
            is_end = lax.broadcasted_iota(jnp.int32, (T, LANES), 0) == T - 1
            v = v + jnp.where(is_end, final, 0.0)
            dact[:T, at] = dte[:, at] * got + prm[l, 7:8, at] * d_y
            picks = et[at, :]
            return (sum_v + split_dot(v, picks), sum_w + split_dot(x_now * got, picks))

        zero = jnp.zeros((T, LANES), F32)
        sum_v, sum_w = lax.fori_loop(0, pairs, join, (zero, zero))

        dcb_low = dcbt[...].astype(BF16)
        gin_low = gin[...].astype(BF16)
        ent_low = s_ent[l].astype(BF16)
        dact[:T, I : I + N] = dot(dcb_low, Cb[l]) + dot_nt(xtl[...], gin_low)
        dact[:T, I + N :] = dot_tn(dcb_low, Bb[l]) + dot_nt(dye[...], ent_low)

        def conv_pre(j, _):
            at = lanes(j)
            total, moved = conv_sum(l, at, xin[l, :, at].astype(F32))
            sig = lax.logistic(total)
            got = dact[:T, at] * (sig * (1.0 + total * (1.0 - sig)))
            dact[:T, at] = got
            edge_send[l, :, at] = got[:EDGE].astype(BF16)
            small[l, 5:6, at] = jnp.sum(got, axis=0, keepdims=True)
            for shift in range(4):
                small[l, 4 - shift : 5 - shift, at] = jnp.sum(
                    got * moved[shift], axis=0, keepdims=True
                )
            return 0

        lax.fori_loop(0, XB // LANES, conv_pre, 0)
        edge = links.remote(edge_send.at[l], edge_recv.at[l], prev_dev, has_prev)
        start_if(has_prev, edge)

        d_log = lax.dot_general(
            tri[...], sum_v, (((0,), (0,)), ((), ())),
            precision=lax.Precision.HIGHEST, preferred_element_type=F32,
        )
        rate = -jnp.exp(hp1)
        d_raw = (sum_w + d_log * rate) * sgdt[l]
        small[l, 6:7, I : I + LANES] = jnp.sum(d_raw, axis=0, keepdims=True)
        small[l, 6:7, I + LANES : I + 2 * LANES] = jnp.sum(
            d_log * rate * dtv[l], axis=0, keepdims=True
        )
        d_raw = jnp.where(lax.broadcasted_iota(jnp.int32, (T, LANES), 1) < heads, d_raw, 0.0)
        gp[l, :, 2 * I + 2 * N :] = d_raw.astype(BF16)
        dt_rows = bc_rows.shape[1] - Q2
        bc_rows[l, Q2:, :] = jnp.transpose(d_raw)[:dt_rows].astype(BF16)
        gap_join()

        @pl.when(is_last)
        def _():
            dact[T:, :] = jnp.zeros((EDGE, XB), F32)

        @pl.when(has_next)
        def _():
            edge.wait_recv()
            dact[T:, :] = edge_recv[l].astype(F32)

        def conv_in(j, _):
            at = lanes(j)
            v = dact[:, at]
            total = prm[l, 4:5, at] * v[:T]
            for shift in range(1, 4):
                moved = pltpu.roll(v, T + EDGE - shift, 0)
                total = total + prm[l, 4 - shift : 5 - shift, at] * moved[:T]
            dact[:T, at] = total
            return 0

        lax.fori_loop(0, XB // LANES, conv_in, 0)
        gp[l, :, :I] = dact[:T, :I].astype(BF16)
        gp[l, :, 2 * I : 2 * I + 2 * N] = dact[:T, I:].astype(BF16)

        def normed_all(j, _):
            at = lanes(j, ntile)
            total = dot_nt(gp[l, :, I : 2 * I], wxz[l, 1, at, :])
            total = total + dot_nt(gp[l, :, :I], wxz[l, 0, at, :])
            total = total + dot_nt(gp[l, :, 2 * I : 2 * I + 2 * N], wbc[l, at, :])
            total = total + dot(gp[l, :, 2 * I + 2 * N :], wdt[l, :, at])
            rs_send[1 - l, :, at] = total.astype(BF16)
            return 0

        for copy in rs_copies[1 - l]:
            copy.wait_send()
        rs_start, rs_part = reduce_rows(1 - l)
        for q in range(parts_rs):
            lax.fori_loop(q * RW // ntile, (q + 1) * RW // ntile, normed_all, 0)
            rs_start(q)
        ready_x = collect(l, gp.at[l, :, pl.ds(0, I)], rhs.at[2, c])
        gap_rs(ready_x)
        got = jnp.concatenate([rs_part(q) for q in range(parts_rs)], axis=1)
        v = hb[l, own_rows, :].astype(F32)
        rstd = lax.rsqrt(jnp.mean(v * v, axis=1, keepdims=True) + EPSILON)
        small[l, 0:1, :] = jnp.sum(got * v * rstd, axis=0, keepdims=True)
        hat = got * prm[l, 0:1, :]
        inner = jnp.sum(hat * v, axis=1, keepdims=True)
        return (
            rstd * hat - v * (rstd * rstd * rstd) * inner / D
            + eb[l, own_rows, :].astype(F32)
        )

    def bc_start(l):
        copies = []
        bc_t[l] = jnp.transpose(dact[:T, I:]).astype(BF16)
        for d, peer in enumerate(head_peers):
            rows = pl.ds(pl.multiple_of(lax.rem(k + d + 1, n_head) * Q2, Q2), Q2)
            copy = links.remote(bc_t.at[l, rows], bc_recv.at[l, d], peer)
            copy.start()
            copies.append(copy)
        return copies

    def bc_mid(l, copies):
        total = bc_t[l, pl.ds(pl.multiple_of(k * Q2, Q2), Q2), :].astype(F32)
        for d, copy in enumerate(copies):
            copy.wait_recv()
            total = total + bc_recv[l, d].astype(F32)
        bc_rows[l, :Q2, :] = total.astype(BF16)
        return collect(l, bc_rows.at[l], bc_rhs.at[c])

    def bc_block(j):
        rows = pl.ds(pl.multiple_of(j * DB, DB), DB)
        return dot_nt(bc_rhs[0], lt[1, 0, rows, :]) + dot_nt(bc_rhs[1], lt[1, 1, rows, :])

    def bc_copies(l):
        return [
            links.remote(bc_send.at[d], bc_land.at[d], peer, c == l)
            for d, peer in enumerate(seq_peers)
        ]

    def bc_out_start(ready, copies):
        ready()
        for d, copy in enumerate(copies):
            bc_send[d] = bc_block(lax.rem(s + d + 1, n_seq)).astype(BF16)
            copy.start()

    def bc_gather_copies(l):
        return [
            links.remote(bc_all.at[k], bc_all.at[k], peer, c == l) for peer in head_peers
        ]

    def bc_sum(copies, gathers):
        total = bc_block(s)
        for d, copy in enumerate(copies):
            copy.wait_recv()
            total = total + bc_land[d].astype(F32)
        bc_all[k] = total[:Q2]
        for h in range(heads):
            gw_dt[h] = total[Q2 + h : Q2 + h + 1]
        for copy in gathers:
            copy.start()

    def bc_finish(gathers):
        for copy in gathers:
            copy.wait_recv()
        whole = jnp.concatenate([bc_all[i] for i in range(n_head)], axis=0)
        gw_bc[...] = jnp.transpose(whole) if DB % LANES == 0 else whole

    def small_start(l):
        copy = links.remote(small.at[l], sm_o, other, c != l)
        start_if(c != l, copy)
        heads_to = [
            links.remote(sm_t, sm_h.at[d], peer, c == l) for d, peer in enumerate(head_peers)
        ]
        seqs_to = [
            links.remote(sm_u, sm_z.at[d], peer, c == l) for d, peer in enumerate(seq_peers)
        ]
        return copy, heads_to, seqs_to

    def small_heads(l, copies):
        copies[0].wait_recv()
        sm_t[...] = small[l] + sm_o[...]
        for copy in copies[1]:
            copy.start()

    def small_seqs(copies):
        sm_u[...] = sm_t[...]
        for d, copy in enumerate(copies[1]):
            copy.wait_recv()
            sm_u[0:1, :] += sm_h[d, 0:1, :]
            sm_u[1:6, I : I + 2 * N] += sm_h[d, 1:6, I : I + 2 * N]
        for copy in copies[2]:
            copy.start()

    def small_finish(copies):
        total = sm_u[...]
        for d, copy in enumerate(copies[2]):
            copy.wait_recv()
            total = total + sm_z[d]
        g_gain[...] = total[0:1]
        for r in range(5):
            g_conv_x[r] = total[1 + r : 2 + r, :I]
            g_conv_bc[r] = total[1 + r : 2 + r, I : I + 2 * N]
        g_out[...] = total[6:7, :I]
        g_head[0] = total[6:7, I : I + heads]
        g_head[1] = total[6:7, I + LANES : I + LANES + heads]
        g_head[2] = split_dot(total[:, :I], et[...])[7:8, :heads]

    def deliver(kind):
        copy = links.remote(end_send.at[kind], ends.at[c], other, c != kind)

        def put(q, rows):
            @pl.when(c == kind)
            def _():
                ends[c, :, pl.ds(q * RW, RW)] = rows.astype(F32)

            @pl.when(c != kind)
            def _():
                end_send[kind, :, pl.ds(q * RW, RW)] = rows.astype(F32)
                if q == parts_rs - 1:
                    copy.start()

        def finish():
            wait_if(c == kind, copy)

        return put, finish

    on0, on1 = pl.when(c == 0), pl.when(c == 1)
    end0, end1 = pl.when(is_end & (c == 0)), pl.when(is_end & (c == 1))
    first0, last0 = pl.when(is_first & (c == 0)), pl.when(is_last & (c == 0))
    first1, last1 = pl.when(is_first & (c == 1)), pl.when(is_last & (c == 1))
    far = (far_copies(0, (1,), (1, 2)), far_copies(1, (0, 1), (0, 1, 2)))
    got = {}

    def up1(l, piece):
        z_forward(l, piece, True, True)

    def up2(l, piece):
        z_forward(l, piece, True, False)

    def down1(l, piece, part=None):
        z_forward(l, piece, False, True, part)

    def down2(l, piece):
        z_forward(l, piece, False, False)

    def nothing():
        pass

    run_e1, ready_e1 = collect_transposed(1, 0, eb.at[1])
    run_n0, ready_n0 = collect_transposed(0, 1, nm)
    run_n1, ready_n1 = collect_transposed(1, 1, nm)

    def send_e1():
        @on1
        def _():
            ready_e1()
            far[1][0][0].start()

    def send_n0():
        @on0
        def _():
            ready_n0()
            far[0][0][1].start()

    def gap():
        run_n0()

        @pl.when(is_first)
        def _():
            send_n0()

        load_e.wait()
        run_e1()

        @pl.when(is_last)
        def _():
            send_e1()

    def gap_rs():
        @pl.when(is_last)
        def _():
            send_n0()

        @pl.when(inside)
        def _():
            @on0
            def _():
                ready_n0()

        @pl.when(s < n_seq - 1)
        def _():
            @on1
            def _():
                ready_e1()

    put, finish_gather = gather_rows(hb.at[1])
    ready_u0 = forward(0, nothing, gap, gap_rs, put)
    finish_gather()

    def gap():
        @on1
        def _():
            ready_n1()

        @end1
        def _():
            far[1][0][1].start()

    put, finish_out = deliver(1)
    ready_u1 = forward(1, run_n1, gap, nothing, put)

    def gap_dot():
        @on1
        def _():
            ready_u1()

        @on1
        def _():
            z_first(0)

    def gap_chain(ready):
        @on1
        def _():
            ready()

        @first1
        def _():
            far[1][1][1].start()

    def gap_join():
        @last1
        def _():
            far[1][1][0].start()
            far[1][1][1].start()

        @on1
        def _():
            up1(1, 0)

    def gap_rs(ready):
        got["bc1"] = bc_start(1)

        @on1
        def _():
            ready()

        @end1
        def _():
            far[1][1][2].start()

        @on1
        def _():
            up1(1, 1)
            down1(1, 0)

    rows = backward(1, gap_dot, gap_chain, nothing, gap_join, gap_rs)
    put, finish_gather = gather_rows(eb.at[0])
    for q in range(parts_rs):
        put(q, rows[:, q * RW : (q + 1) * RW].astype(BF16))
    small1 = small_start(1)
    ready_bc1 = bc_mid(1, got["bc1"])
    bc_to1, bc_g1 = bc_copies(1), bc_gather_copies(1)

    @on1
    def _():
        down1(1, 1)
        up2(1, 0)

    finish_gather()

    run_e0, ready_e0 = collect_transposed(0, 0, eb.at[0])

    def gap_dot():
        run_e0()

        @on1
        def _():
            up1(1, 2)
            down2(1, 0)
            small_heads(1, small1)

        @on0
        def _():
            ready_u0()
            ready_e0()
            z_first(0)
            z_last(0, 0)

    def gap_chain(ready):
        @on1
        def _():
            up2(1, 1)
            small_seqs(small1)

        @on0
        def _():
            z_last(0, 1)
            ready()

        @first0
        def _():
            far[0][1][1].start()

    def gap_after():
        @on1
        def _():
            down1(1, 2, 0)

    def gap_join():
        @on0
        def _():
            z_last(0, 2)

        @last0
        def _():
            far[0][1][1].start()

        @on0
        def _():
            up1(0, 0)

        @on1
        def _():
            down1(1, 2, 1)

    def gap_rs(ready):
        got["bc0"] = bc_start(0)

        @on0
        def _():
            ready()

        @end0
        def _():
            far[0][1][2].start()

        @on0
        def _():
            up1(0, 1)

        @on1
        def _():
            down2(1, 1)
            up2(1, 2)
            bc_out_start(ready_bc1, bc_to1)
            z_final(1, 0)

    rows = backward(0, gap_dot, gap_chain, gap_after, gap_join, gap_rs)
    put, finish_in = deliver(0)
    for q in range(parts_rs):
        put(q, rows[:, q * RW : (q + 1) * RW])
    small0 = small_start(0)
    ready_bc0 = bc_mid(0, got["bc0"])
    bc_to0, bc_g0 = bc_copies(0), bc_gather_copies(0)

    @on1
    def _():
        small_finish(small1)
        bc_sum(bc_to1, bc_g1)
        z_final(1, 1)
        down2(1, 2)
        bc_finish(bc_g1)
        z_final(1, 2)

    @on0
    def _():
        bc_out_start(ready_bc0, bc_to0)
        down1(0, 0)
        up1(0, 2)
        small_heads(0, small0)
        up2(0, 0)
        down1(0, 1)
        down2(0, 0)
        up2(0, 1)
        down1(0, 2)
        z_final(0, 0)
        small_seqs(small0)
        down2(0, 1)
        bc_sum(bc_to0, bc_g0)
        z_final(0, 1)
        up2(0, 2)
        down2(0, 2)
        small_finish(small0)
        bc_finish(bc_g0)
        z_final(0, 2)

    finish_out()
    finish_in()
    save = links.local(ends, ends_out)
    save.start()
    save.wait()

    @pl.when(inside)
    def _():
        for i in range(n_seq - 1):
            z_sent(1, i)
            z_sent(2, i)

    @pl.when(is_first | (is_last & (c == 0)))
    def _():
        for i in range(n_seq - 1):
            z_sent(0, i)

    for l, copy in lt_sends:

        @pl.when(c != l)
        def _():
            copy.wait_send()

    for slot in range(2):
        for copy in rs_copies[slot]:
            copy.wait_send()
    links.drain()


def run_layers(tokens, cotangent, w_xz, w_bc, w_dt, w_out, in_gain, in_conv_x, in_conv_bc, in_head, in_out):
    n_seq, n_head = lax.axis_size("seq"), lax.axis_size("head")
    _, T, D = tokens.shape
    I = w_xz.shape[2]
    N = w_bc.shape[1] // 2
    heads = in_head.shape[2]
    XB = I + 2 * N
    G = 2 * I + 2 * N + LANES
    Q = T // n_head
    DB = D // n_seq
    BR = 2 * N // n_head + (heads + 15) // 16 * 16
    sems = 144 + 4 * (n_seq + n_head)
    S = jax.ShapeDtypeStruct
    V = pltpu.VMEM
    dma = pltpu.SemaphoreType.DMA
    vm = pl.BlockSpec(memory_space=pltpu.VMEM)
    hbm = pl.BlockSpec(memory_space=pl.ANY)
    scratch = [
        V((2, 2, D, I), BF16), V((2, D, 2 * N), BF16), V((2, LANES, D), BF16), V((2, I, D), BF16),
        V((2, 8, D), F32), V((2, T, D), BF16), V((2, T, D), BF16), V((T, D), BF16),
        V((2, T + EDGE, XB), BF16), V((2, T, I), F32), V((2, T, XB), F32),
        V((T, I), F32), V((T, I), F32), V((2, T, I), F32),
        V((2, T, LANES), F32), V((2, T, LANES), F32), V((2, T, LANES), F32), V((2, LANES, T), F32),
        V((2, N, T), BF16), V((2, N, T), BF16), V((2, T, N), BF16), V((2, T, N), BF16),
        V((2, N, I), F32), V((2, N, I), F32), V((T, I), BF16), V((T, I), BF16),
        V((2, T, LANES), F32),
        V((T, I), F32), V((T, I), F32), V((T, I), BF16), V((T, I), BF16),
        V((N, I), F32), V((N, I), F32), V((T + EDGE, XB), F32),
        V((T, T), F32), V((2, T, G), BF16), V((2, T, I), BF16), V((2, 8, D), F32),
        V((4, 8, T), F32), V((4, n_head - 1, 8, T), F32),
        V((2, T, D), BF16), V((2, n_head - 1, Q, D), BF16),
        V((4, 3, N, I // 3), BF16), V((4, 3, N, I // 3), BF16),
        V((2, EDGE, XB), BF16), V((2, EDGE, XB), BF16),
        V((2, Q, D), F32), V((2, Q, D), F32), V((I, LANES), BF16), V((T, T), F32),
        V((2, 2, D, T), BF16), V((D, T), BF16), V((3, 2, T, I), BF16),
        V((2, n_seq - 1, DB, I), BF16), V((2, DB, I), BF16), V((DB, I), F32), V((I, DB), F32),
        V((2, DB, T), BF16), V((2, T, I), BF16),
        V((2, n_head - 1, 2 * N // n_head, T), BF16), V((2, 2 * N, T), BF16), V((2, BR, T), BF16),
        V((2, BR, T), BF16), V((n_seq - 1, BR, DB), BF16), V((n_seq - 1, BR, DB), BF16),
        V((n_head, 2 * N // n_head, DB), F32),
        V((8, D), F32), V((8, D), F32), V((n_head - 1, 8, D), F32), V((8, D), F32),
        V((n_seq - 1, 8, D), F32),
        dma((24,)), dma((sems,)), dma((sems,)),
        dma((3 * (n_seq - 1),)), dma((3 * (n_seq + 1),)), dma((4,)),
    ]
    dims = (n_seq, n_head, T, D, I, N, heads)
    return pl.pallas_call(
        functools.partial(layer_kernel, dims),
        out_shape=(
            S((2, Q, D), F32), S((I, DB) if DB % LANES == 0 else (DB, I), F32), S((2, DB, I), F32),
            S((DB, 2 * N) if DB % LANES == 0 else (2 * N, DB), F32), S((heads, 1, DB), F32),
            S((1, D), F32), S((5, 1, I), F32), S((5, 1, 2 * N), F32), S((3, 1, heads), F32),
            S((1, I), F32),
            S((3, n_seq + 1, DB, I), BF16), S((2, 2, D, T), BF16), S((3, 2, T, I), BF16),
        ),
        in_specs=[hbm] * 6 + [vm] * 5,
        out_specs=(hbm, hbm, hbm, vm, vm, vm, vm, vm, vm, vm, hbm, hbm, hbm),
        scratch_shapes=scratch,
        compiler_params=pltpu.CompilerParams(
            collective_id=0, has_side_effects=True, vmem_limit_bytes=63 * 2**20
        ),
        name="layers",
    )(
        tokens, cotangent, w_xz, w_bc, w_dt, w_out, in_gain, in_conv_x, in_conv_bc, in_head, in_out
    )[:10]


def body(
    tokens, cotangent, norm_gain, w_xz, w_bc, w_dt, conv_x, conv_bc, head_params, out_gain, w_out
):
    heads = w_dt.shape[2]
    dt_rows = jnp.pad(w_dt[0].T, ((0, LANES - heads), (0, 0)))
    ends, gw_out, gw_xz, gw_bc, gw_dt, g_gain, g_conv_x, g_conv_bc, g_head, g_out = run_layers(
        tokens,
        cotangent,
        jnp.swapaxes(w_xz[0], 0, 1),
        w_bc[0],
        dt_rows,
        w_out[0],
        norm_gain,
        jnp.swapaxes(conv_x, 0, 1),
        jnp.swapaxes(conv_bc, 0, 1),
        jnp.swapaxes(head_params, 0, 1),
        out_gain,
    )
    if gw_bc.shape[1] != w_bc.shape[2]:
        gw_bc = gw_bc.T
        gw_out = gw_out.T
    return (
        ends[None],
        g_gain,
        jnp.swapaxes(gw_xz, 0, 1)[None],
        gw_bc[None],
        jnp.transpose(gw_dt, (1, 2, 0)),
        jnp.swapaxes(g_conv_x, 0, 1),
        jnp.swapaxes(g_conv_bc, 0, 1),
        jnp.swapaxes(g_head, 0, 1),
        g_out,
        gw_out[None],
    )


def solution(mesh):
    placed = (
        P(None, "seq", None),
        P(None, "seq", None),
        P("section", None),
        P("section", None, None, "head"),
        P("section", None, None),
        P("section", None, "head"),
        P("section", None, "head"),
        P("section", None, None),
        P("section", None, "head"),
        P("section", "head"),
        P("section", "head", None),
    )
    return jax.shard_map(
        body,
        mesh=mesh,
        in_specs=placed,
        out_specs=(
            P("section", None, ("seq", "head"), None),
            P("section", None),
            P("section", "seq", None, "head"),
            P("section", "seq", None),
            P("section", "seq", "head"),
            P("section", None, "head"),
            P("section", None, None),
            P("section", None, "head"),
            P("section", "head"),
            P("section", "head", "seq"),
        ),
        check_vma=False,
    )
```

```python
import functools

import jax
import jax.numpy as jnp
from jax import lax
from jax.experimental import pallas as pl
from jax.experimental.pallas import tpu as pltpu
from jax.sharding import PartitionSpec as P

EPSILON = 1e-05
MESH = pl.DeviceIdType.MESH
LANES = 128
EDGE = 16
F32 = jnp.float32
BF16 = jnp.bfloat16


def dot(a, b):
    return lax.dot_general(a, b, (((1,), (0,)), ((), ())), preferred_element_type=F32)


def dot_nt(a, b):
    return lax.dot_general(a, b, (((1,), (1,)), ((), ())), preferred_element_type=F32)


def dot_tn(a, b):
    return lax.dot_general(a, b, (((0,), (0,)), ((), ())), preferred_element_type=F32)


def exact_dot(a, b):
    return lax.dot_general(
        a, b, (((1,), (0,)), ((), ())), precision=lax.Precision.HIGHEST, preferred_element_type=F32
    )


def split_dot(a, b):
    high = a.astype(BF16)
    return dot(high, b) + dot((a - high.astype(F32)).astype(BF16), b)


class Links:
    def __init__(self, local_sem, send_sem, recv_sem):
        self.local_sem, self.send_sem, self.recv_sem = local_sem, send_sem, recv_sem
        self.local_count = 0
        self.count = 0
        self.pending = []

    def local(self, src, dst):
        index = self.local_count
        assert index < self.local_sem.shape[0]
        self.local_count += 1
        return pltpu.make_async_copy(src, dst, self.local_sem.at[index])

    def remote(self, src, dst, peer, when=None):
        index = self.count
        assert index < self.send_sem.shape[0]
        self.count += 1
        copy = pltpu.make_async_remote_copy(
            src_ref=src,
            dst_ref=dst,
            send_sem=self.send_sem.at[index],
            recv_sem=self.recv_sem.at[index],
            device_id=peer,
            device_id_type=MESH,
        )
        self.pending.append((copy, when))
        return copy

    def drain(self):
        for copy, when in self.pending:
            if when is None:
                copy.wait_send()
            else:

                @pl.when(when)
                def _():
                    copy.wait_send()


def wait_if(condition, copy):
    @pl.when(condition)
    def _():
        copy.wait_recv()


def start_if(condition, copy):
    @pl.when(condition)
    def _():
        copy.start()


def lanes(i, width=LANES):
    if isinstance(i, int):
        return pl.ds(i * width, width)
    return pl.ds(pl.multiple_of(i * width, width), width)


def layer_kernel(dims, *refs):
    (n_seq, n_head, T, D, I, N, heads) = dims
    (
        tokens, cotangent, w_xz, w_bc, w_dt, w_out, in_gain, in_conv_x, in_conv_bc, in_head, in_out,
        ends_out, gw_out, gw_xz, gw_bc, gw_dt, g_gain, g_conv_x, g_conv_bc, g_head, g_out, z_land, far_lt, far_rhs,
        wxz, wbc, wdt, wo, prm, hb, eb, nm, xin, z, act, dte, cume, y0,
        sgdt, dtv, cum, cumT, CT, BT, Bb, Cb, st_loc, s_ent, xtb, xtl, qb,
        du, dy, dyb, dye, dst_loc, gin, dact, dcbt, gp, us, small,
        row_send, row_recv, rs_send, rs_recv, ch_send, ch_recv, edge_send, edge_recv,
        end_send, ends, et, tri,
        lt, lt_send, rhs, z_send, z_in, z_acc, z_turn, far_l, far_r, bc_recv, bc_t, bc_rows, bc_rhs, bc_send, bc_land, bc_all,
        sm_o, sm_t, sm_h, sm_u, sm_z,
        local_sem, send_sem, recv_sem, zs_sem, zr_sem, zi_sem,
    ) = refs
    c = lax.axis_index("section")
    s = lax.axis_index("seq")
    k = lax.axis_index("head")
    links = Links(local_sem, send_sem, recv_sem)
    Q = T // n_head
    XB = I + 2 * N
    DB = D // n_seq
    pairs = I // LANES
    head_size = I // heads
    is_first = s == 0
    is_last = s == n_seq - 1
    has_prev = s > 0
    has_next = s < n_seq - 1
    other = {"section": 1 - c}
    prev_dev = {"seq": jnp.maximum(s - 1, 0)}
    next_dev = {"seq": jnp.minimum(s + 1, n_seq - 1)}
    if n_head == 4:
        peer_at = [3 - k, k + 1 - 2 * lax.rem(k, 2), lax.rem(k + 2, 4)]
    else:
        peer_at = [lax.rem(k + d, n_head) for d in range(1, n_head)]
    head_peers = [{"head": at} for at in peer_at]
    seq_peers = [{"seq": lax.rem(s + d, n_seq)} for d in range(1, n_seq)]
    own_rows = pl.ds(pl.multiple_of(k * Q, Q), Q)
    chunks = 6
    CW = I // chunks
    ntile = 256
    inner_total = I * n_head
    Q2 = 2 * N // n_head
    rs_copies = {}
    parts_rs = 3
    RW = D // parts_rs

    barrier = pltpu.get_barrier_semaphore()
    for peer in [other] + head_peers + seq_peers:
        pl.semaphore_signal(barrier, inc=1, device_id=peer, device_id_type=MESH)

    load_h = links.local(tokens.at[c], hb.at[0])
    load_e = links.local(cotangent.at[c], eb.at[1])
    load_h.start()
    parts = (
        (w_xz.at[0], wxz.at[c, 0]),
        (w_bc, wbc.at[c]),
        (w_dt, wdt.at[c]),
        (w_xz.at[1], wxz.at[c, 1]),
        (w_out, wo.at[c]),
    )
    mine = [links.local(src, dst) for src, dst in parts]
    for copy in mine:
        copy.start()
    load_e.start()
    pl.semaphore_wait(barrier, n_head + n_seq - 1)
    low_row = lax.broadcasted_iota(jnp.int32, (1, LANES), 1) < head_size
    prm[c] = jnp.zeros((8, D), F32)
    prm[c, 0:1, :] = in_gain[...]
    for r in range(5):
        prm[c, 1 + r : 2 + r, :I] = in_conv_x[r]
        prm[c, 1 + r : 2 + r, I : I + 2 * N] = in_conv_bc[r]
    prm[c, 6:7, :I] = in_out[...]
    prm[c, 6:7, I : I + heads] = in_head[0]
    prm[c, 6:7, I + LANES : I + LANES + heads] = in_head[1]
    skips = in_head[2]
    for p in range(pairs):
        prm[c, 7:8, lanes(p)] = jnp.where(
            low_row, skips[:, 2 * p : 2 * p + 1], skips[:, 2 * p + 1 : 2 * p + 2]
        )
    theirs = [links.remote(prm.at[c], prm.at[c], other)]
    theirs += [links.remote(src, dst, other) for src, dst in parts]
    for copy in theirs:
        copy.start()

    def weights_ready(layer, which):
        @pl.when(c == layer)
        def _():
            for i in which:
                if i:
                    mine[i - 1].wait()

        @pl.when(c != layer)
        def _():
            for i in which:
                theirs[i].wait_recv()

    row_i = lax.broadcasted_iota(jnp.int32, (T, T), 0)
    col_i = lax.broadcasted_iota(jnp.int32, (T, T), 1)
    tri[...] = jnp.where(row_i >= col_i, 1.0, 0.0)
    er = lax.broadcasted_iota(jnp.int32, (I, LANES), 0)
    ec = lax.broadcasted_iota(jnp.int32, (I, LANES), 1)
    et[...] = jnp.where(
        (er >= ec * head_size) & (er < (ec + 1) * head_size), 1.0, 0.0
    ).astype(BF16)
    small[...] = jnp.zeros_like(small)
    load_h.wait()

    def exchange_rows(total_cols, slot):
        summed = jnp.sum(total_cols, axis=1, keepdims=True)
        as_row = jnp.transpose(jnp.broadcast_to(summed, (T, LANES)))[:8]
        row_send[slot] = as_row
        copies = []
        for d, peer in enumerate(head_peers):
            copy = links.remote(row_send.at[slot], row_recv.at[slot, d], peer)
            copy.start()
            copies.append(copy)

        def finish():
            total = row_send[slot]
            for d, copy in enumerate(copies):
                copy.wait_recv()
                total = total + row_recv[slot, d]
            wide = jnp.broadcast_to(total[:1], (LANES, T))
            return jnp.transpose(wide)

        return finish

    def reduce_rows(slot):
        copies = []
        for q in range(parts_rs):
            at = pl.ds(q * RW, RW)
            row = []
            for d, peer in enumerate(head_peers):
                rows = pl.ds(pl.multiple_of(peer_at[d] * Q, Q), Q)
                row.append(
                    links.remote(rs_send.at[slot, rows, at], rs_recv.at[slot, d, :, at], peer)
                )
                links.pending.pop()
            copies.append(row)
        rs_copies[slot] = [copy for row in copies for copy in row]

        def send(q):
            for copy in copies[q]:
                copy.start()

        def part(q):
            at = pl.ds(q * RW, RW)
            total = rs_send[slot, own_rows, at].astype(F32)
            for d, copy in enumerate(copies[q]):
                copy.wait_recv()
                total = total + rs_recv[slot, d, :, at].astype(F32)
            return total

        return send, part

    def gather_rows(target):
        copies = []
        for q in range(parts_rs):
            at = target.at[own_rows, pl.ds(q * RW, RW)]
            copies.append([links.remote(at, at, peer) for peer in head_peers])

        def send(q, rows):
            target[own_rows, pl.ds(q * RW, RW)] = rows
            for copy in copies[q]:
                copy.start()

        def finish():
            for row in copies:
                for copy in row:
                    copy.wait_recv()

        return send, finish

    def chain(slot, forward, local, dec_row, into):
        starts, goes_on = (is_first, has_next) if forward else (is_last, has_prev)
        receives = has_prev if forward else has_next
        peer = next_dev if forward else prev_dev
        copies = []
        for j in range(chunks):
            copies.append(
                links.remote(ch_send.at[slot, j], ch_recv.at[slot, j], peer, goes_on)
            )

        def begin():
            @pl.when(starts)
            def _():
                for j in range(chunks):
                    ch_send[slot, j] = local[:, lanes(j, CW)].astype(BF16)
                    start_if(goes_on, copies[j])

        def finish():
            @pl.when(starts)
            def _():
                into[...] = jnp.zeros_like(into)

            @pl.when(receives)
            def _():
                for j in range(chunks):
                    copies[j].wait_recv()
                    at = lanes(j, CW)
                    arrived = ch_recv[slot, j].astype(F32)
                    into[:, at] = arrived

                    @pl.when(goes_on)
                    def _():
                        ch_send[slot, j] = (
                            arrived * dec_row[:, j * CW : (j + 1) * CW] + local[:, at]
                        ).astype(BF16)
                        copies[j].start()

        return begin, finish

    def collect(l, src, dst):
        near = links.local(src, dst)
        far = links.remote(src, dst, other, c != l)

        @pl.when(c == l)
        def _():
            near.start()

        @pl.when(c != l)
        def _():
            far.start()

        def ready():
            near.wait()
            far.wait_recv()

        return ready

    lt_sends = []

    def collect_transposed(l, kind, src):
        far = links.remote(lt_send, lt.at[kind, c], other, c != l)
        links.pending.pop()
        before = [copy for layer, copy in lt_sends if layer == l]
        lt_sends[:] = [item for item in lt_sends if item[0] != l] + [(l, far)]

        def run():
            @pl.when(c == l)
            def _():
                def turn(t, _):
                    lt[kind, c, lanes(t), :] = jnp.transpose(src[:, lanes(t)].astype(F32)).astype(BF16)
                    return 0

                lax.fori_loop(0, D // LANES, turn, 0)

            @pl.when(c != l)
            def _():
                for copy in before:
                    copy.wait_send()

                def turn(t, _):
                    lt_send[lanes(t), :] = jnp.transpose(src[:, lanes(t)].astype(F32)).astype(BF16)
                    return 0

                lax.fori_loop(0, D // LANES, turn, 0)
                far.start()

        def ready():
            far.wait_recv()

        return run, ready

    low_half = s < n_seq // 2
    is_end = is_first | is_last
    inside = has_prev & has_next
    inward = {"seq": jnp.where(is_first, 1, jnp.where(is_last, n_seq - 2, s))}

    def far_copies(l, kinds, pieces):
        def one(a, there, i):
            ends = is_end if far_up(l, i) else is_last
            return links.remote(a.at[i], there.at[i], inward, ends & (c == l))

        return (
            {i: one(lt, far_lt, i) for i in kinds},
            {i: one(rhs, far_rhs, i) for i in pieces},
        )

    def far_up(l, piece):
        return piece > 0

    def far_down(l, piece):
        return l == 1 or piece > 0

    def z_copy(piece, j, up):
        if up:
            slot, peer = j, next_dev
        else:
            slot, peer = jnp.where(j == s - 1, n_seq, j), prev_dev
        index = jnp.where(j < s, j, j - 1)
        return pltpu.make_async_remote_copy(
            src_ref=z_send.at[piece % 2, index],
            dst_ref=z_land.at[piece, slot],
            send_sem=zs_sem.at[piece * (n_seq - 1) + index],
            recv_sem=zr_sem.at[piece * (n_seq + 1) + slot],
            device_id=peer,
            device_id_type=MESH,
        )

    def z_arrived(piece, slot, into):
        pltpu.make_async_remote_copy(
            src_ref=z_send.at[piece % 2, 0],
            dst_ref=z_land.at[piece, slot],
            send_sem=zs_sem.at[piece * (n_seq - 1)],
            recv_sem=zr_sem.at[piece * (n_seq + 1) + slot],
            device_id=prev_dev,
            device_id_type=MESH,
        ).wait_recv()
        return pltpu.make_async_copy(z_land.at[piece, slot], z_in.at[into], zi_sem.at[into])

    def z_block(piece, j, store, far):
        kind = 0 if piece == 0 else 1
        rows = pl.ds(pl.multiple_of(j * DB, DB), DB)
        if far:
            load = pltpu.make_async_copy(far_lt.at[kind, :, rows], far_l, zi_sem.at[2])
            load.start()
            load.wait()

        def tile(t, _):
            at = lanes(t, ntile)
            value = dot(lt[kind, 0, rows, :], rhs[piece, 0, :, at]) + dot(
                lt[kind, 1, rows, :], rhs[piece, 1, :, at]
            )
            if far:
                value = value + dot(far_l[0], far_r[0, :, at]) + dot(far_l[1], far_r[1, :, at])
            store(at, value)
            return 0

        lax.fori_loop(0, I // ntile, tile, 0)

    def z_one(piece, j, up):
        index = jnp.where(j < s, j, j - 1)
        def store(at, value):
            z_send[piece % 2, index, :, at] = value.astype(BF16)

        z_block(piece, j, store, False)
        z_copy(piece, j, up).start()
        return 0

    def z_first(piece):
        @pl.when(is_first)
        def _():
            lax.fori_loop(0, n_seq - 1, lambda i, _: z_one(piece, n_seq - 1 - i, True), 0)

    def z_last(piece, part):
        low, high = (n_seq - 1) * part // 3, (n_seq - 1) * (part + 1) // 3

        @pl.when(is_last)
        def _():
            lax.fori_loop(low, high, lambda i, _: z_one(piece, i, False), 0)

    def far_load(piece):
        load = pltpu.make_async_copy(far_rhs.at[piece], far_r, zi_sem.at[3])
        load.start()
        load.wait()

    def z_sent(piece, index):
        pltpu.make_async_remote_copy(
            src_ref=z_send.at[piece % 2, index],
            dst_ref=z_land.at[piece, 0],
            send_sem=zs_sem.at[piece * (n_seq - 1) + index],
            recv_sem=zr_sem.at[piece * (n_seq + 1)],
            device_id=next_dev,
            device_id_type=MESH,
        ).wait_send()

    def z_forward(l, piece, up, first, part=None):
        mine = inside & (low_half if up == first else jnp.logical_not(low_half))
        count = n_seq - 1 - s if up else s
        begin, end = 0, count
        if part is not None:
            begin, end = (0, count // 2) if part == 0 else (count // 2, count)

        def one(i, _, far):
            j = n_seq - 1 - i if up else i
            index = jnp.where(j < s, j, j - 1)
            if piece == 2:
                z_sent(0, index)
            if not far:
                load = z_arrived(piece, j, 0)
                load.start()
                load.wait()

            def store(at, value):
                if not far:
                    value = value + z_in[0, :, at].astype(F32)
                z_send[piece % 2, index, :, at] = value.astype(BF16)

            z_block(piece, j, store, far)
            z_copy(piece, j, up).start()
            return 0

        use_far = far_up(l, piece) if up else far_down(l, piece)
        near = s == 1 if up else s == n_seq - 2
        if first and use_far:

            @pl.when(mine & near)
            def _():
                if not part:
                    if piece < 2:
                        far[l][0][piece].wait_recv()
                    far[l][1][piece].wait_recv()
                far_load(piece)
                lax.fori_loop(begin, end, functools.partial(one, far=True), 0)

            if n_seq > 4:

                @pl.when(mine & jnp.logical_not(near))
                def _():
                    lax.fori_loop(begin, end, functools.partial(one, far=False), 0)

        else:

            @pl.when(mine)
            def _():
                lax.fori_loop(begin, end, functools.partial(one, far=False), 0)

    def z_final(l, piece):
        by_low, by_high = far_up(l, piece), far_down(l, piece)
        from_low = s >= (2 if by_low else 1)
        from_high = s < n_seq - (2 if by_high else 1)
        near = ((s == 1) & by_low) | ((s == n_seq - 2) & by_high)

        @pl.when(from_low)
        def _():
            z_arrived(piece, s, 0).start()

        @pl.when(from_high)
        def _():
            z_arrived(piece, n_seq, 1).start()

        def hold(at, value):
            z_acc[:, at] = value

        if by_low or by_high:

            @pl.when(near)
            def _():
                far_load(piece)
                z_block(piece, s, hold, True)

            @pl.when(jnp.logical_not(near))
            def _():
                z_block(piece, s, hold, False)

        else:
            z_block(piece, s, hold, False)

        @pl.when(from_low)
        def _():
            pltpu.make_async_copy(z_land.at[piece, s], z_in.at[0], zi_sem.at[0]).wait()
            z_acc[...] += z_in[0].astype(F32)

        @pl.when(from_high)
        def _():
            pltpu.make_async_copy(z_land.at[piece, n_seq], z_in.at[1], zi_sem.at[1]).wait()
            z_acc[...] += z_in[1].astype(F32)

        if piece == 0 and DB % LANES == 0:
            for t in range(I // ntile):
                z_turn[t * ntile : (t + 1) * ntile, :] = jnp.transpose(z_acc[:, t * ntile : (t + 1) * ntile])
            save = pltpu.make_async_copy(z_turn, gw_out, zi_sem.at[0])
        else:
            target = gw_out if piece == 0 else gw_xz.at[2 - piece]
            save = pltpu.make_async_copy(z_acc, target, zi_sem.at[0])
        save.start()
        save.wait()

    lane_low = lax.broadcasted_iota(jnp.int32, (T, LANES), 1) < head_size
    later = row_i >= col_i
    earlier = col_i >= row_i

    def spread_heads(l):
        for p in range(pairs):
            at = lanes(p)
            dte[:, at] = jnp.where(
                lane_low, dtv[l, :, 2 * p : 2 * p + 1], dtv[l, :, 2 * p + 1 : 2 * p + 2]
            )
            cume[:, at] = jnp.where(
                lane_low, cum[l, :, 2 * p : 2 * p + 1], cum[l, :, 2 * p + 1 : 2 * p + 2]
            )

    def steps(l):
        def one(p, _):
            at = lanes(p)
            acc = cume[:, at]
            stepped = dte[:, at] * act[l, :, at]
            xtb[:, at] = stepped.astype(BF16)
            xtl[:, at] = (stepped * jnp.exp(acc[T - 1 : T] - acc)).astype(BF16)
            return 0

        lax.fori_loop(0, pairs, one, 0)

    def conv_sum(l, at, v):
        total = prm[l, 5:6, at] + prm[l, 4:5, at] * v[EDGE:]
        moved = []
        for shift in range(1, 4):
            moved.append(pltpu.roll(v, shift, 0)[EDGE:])
            total = total + prm[l, 4 - shift : 5 - shift, at] * moved[-1]
        return total, [v[EDGE:]] + moved

    def forward(l, gap_norm, gap_chain):
        weights_ready(l, [0])
        gain = prm[l, 0:1, :]

        def norm_rows(i, _):
            rows = pl.ds(pl.multiple_of(i * 32, 32), 32)
            v = hb[l, rows, :].astype(F32)
            rstd = lax.rsqrt(jnp.mean(v * v, axis=1, keepdims=True) + EPSILON)
            nm[rows, :] = (v * rstd * gain).astype(BF16)
            return 0

        lax.fori_loop(0, T // 32, norm_rows, 0)

        gap_norm()
        weights_ready(l, [1, 2, 3])

        def project_x(j, _):
            xin[l, EDGE:, lanes(j, ntile)] = dot(
                nm[...], wxz[l, 0, :, lanes(j, ntile)]
            ).astype(BF16)
            return 0

        lax.fori_loop(0, I // ntile, project_x, 0)
        xin[l, EDGE:, I:] = dot(nm[...], wbc[l]).astype(BF16)

        edge = links.remote(
            xin.at[l, pl.ds(T, EDGE)], xin.at[l, pl.ds(0, EDGE)], next_dev, has_next
        )
        start_if(has_next, edge)

        dt_raw = dot_nt(nm[...], wdt[l])
        hp0 = prm[l, 6:7, I : I + LANES]
        hp1 = prm[l, 6:7, I + LANES : I + 2 * LANES]
        pre_dt = dt_raw + hp0
        sgdt[l] = lax.logistic(pre_dt)
        step = jnp.maximum(pre_dt, 0.0) + jnp.log1p(jnp.exp(-jnp.abs(pre_dt)))
        dtv[l] = step
        cum[l] = exact_dot(tri[...], -jnp.exp(hp1) * step)
        cumT[l] = jnp.transpose(cum[l])

        weights_ready(l, [4])

        def project_z(j, _):
            z[l, :, lanes(j, ntile)] = dot(nm[...], wxz[l, 1, :, lanes(j, ntile)])
            return 0

        lax.fori_loop(0, I // ntile, project_z, 0)

        @pl.when(is_first)
        def _():
            xin[l, :EDGE, :] = jnp.zeros((EDGE, XB), BF16)

        wait_if(has_prev, edge)

        def conv(j, _):
            at = lanes(j)
            total, _ = conv_sum(l, at, xin[l, :, at].astype(F32))
            act[l, :, at] = total * lax.logistic(total)
            return 0

        lax.fori_loop(0, XB // LANES, conv, 0)

        mat_b = act[l, :, I : I + N]
        mat_c = act[l, :, I + N :]
        Bb[l] = mat_b.astype(BF16)
        Cb[l] = mat_c.astype(BF16)
        BT[l] = jnp.transpose(mat_b).astype(BF16)
        CT[l] = jnp.transpose(mat_c).astype(BF16)
        spread_heads(l)
        steps(l)

        def local_state(j, _):
            st_loc[l, :, lanes(j, ntile)] = dot(BT[l], xtl[:, lanes(j, ntile)])
            return 0

        lax.fori_loop(0, I // ntile, local_state, 0)
        begin, finish_chain = chain(
            l, True, st_loc.at[l], jnp.exp(cume[T - 1 : T, :]), s_ent.at[l]
        )
        begin()

        cb = dot_nt(Cb[l], Bb[l])

        def intra(p, _):
            at = lanes(p)
            wide = cume[:, at]
            values = xtb[:, at]
            total = jnp.zeros((T, LANES), F32)
            for half in range(2):
                column = wide[:, half * head_size : half * head_size + 1]
                row = cumT[l, pl.ds(2 * p + half, 1), :]
                decay = jnp.where(later, jnp.exp(jnp.minimum(column - row, 0.0)), 0.0)
                mix = (cb * decay).astype(BF16)
                kept = jnp.where(lane_low == (half == 0), values, jnp.zeros_like(values))
                total = total + dot(mix, kept)
            y0[l, :, at] = total
            return 0

        lax.fori_loop(0, pairs, intra, 0)
        gap_chain()
        finish_chain()

        def gate(p, ssq):
            at = lanes(p)
            carried = dot(Cb[l], s_ent[l, :, at].astype(BF16))
            y = y0[l, :, at] + jnp.exp(cume[:, at]) * carried
            y0[l, :, at] = y
            full = y + prm[l, 7:8, at] * act[l, :, at]
            gate_in = z[l, :, at]
            value = full * (gate_in * lax.logistic(gate_in))
            dye[:, at] = (value * prm[l, 6:7, at]).astype(BF16)
            return ssq + value * value

        ssq = lax.fori_loop(0, pairs, gate, jnp.zeros((T, LANES), F32))
        return exchange_rows(ssq, l)

    def project_branch(l):
        if l == 0:
            weights_ready(l, [5])
        rs_start, rs_part = reduce_rows(l)

        def project_out(j, _):
            rs_send[l, :, lanes(j, ntile)] = dot(dye[...], wo[l, :, lanes(j, ntile)]).astype(BF16)
            return 0

        for q in range(parts_rs):
            lax.fori_loop(q * RW // ntile, (q + 1) * RW // ntile, project_out, 0)
            rs_start(q)
        return rs_part

    def gated(l, at):
        gate_in = z[l, :, at]
        return (y0[l, :, at] + prm[l, 7:8, at] * act[l, :, at]) * (gate_in * lax.logistic(gate_in))

    def scale_branch(l, finish_rows):
        qb[l] = lax.rsqrt(finish_rows() / inner_total + EPSILON)

        def scaled(p, _):
            at = lanes(p)
            us[l, :, at] = (gated(l, at) * qb[l] * prm[l, 6:7, at]).astype(BF16)
            return 0

        lax.fori_loop(0, pairs, scaled, 0)
        return collect(l, us.at[l], rhs.at[0, c])

    def finish_branch(l, rs_part, put):
        q_own = qb[l, own_rows, :][:, :1]
        for q in range(parts_rs):
            at = pl.ds(q * RW, RW)
            rows = hb[l, own_rows, at].astype(F32) + q_own * rs_part(q)
            put(q, rows.astype(BF16))

    def backward(l, gap_dot, gap_chain, gap_after, gap_join, gap_rs):
        hp1 = prm[l, 6:7, I + LANES : I + 2 * LANES]

        def start_du(j, acc):
            at = lanes(j, ntile)
            got = dot_nt(eb[l], wo[l, at, :])
            du[:, at] = got
            value = got * gated(l, at)
            weighted = value * prm[l, 6:7, at]
            return acc + weighted[:, :LANES] + weighted[:, LANES:]

        if l == 1:
            weights_ready(l, [5])
        acc = lax.fori_loop(0, I // ntile, start_du, jnp.zeros((T, LANES), F32))
        finish_rows = exchange_rows(acc, 2 + l)
        if l == 0:
            spread_heads(l)
            steps(l)
        gap_dot()
        dot_all = finish_rows()

        def through_gate(p, _):
            at = lanes(p)
            q = qb[l]
            gate_in = z[l, :, at]
            sig = lax.logistic(gate_in)
            silu = gate_in * sig
            x_now = act[l, :, at]
            full = y0[l, :, at] + prm[l, 7:8, at] * x_now
            small[l, 6:7, at] = jnp.sum(du[:, at] * full * silu * q, axis=0, keepdims=True)
            dg = q * (du[:, at] * prm[l, 6:7, at]) - full * silu * (q * q * q) * (
                dot_all / inner_total
            )
            d_y = dg * silu
            gp[l, :, lanes(p + pairs)] = (
                dg * full * sig * (1.0 + gate_in * (1.0 - sig))
            ).astype(BF16)
            small[l, 7:8, at] = jnp.sum(d_y * x_now, axis=0, keepdims=True)
            dy[:, at] = d_y
            dyb[:, at] = d_y.astype(BF16)
            dye[:, at] = (d_y * jnp.exp(cume[:, at])).astype(BF16)
            return 0

        lax.fori_loop(0, pairs, through_gate, 0)

        def local_state(j, _):
            dst_loc[:, lanes(j, ntile)] = dot(CT[l], dye[:, lanes(j, ntile)])
            return 0

        lax.fori_loop(0, I // ntile, local_state, 0)
        begin, finish_chain = chain(
            2 + l, False, dst_loc, jnp.exp(cume[T - 1 : T, :]), gin
        )
        begin()
        ready_z = collect(l, gp.at[l, :, pl.ds(I, I)], rhs.at[1, c])

        cbt = dot_nt(Bb[l], Cb[l])
        dcbt[...] = jnp.zeros_like(dcbt)

        def intra(p, _):
            at = lanes(p)
            wide = cume[:, at]
            values = xtb[:, at]
            grads = dyb[:, at]
            total = jnp.zeros((T, LANES), F32)
            for half in range(2):
                column = wide[:, half * head_size : half * head_size + 1]
                row = cumT[l, pl.ds(2 * p + half, 1), :]
                decay = jnp.where(earlier, jnp.exp(jnp.minimum(row - column, 0.0)), 0.0)
                mix = (cbt * decay).astype(BF16)
                kept = jnp.where(lane_low == (half == 0), grads, jnp.zeros_like(grads))
                total = total + dot(mix, kept)
                dcbt[...] += dot_nt(values, kept) * decay
            du[:, at] = total
            return 0

        lax.fori_loop(0, pairs, intra, 0)
        gap_chain(ready_z)
        finish_chain()
        gap_after()

        def join(p, carry):
            sum_v, sum_w = carry
            at = lanes(p)
            into = gin[:, at]
            acc = cume[:, at]
            end = acc[T - 1 : T]
            got = du[:, at] + jnp.exp(end - acc) * dot(Bb[l], into.astype(BF16))
            x_now = act[l, :, at]
            d_y = dy[:, at]
            leaving = s_ent[l, :, at] * jnp.exp(end) + st_loc[l, :, at]
            final = jnp.sum(into * leaving, axis=0, keepdims=True)
            v = dyb[:, at].astype(F32) * y0[l, :, at] - xtb[:, at].astype(F32) * got
            is_end = lax.broadcasted_iota(jnp.int32, (T, LANES), 0) == T - 1
            v = v + jnp.where(is_end, final, 0.0)
            dact[:T, at] = dte[:, at] * got + prm[l, 7:8, at] * d_y
            picks = et[at, :]
            return (sum_v + split_dot(v, picks), sum_w + split_dot(x_now * got, picks))

        zero = jnp.zeros((T, LANES), F32)
        sum_v, sum_w = lax.fori_loop(0, pairs, join, (zero, zero))

        dcb_low = dcbt[...].astype(BF16)
        gin_low = gin[...].astype(BF16)
        ent_low = s_ent[l].astype(BF16)
        dact[:T, I : I + N] = dot(dcb_low, Cb[l]) + dot_nt(xtl[...], gin_low)
        dact[:T, I + N :] = dot_tn(dcb_low, Bb[l]) + dot_nt(dye[...], ent_low)

        def conv_pre(j, _):
            at = lanes(j)
            total, moved = conv_sum(l, at, xin[l, :, at].astype(F32))
            sig = lax.logistic(total)
            got = dact[:T, at] * (sig * (1.0 + total * (1.0 - sig)))
            dact[:T, at] = got
            edge_send[l, :, at] = got[:EDGE].astype(BF16)
            small[l, 5:6, at] = jnp.sum(got, axis=0, keepdims=True)
            for shift in range(4):
                small[l, 4 - shift : 5 - shift, at] = jnp.sum(
                    got * moved[shift], axis=0, keepdims=True
                )
            return 0

        lax.fori_loop(0, XB // LANES, conv_pre, 0)
        edge = links.remote(edge_send.at[l], edge_recv.at[l], prev_dev, has_prev)
        start_if(has_prev, edge)

        d_log = lax.dot_general(
            tri[...], sum_v, (((0,), (0,)), ((), ())),
            precision=lax.Precision.HIGHEST, preferred_element_type=F32,
        )
        rate = -jnp.exp(hp1)
        d_raw = (sum_w + d_log * rate) * sgdt[l]
        small[l, 6:7, I : I + LANES] = jnp.sum(d_raw, axis=0, keepdims=True)
        small[l, 6:7, I + LANES : I + 2 * LANES] = jnp.sum(
            d_log * rate * dtv[l], axis=0, keepdims=True
        )
        d_raw = jnp.where(lax.broadcasted_iota(jnp.int32, (T, LANES), 1) < heads, d_raw, 0.0)
        gp[l, :, 2 * I + 2 * N :] = d_raw.astype(BF16)
        dt_rows = bc_rows.shape[1] - Q2
        bc_rows[l, Q2:, :] = jnp.transpose(d_raw)[:dt_rows].astype(BF16)
        gap_join()

        @pl.when(is_last)
        def _():
            dact[T:, :] = jnp.zeros((EDGE, XB), F32)

        @pl.when(has_next)
        def _():
            edge.wait_recv()
            dact[T:, :] = edge_recv[l].astype(F32)

        def conv_in(j, _):
            at = lanes(j)
            v = dact[:, at]
            total = prm[l, 4:5, at] * v[:T]
            for shift in range(1, 4):
                moved = pltpu.roll(v, T + EDGE - shift, 0)
                total = total + prm[l, 4 - shift : 5 - shift, at] * moved[:T]
            dact[:T, at] = total
            return 0

        lax.fori_loop(0, XB // LANES, conv_in, 0)
        gp[l, :, :I] = dact[:T, :I].astype(BF16)
        gp[l, :, 2 * I : 2 * I + 2 * N] = dact[:T, I:].astype(BF16)

        def normed_all(j, _):
            at = lanes(j, ntile)
            total = dot_nt(gp[l, :, I : 2 * I], wxz[l, 1, at, :])
            total = total + dot_nt(gp[l, :, :I], wxz[l, 0, at, :])
            total = total + dot_nt(gp[l, :, 2 * I : 2 * I + 2 * N], wbc[l, at, :])
            total = total + dot(gp[l, :, 2 * I + 2 * N :], wdt[l, :, at])
            rs_send[1 - l, :, at] = total.astype(BF16)
            return 0

        for copy in rs_copies[1 - l]:
            copy.wait_send()
        rs_start, rs_part = reduce_rows(1 - l)
        for q in range(parts_rs):
            lax.fori_loop(q * RW // ntile, (q + 1) * RW // ntile, normed_all, 0)
            rs_start(q)
        ready_x = collect(l, gp.at[l, :, pl.ds(0, I)], rhs.at[2, c])
        gap_rs(ready_x)
        got = jnp.concatenate([rs_part(q) for q in range(parts_rs)], axis=1)
        v = hb[l, own_rows, :].astype(F32)
        rstd = lax.rsqrt(jnp.mean(v * v, axis=1, keepdims=True) + EPSILON)
        small[l, 0:1, :] = jnp.sum(got * v * rstd, axis=0, keepdims=True)
        hat = got * prm[l, 0:1, :]
        inner = jnp.sum(hat * v, axis=1, keepdims=True)
        return (
            rstd * hat - v * (rstd * rstd * rstd) * inner / D
            + eb[l, own_rows, :].astype(F32)
        )

    def bc_start(l):
        copies = []
        bc_t[l] = jnp.transpose(dact[:T, I:]).astype(BF16)
        for d, peer in enumerate(head_peers):
            rows = pl.ds(pl.multiple_of(peer_at[d] * Q2, Q2), Q2)
            copy = links.remote(bc_t.at[l, rows], bc_recv.at[l, d], peer)
            copy.start()
            copies.append(copy)
        return copies

    def bc_mid(l, copies):
        total = bc_t[l, pl.ds(pl.multiple_of(k * Q2, Q2), Q2), :].astype(F32)
        for d, copy in enumerate(copies):
            copy.wait_recv()
            total = total + bc_recv[l, d].astype(F32)
        bc_rows[l, :Q2, :] = total.astype(BF16)
        return collect(l, bc_rows.at[l], bc_rhs.at[c])

    def bc_block(j):
        rows = pl.ds(pl.multiple_of(j * DB, DB), DB)
        return dot_nt(bc_rhs[0], lt[1, 0, rows, :]) + dot_nt(bc_rhs[1], lt[1, 1, rows, :])

    def bc_copies(l):
        return [
            links.remote(bc_send.at[d], bc_land.at[d], peer, c == l)
            for d, peer in enumerate(seq_peers)
        ]

    def bc_out_start(ready, copies):
        ready()
        for d, copy in enumerate(copies):
            bc_send[d] = bc_block(lax.rem(s + d + 1, n_seq)).astype(BF16)
            copy.start()

    def bc_gather_copies(l):
        return [
            links.remote(bc_all.at[k], bc_all.at[k], peer, c == l) for peer in head_peers
        ]

    def bc_sum(copies, gathers):
        total = bc_block(s)
        for d, copy in enumerate(copies):
            copy.wait_recv()
            total = total + bc_land[d].astype(F32)
        bc_all[k] = total[:Q2]
        for h in range(heads):
            gw_dt[h] = total[Q2 + h : Q2 + h + 1]
        for copy in gathers:
            copy.start()

    def bc_finish(gathers):
        for copy in gathers:
            copy.wait_recv()
        whole = jnp.concatenate([bc_all[i] for i in range(n_head)], axis=0)
        gw_bc[...] = jnp.transpose(whole) if DB % LANES == 0 else whole

    def small_start(l):
        copy = links.remote(small.at[l], sm_o, other, c != l)
        start_if(c != l, copy)
        heads_to = [
            links.remote(sm_t, sm_h.at[d], peer, c == l) for d, peer in enumerate(head_peers)
        ]
        seqs_to = [
            links.remote(sm_u, sm_z.at[d], peer, c == l) for d, peer in enumerate(seq_peers)
        ]
        return copy, heads_to, seqs_to

    def small_heads(l, copies):
        copies[0].wait_recv()
        sm_t[...] = small[l] + sm_o[...]
        for copy in copies[1]:
            copy.start()

    def small_seqs(copies):
        sm_u[...] = sm_t[...]
        for d, copy in enumerate(copies[1]):
            copy.wait_recv()
            sm_u[0:1, :] += sm_h[d, 0:1, :]
            sm_u[1:6, I : I + 2 * N] += sm_h[d, 1:6, I : I + 2 * N]
        for copy in copies[2]:
            copy.start()

    def small_finish(copies):
        total = sm_u[...]
        for d, copy in enumerate(copies[2]):
            copy.wait_recv()
            total = total + sm_z[d]
        g_gain[...] = total[0:1]
        for r in range(5):
            g_conv_x[r] = total[1 + r : 2 + r, :I]
            g_conv_bc[r] = total[1 + r : 2 + r, I : I + 2 * N]
        g_out[...] = total[6:7, :I]
        g_head[0] = total[6:7, I : I + heads]
        g_head[1] = total[6:7, I + LANES : I + LANES + heads]
        g_head[2] = split_dot(total[:, :I], et[...])[7:8, :heads]

    def deliver(kind):
        copy = links.remote(end_send.at[kind], ends.at[c], other, c != kind)

        def put(q, rows):
            @pl.when(c == kind)
            def _():
                ends[c, :, pl.ds(q * RW, RW)] = rows.astype(F32)

            @pl.when(c != kind)
            def _():
                end_send[kind, :, pl.ds(q * RW, RW)] = rows.astype(F32)
                if q == parts_rs - 1:
                    copy.start()

        def finish():
            wait_if(c == kind, copy)

        return put, finish

    on0, on1 = pl.when(c == 0), pl.when(c == 1)
    end0, end1 = pl.when(is_end & (c == 0)), pl.when(is_end & (c == 1))
    first0, last0 = pl.when(is_first & (c == 0)), pl.when(is_last & (c == 0))
    first1, last1 = pl.when(is_first & (c == 1)), pl.when(is_last & (c == 1))
    far = (far_copies(0, (1,), (1, 2)), far_copies(1, (0, 1), (0, 1, 2)))
    got = {}

    def up1(l, piece):
        z_forward(l, piece, True, True)

    def up2(l, piece):
        z_forward(l, piece, True, False)

    def down1(l, piece, part=None):
        z_forward(l, piece, False, True, part)

    def down2(l, piece):
        z_forward(l, piece, False, False)

    def nothing():
        pass

    run_e1, ready_e1 = collect_transposed(1, 0, eb.at[1])
    run_n0, ready_n0 = collect_transposed(0, 1, nm)
    run_n1, ready_n1 = collect_transposed(1, 1, nm)

    def send_e1():
        @on1
        def _():
            ready_e1()
            far[1][0][0].start()

    def send_n0():
        @on0
        def _():
            ready_n0()
            far[0][0][1].start()

    def gap():
        run_n0()

        @pl.when(is_first)
        def _():
            send_n0()

        load_e.wait()
        run_e1()

        @pl.when(is_last)
        def _():
            send_e1()

    def gap_rs():
        @pl.when(is_last)
        def _():
            send_n0()

        @pl.when(inside)
        def _():
            @on0
            def _():
                ready_n0()

        @pl.when(s < n_seq - 1)
        def _():
            @on1
            def _():
                ready_e1()

    put, finish_gather = gather_rows(hb.at[1])
    finish_q = forward(0, nothing, gap)
    rs_part = project_branch(0)
    ready_u0 = scale_branch(0, finish_q)
    gap_rs()
    finish_branch(0, rs_part, put)
    finish_gather()

    def gap():
        @on1
        def _():
            ready_n1()

        @end1
        def _():
            far[1][0][1].start()

    put, finish_out = deliver(1)
    finish_q1 = forward(1, run_n1, gap)

    def gap_dot():
        got["rs1"] = project_branch(1)
        ready_u1 = scale_branch(1, finish_q1)

        @on1
        def _():
            ready_u1()

        @on1
        def _():
            z_first(0)

    def gap_chain(ready):
        @on1
        def _():
            ready()

        @first1
        def _():
            far[1][1][1].start()

    def gap_join():
        @last1
        def _():
            far[1][1][0].start()
            far[1][1][1].start()

        finish_branch(1, got["rs1"], put)

        @on1
        def _():
            up1(1, 0)

    def gap_rs(ready):
        got["bc1"] = bc_start(1)

        @on1
        def _():
            ready()

        @end1
        def _():
            far[1][1][2].start()

        @on1
        def _():
            up1(1, 1)
            down1(1, 0)

    rows = backward(1, gap_dot, gap_chain, nothing, gap_join, gap_rs)
    put, finish_gather = gather_rows(eb.at[0])
    for q in range(parts_rs):
        put(q, rows[:, q * RW : (q + 1) * RW].astype(BF16))
    small1 = small_start(1)
    ready_bc1 = bc_mid(1, got["bc1"])
    bc_to1, bc_g1 = bc_copies(1), bc_gather_copies(1)

    @on1
    def _():
        down1(1, 1)
        up1(1, 2)
        up2(1, 0)
        down1(1, 2, 0)

    finish_gather()

    run_e0, ready_e0 = collect_transposed(0, 0, eb.at[0])

    def gap_dot():
        run_e0()

        @on1
        def _():
            down2(1, 0)
            small_heads(1, small1)

        @on0
        def _():
            ready_u0()
            ready_e0()
            z_first(0)
            z_last(0, 0)

    def gap_chain(ready):
        @on1
        def _():
            up2(1, 1)
            small_seqs(small1)

        @on0
        def _():
            z_last(0, 1)
            ready()

        @first0
        def _():
            far[0][1][1].start()

    def gap_after():
        @on1
        def _():
            down1(1, 2, 1)

    def gap_join():
        @on0
        def _():
            z_last(0, 2)

        @last0
        def _():
            far[0][1][1].start()

        @on0
        def _():
            up1(0, 0)

    def gap_rs(ready):
        got["bc0"] = bc_start(0)

        @on0
        def _():
            ready()

        @end0
        def _():
            far[0][1][2].start()

        @on0
        def _():
            up1(0, 1)

        @on1
        def _():
            down2(1, 1)
            up2(1, 2)
            bc_out_start(ready_bc1, bc_to1)
            z_final(1, 0)

    rows = backward(0, gap_dot, gap_chain, gap_after, gap_join, gap_rs)
    put, finish_in = deliver(0)
    for q in range(parts_rs):
        put(q, rows[:, q * RW : (q + 1) * RW])
    small0 = small_start(0)
    ready_bc0 = bc_mid(0, got["bc0"])
    bc_to0, bc_g0 = bc_copies(0), bc_gather_copies(0)

    @on1
    def _():
        small_finish(small1)
        bc_sum(bc_to1, bc_g1)
        z_final(1, 1)
        down2(1, 2)
        bc_finish(bc_g1)
        z_final(1, 2)

    @on0
    def _():
        bc_out_start(ready_bc0, bc_to0)
        down1(0, 0)
        up1(0, 2)
        small_heads(0, small0)
        up2(0, 0)
        down1(0, 1)
        down2(0, 0)
        up2(0, 1)
        down1(0, 2)
        z_final(0, 0)
        small_seqs(small0)
        down2(0, 1)
        bc_sum(bc_to0, bc_g0)
        z_final(0, 1)
        up2(0, 2)
        down2(0, 2)
        small_finish(small0)
        bc_finish(bc_g0)
        z_final(0, 2)

    finish_out()
    finish_in()
    save = links.local(ends, ends_out)
    save.start()
    save.wait()

    @pl.when(inside)
    def _():
        for i in range(n_seq - 1):
            z_sent(1, i)
            z_sent(2, i)

    @pl.when(is_first | (is_last & (c == 0)))
    def _():
        for i in range(n_seq - 1):
            z_sent(0, i)

    for l, copy in lt_sends:

        @pl.when(c != l)
        def _():
            copy.wait_send()

    for slot in range(2):
        for copy in rs_copies[slot]:
            copy.wait_send()
    links.drain()


def run_layers(tokens, cotangent, w_xz, w_bc, w_dt, w_out, in_gain, in_conv_x, in_conv_bc, in_head, in_out):
    n_seq, n_head = lax.axis_size("seq"), lax.axis_size("head")
    _, T, D = tokens.shape
    I = w_xz.shape[2]
    N = w_bc.shape[1] // 2
    heads = in_head.shape[2]
    XB = I + 2 * N
    G = 2 * I + 2 * N + LANES
    Q = T // n_head
    DB = D // n_seq
    BR = 2 * N // n_head + (heads + 15) // 16 * 16
    sems = 160 + 4 * (n_seq + n_head)
    S = jax.ShapeDtypeStruct
    V = pltpu.VMEM
    dma = pltpu.SemaphoreType.DMA
    vm = pl.BlockSpec(memory_space=pltpu.VMEM)
    hbm = pl.BlockSpec(memory_space=pl.ANY)
    scratch = [
        V((2, 2, D, I), BF16), V((2, D, 2 * N), BF16), V((2, LANES, D), BF16), V((2, I, D), BF16),
        V((2, 8, D), F32), V((2, T, D), BF16), V((2, T, D), BF16), V((T, D), BF16),
        V((2, T + EDGE, XB), BF16), V((2, T, I), F32), V((2, T, XB), F32),
        V((T, I), F32), V((T, I), F32), V((2, T, I), F32),
        V((2, T, LANES), F32), V((2, T, LANES), F32), V((2, T, LANES), F32), V((2, LANES, T), F32),
        V((2, N, T), BF16), V((2, N, T), BF16), V((2, T, N), BF16), V((2, T, N), BF16),
        V((2, N, I), F32), V((2, N, I), F32), V((T, I), BF16), V((T, I), BF16),
        V((2, T, LANES), F32),
        V((T, I), F32), V((T, I), F32), V((T, I), BF16), V((T, I), BF16),
        V((N, I), F32), V((N, I), F32), V((T + EDGE, XB), F32),
        V((T, T), F32), V((2, T, G), BF16), V((2, T, I), BF16), V((2, 8, D), F32),
        V((4, 8, T), F32), V((4, n_head - 1, 8, T), F32),
        V((2, T, D), BF16), V((2, n_head - 1, Q, D), BF16),
        V((4, 6, N, I // 6), BF16), V((4, 6, N, I // 6), BF16),
        V((2, EDGE, XB), BF16), V((2, EDGE, XB), BF16),
        V((2, Q, D), F32), V((2, Q, D), F32), V((I, LANES), BF16), V((T, T), F32),
        V((2, 2, D, T), BF16), V((D, T), BF16), V((3, 2, T, I), BF16),
        V((2, n_seq - 1, DB, I), BF16), V((2, DB, I), BF16), V((DB, I), F32), V((I, DB), F32),
        V((2, DB, T), BF16), V((2, T, I), BF16),
        V((2, n_head - 1, 2 * N // n_head, T), BF16), V((2, 2 * N, T), BF16), V((2, BR, T), BF16),
        V((2, BR, T), BF16), V((n_seq - 1, BR, DB), BF16), V((n_seq - 1, BR, DB), BF16),
        V((n_head, 2 * N // n_head, DB), F32),
        V((8, D), F32), V((8, D), F32), V((n_head - 1, 8, D), F32), V((8, D), F32),
        V((n_seq - 1, 8, D), F32),
        dma((24,)), dma((sems,)), dma((sems,)),
        dma((3 * (n_seq - 1),)), dma((3 * (n_seq + 1),)), dma((4,)),
    ]
    dims = (n_seq, n_head, T, D, I, N, heads)
    return pl.pallas_call(
        functools.partial(layer_kernel, dims),
        out_shape=(
            S((2, Q, D), F32), S((I, DB) if DB % LANES == 0 else (DB, I), F32), S((2, DB, I), F32),
            S((DB, 2 * N) if DB % LANES == 0 else (2 * N, DB), F32), S((heads, 1, DB), F32),
            S((1, D), F32), S((5, 1, I), F32), S((5, 1, 2 * N), F32), S((3, 1, heads), F32),
            S((1, I), F32),
            S((3, n_seq + 1, DB, I), BF16), S((2, 2, D, T), BF16), S((3, 2, T, I), BF16),
        ),
        in_specs=[hbm] * 6 + [vm] * 5,
        out_specs=(hbm, hbm, hbm, vm, vm, vm, vm, vm, vm, vm, hbm, hbm, hbm),
        scratch_shapes=scratch,
        compiler_params=pltpu.CompilerParams(
            collective_id=0, has_side_effects=True, vmem_limit_bytes=63 * 2**20
        ),
        name="layers",
    )(
        tokens, cotangent, w_xz, w_bc, w_dt, w_out, in_gain, in_conv_x, in_conv_bc, in_head, in_out
    )[:10]


def body(
    tokens, cotangent, norm_gain, w_xz, w_bc, w_dt, conv_x, conv_bc, head_params, out_gain, w_out
):
    heads = w_dt.shape[2]
    dt_rows = jnp.pad(w_dt[0].T, ((0, LANES - heads), (0, 0)))
    ends, gw_out, gw_xz, gw_bc, gw_dt, g_gain, g_conv_x, g_conv_bc, g_head, g_out = run_layers(
        tokens,
        cotangent,
        jnp.swapaxes(w_xz[0], 0, 1),
        w_bc[0],
        dt_rows,
        w_out[0],
        norm_gain,
        jnp.swapaxes(conv_x, 0, 1),
        jnp.swapaxes(conv_bc, 0, 1),
        jnp.swapaxes(head_params, 0, 1),
        out_gain,
    )
    if gw_bc.shape[1] != w_bc.shape[2]:
        gw_bc = gw_bc.T
        gw_out = gw_out.T
    return (
        ends[None],
        g_gain,
        jnp.swapaxes(gw_xz, 0, 1)[None],
        gw_bc[None],
        jnp.transpose(gw_dt, (1, 2, 0)),
        jnp.swapaxes(g_conv_x, 0, 1),
        jnp.swapaxes(g_conv_bc, 0, 1),
        jnp.swapaxes(g_head, 0, 1),
        g_out,
        gw_out[None],
    )


def solution(mesh):
    placed = (
        P(None, "seq", None),
        P(None, "seq", None),
        P("section", None),
        P("section", None, None, "head"),
        P("section", None, None),
        P("section", None, "head"),
        P("section", None, "head"),
        P("section", None, None),
        P("section", None, "head"),
        P("section", "head"),
        P("section", "head", None),
    )
    return jax.shard_map(
        body,
        mesh=mesh,
        in_specs=placed,
        out_specs=(
            P("section", None, ("seq", "head"), None),
            P("section", None),
            P("section", "seq", None, "head"),
            P("section", "seq", None),
            P("section", "seq", "head"),
            P("section", None, "head"),
            P("section", None, None),
            P("section", None, "head"),
            P("section", "head"),
            P("section", "head", "seq"),
        ),
        check_vma=False,
    )
```

```python
import functools

import jax
import jax.numpy as jnp
from jax import lax
from jax.experimental import pallas as pl
from jax.experimental.pallas import tpu as pltpu
from jax.sharding import PartitionSpec as P

EPSILON = 1e-05
MESH = pl.DeviceIdType.MESH
LANES = 128
EDGE = 16
F32 = jnp.float32
BF16 = jnp.bfloat16


def dot(a, b):
    return lax.dot_general(a, b, (((1,), (0,)), ((), ())), preferred_element_type=F32)


def dot_nt(a, b):
    return lax.dot_general(a, b, (((1,), (1,)), ((), ())), preferred_element_type=F32)


def dot_tn(a, b):
    return lax.dot_general(a, b, (((0,), (0,)), ((), ())), preferred_element_type=F32)


def exact_dot(a, b):
    return lax.dot_general(
        a, b, (((1,), (0,)), ((), ())), precision=lax.Precision.HIGHEST, preferred_element_type=F32
    )


def split_dot(a, b):
    high = a.astype(BF16)
    return dot(high, b) + dot((a - high.astype(F32)).astype(BF16), b)


class Links:
    def __init__(self, local_sem, send_sem, recv_sem):
        self.local_sem, self.send_sem, self.recv_sem = local_sem, send_sem, recv_sem
        self.local_count = 0
        self.count = 0
        self.pending = []

    def local(self, src, dst):
        index = self.local_count
        assert index < self.local_sem.shape[0]
        self.local_count += 1
        return pltpu.make_async_copy(src, dst, self.local_sem.at[index])

    def remote(self, src, dst, peer, when=None):
        index = self.count
        assert index < self.send_sem.shape[0]
        self.count += 1
        copy = pltpu.make_async_remote_copy(
            src_ref=src,
            dst_ref=dst,
            send_sem=self.send_sem.at[index],
            recv_sem=self.recv_sem.at[index],
            device_id=peer,
            device_id_type=MESH,
        )
        self.pending.append((copy, when))
        return copy

    def drain(self):
        for copy, when in self.pending:
            if when is None:
                copy.wait_send()
            else:

                @pl.when(when)
                def _():
                    copy.wait_send()


def wait_if(condition, copy):
    @pl.when(condition)
    def _():
        copy.wait_recv()


def start_if(condition, copy):
    @pl.when(condition)
    def _():
        copy.start()


def lanes(i, width=LANES):
    if isinstance(i, int):
        return pl.ds(i * width, width)
    return pl.ds(pl.multiple_of(i * width, width), width)


def layer_kernel(dims, *refs):
    (n_seq, n_head, T, D, I, N, heads) = dims
    (
        tokens, cotangent, w_xz, w_bc, w_dt, w_out, in_gain, in_conv_x, in_conv_bc, in_head, in_out,
        ends_out, gw_out, gw_xz, gw_bc, gw_dt, g_gain, g_conv_x, g_conv_bc, g_head, g_out, z_land, far_lt, far_rhs,
        wxz, wbc, wdt, wo, prm, hb, eb, nm, xin, z, act, dte, cume, y0,
        sgdt, dtv, cum, cumT, CT, BT, Bb, Cb, st_loc, s_ent, xtb, xtl, qb,
        du, dy, dyb, dye, dst_loc, gin, dact, dcbt, gp, us, small,
        row_send, row_recv, rs_send, rs_recv, ch_send, ch_recv, edge_send, edge_recv,
        end_send, ends, et, tri,
        lt, lt_send, rhs, z_send, z_in, z_acc, z_turn, far_l, far_r, bc_recv, bc_t, bc_rows, bc_rhs, bc_send, bc_land, bc_all,
        sm_o, sm_t, sm_h, sm_u, sm_z,
        local_sem, send_sem, recv_sem, zs_sem, zr_sem, zi_sem,
    ) = refs
    c = lax.axis_index("section")
    s = lax.axis_index("seq")
    k = lax.axis_index("head")
    links = Links(local_sem, send_sem, recv_sem)
    Q = T // n_head
    XB = I + 2 * N
    DB = D // n_seq
    pairs = I // LANES
    head_size = I // heads
    is_first = s == 0
    is_last = s == n_seq - 1
    has_prev = s > 0
    has_next = s < n_seq - 1
    other = {"section": 1 - c}
    prev_dev = {"seq": jnp.maximum(s - 1, 0)}
    next_dev = {"seq": jnp.minimum(s + 1, n_seq - 1)}
    if n_head == 4:
        peer_at = [3 - k, k + 1 - 2 * lax.rem(k, 2), lax.rem(k + 2, 4)]
    else:
        peer_at = [lax.rem(k + d, n_head) for d in range(1, n_head)]
    head_peers = [{"head": at} for at in peer_at]
    seq_peers = [{"seq": lax.rem(s + d, n_seq)} for d in range(1, n_seq)]
    own_rows = pl.ds(pl.multiple_of(k * Q, Q), Q)
    chunks = 6
    CW = I // chunks
    ntile = 256
    inner_total = I * n_head
    Q2 = 2 * N // n_head
    rs_copies = {}
    parts_rs = 3
    RW = D // parts_rs

    dt_pad = w_dt.shape[0]
    wdt[:, dt_pad:, :] = jnp.zeros((2, LANES - dt_pad, D), BF16)

    barrier = pltpu.get_barrier_semaphore()
    for peer in [other] + head_peers + seq_peers:
        pl.semaphore_signal(barrier, inc=1, device_id=peer, device_id_type=MESH)

    load_h = links.local(tokens.at[c], hb.at[0])
    load_e = links.local(cotangent.at[c], eb.at[1])
    load_h.start()
    parts = (
        (w_xz.at[0], wxz.at[c, 0]),
        (w_bc, wbc.at[c]),
        (w_dt, wdt.at[c, pl.ds(0, dt_pad)]),
        (w_xz.at[1], wxz.at[c, 1]),
        (w_out, wo.at[c]),
    )
    mine = [links.local(src, dst) for src, dst in parts]
    for copy in mine:
        copy.start()
    load_e.start()
    pl.semaphore_wait(barrier, n_head + n_seq - 1)
    low_row = lax.broadcasted_iota(jnp.int32, (1, LANES), 1) < head_size
    prm[c] = jnp.zeros((8, D), F32)
    prm[c, 0:1, :] = in_gain[...]
    for r in range(5):
        prm[c, 1 + r : 2 + r, :I] = in_conv_x[r]
        prm[c, 1 + r : 2 + r, I : I + 2 * N] = in_conv_bc[r]
    prm[c, 6:7, :I] = in_out[...]
    prm[c, 6:7, I : I + heads] = in_head[0]
    prm[c, 6:7, I + LANES : I + LANES + heads] = in_head[1]
    skips = in_head[2]
    for p in range(pairs):
        prm[c, 7:8, lanes(p)] = jnp.where(
            low_row, skips[:, 2 * p : 2 * p + 1], skips[:, 2 * p + 1 : 2 * p + 2]
        )
    theirs = [links.remote(prm.at[c], prm.at[c], other)]
    theirs += [links.remote(src, dst, other) for src, dst in parts]
    for copy in theirs:
        copy.start()

    def weights_ready(layer, which):
        @pl.when(c == layer)
        def _():
            for i in which:
                if i:
                    mine[i - 1].wait()

        @pl.when(c != layer)
        def _():
            for i in which:
                theirs[i].wait_recv()

    row_i = lax.broadcasted_iota(jnp.int32, (T, T), 0)
    col_i = lax.broadcasted_iota(jnp.int32, (T, T), 1)
    tri[...] = jnp.where(row_i >= col_i, 1.0, 0.0)
    er = lax.broadcasted_iota(jnp.int32, (I, LANES), 0)
    ec = lax.broadcasted_iota(jnp.int32, (I, LANES), 1)
    et[...] = jnp.where(
        (er >= ec * head_size) & (er < (ec + 1) * head_size), 1.0, 0.0
    ).astype(BF16)
    small[...] = jnp.zeros_like(small)
    load_h.wait()

    def exchange_rows(total_cols, slot):
        summed = jnp.sum(total_cols, axis=1, keepdims=True)
        as_row = jnp.transpose(jnp.broadcast_to(summed, (T, LANES)))[:8]
        row_send[slot] = as_row
        copies = []
        for d, peer in enumerate(head_peers):
            copy = links.remote(row_send.at[slot], row_recv.at[slot, d], peer)
            copy.start()
            copies.append(copy)

        def finish():
            total = row_send[slot]
            for d, copy in enumerate(copies):
                copy.wait_recv()
                total = total + row_recv[slot, d]
            wide = jnp.broadcast_to(total[:1], (LANES, T))
            return jnp.transpose(wide)

        return finish

    def reduce_rows(slot):
        copies = []
        for q in range(parts_rs):
            at = pl.ds(q * RW, RW)
            row = []
            for d, peer in enumerate(head_peers):
                rows = pl.ds(pl.multiple_of(peer_at[d] * Q, Q), Q)
                row.append(
                    links.remote(rs_send.at[slot, rows, at], rs_recv.at[slot, d, :, at], peer)
                )
                links.pending.pop()
            copies.append(row)
        rs_copies[slot] = [copy for row in copies for copy in row]

        def send(q):
            for copy in copies[q]:
                copy.start()

        def part(q):
            at = pl.ds(q * RW, RW)
            total = rs_send[slot, own_rows, at].astype(F32)
            for d, copy in enumerate(copies[q]):
                copy.wait_recv()
                total = total + rs_recv[slot, d, :, at].astype(F32)
            return total

        return send, part

    def gather_rows(target):
        copies = []
        for q in range(parts_rs):
            at = target.at[own_rows, pl.ds(q * RW, RW)]
            copies.append([links.remote(at, at, peer) for peer in head_peers])

        def send(q, rows):
            target[own_rows, pl.ds(q * RW, RW)] = rows
            for copy in copies[q]:
                copy.start()

        def finish():
            for row in copies:
                for copy in row:
                    copy.wait_recv()

        return send, finish

    def chain(slot, forward, local, dec_row, into):
        starts, goes_on = (is_first, has_next) if forward else (is_last, has_prev)
        receives = has_prev if forward else has_next
        peer = next_dev if forward else prev_dev
        copies = []
        for j in range(chunks):
            copies.append(
                links.remote(ch_send.at[slot, j], ch_recv.at[slot, j], peer, goes_on)
            )

        def begin():
            @pl.when(starts)
            def _():
                for j in range(chunks):
                    ch_send[slot, j] = local[:, lanes(j, CW)].astype(BF16)
                    start_if(goes_on, copies[j])

        def finish():
            @pl.when(starts)
            def _():
                into[...] = jnp.zeros_like(into)

            @pl.when(receives)
            def _():
                for j in range(chunks):
                    copies[j].wait_recv()
                    at = lanes(j, CW)
                    arrived = ch_recv[slot, j].astype(F32)
                    into[:, at] = arrived

                    @pl.when(goes_on)
                    def _():
                        ch_send[slot, j] = (
                            arrived * dec_row[:, j * CW : (j + 1) * CW] + local[:, at]
                        ).astype(BF16)
                        copies[j].start()

        return begin, finish

    def collect(l, src, dst):
        near = links.local(src, dst)
        far = links.remote(src, dst, other, c != l)

        @pl.when(c == l)
        def _():
            near.start()

        @pl.when(c != l)
        def _():
            far.start()

        def ready():
            near.wait()
            far.wait_recv()

        return ready

    lt_sends = []

    def collect_transposed(l, kind, src):
        far = links.remote(lt_send, lt.at[kind, c], other, c != l)
        links.pending.pop()
        before = [copy for layer, copy in lt_sends if layer == l]
        lt_sends[:] = [item for item in lt_sends if item[0] != l] + [(l, far)]

        def run():
            @pl.when(c == l)
            def _():
                def turn(t, _):
                    lt[kind, c, lanes(t), :] = jnp.transpose(src[:, lanes(t)].astype(F32)).astype(BF16)
                    return 0

                lax.fori_loop(0, D // LANES, turn, 0)

            @pl.when(c != l)
            def _():
                for copy in before:
                    copy.wait_send()

                def turn(t, _):
                    lt_send[lanes(t), :] = jnp.transpose(src[:, lanes(t)].astype(F32)).astype(BF16)
                    return 0

                lax.fori_loop(0, D // LANES, turn, 0)
                far.start()

        def ready():
            far.wait_recv()

        return run, ready

    low_half = s < n_seq // 2
    is_end = is_first | is_last
    inside = has_prev & has_next
    inward = {"seq": jnp.where(is_first, 1, jnp.where(is_last, n_seq - 2, s))}

    def far_copies(l, kinds, pieces):
        def one(a, there, i):
            ends = is_end if far_up(l, i) else is_last
            return links.remote(a.at[i], there.at[i], inward, ends & (c == l))

        return (
            {i: one(lt, far_lt, i) for i in kinds},
            {i: one(rhs, far_rhs, i) for i in pieces},
        )

    def far_up(l, piece):
        return piece > 0

    def far_down(l, piece):
        return l == 1 or piece > 0

    def z_copy(piece, j, up):
        if up:
            slot, peer = j, next_dev
        else:
            slot, peer = jnp.where(j == s - 1, n_seq, j), prev_dev
        index = jnp.where(j < s, j, j - 1)
        return pltpu.make_async_remote_copy(
            src_ref=z_send.at[piece % 2, index],
            dst_ref=z_land.at[piece, slot],
            send_sem=zs_sem.at[piece * (n_seq - 1) + index],
            recv_sem=zr_sem.at[piece * (n_seq + 1) + slot],
            device_id=peer,
            device_id_type=MESH,
        )

    def z_arrived(piece, slot, into):
        pltpu.make_async_remote_copy(
            src_ref=z_send.at[piece % 2, 0],
            dst_ref=z_land.at[piece, slot],
            send_sem=zs_sem.at[piece * (n_seq - 1)],
            recv_sem=zr_sem.at[piece * (n_seq + 1) + slot],
            device_id=prev_dev,
            device_id_type=MESH,
        ).wait_recv()
        return pltpu.make_async_copy(z_land.at[piece, slot], z_in.at[into], zi_sem.at[into])

    def z_block(piece, j, store):
        kind = 0 if piece == 0 else 1
        rows = pl.ds(pl.multiple_of(j * DB, DB), DB)

        def tile(t, _):
            at = lanes(t, ntile)
            store(
                at,
                dot(lt[kind, 0, rows, :], rhs[piece, 0, :, at])
                + dot(lt[kind, 1, rows, :], rhs[piece, 1, :, at]),
            )
            return 0

        lax.fori_loop(0, I // ntile, tile, 0)

    def hold(at, value):
        z_acc[:, at] = value

    def far_load(piece):
        return pltpu.make_async_copy(far_rhs.at[piece], far_r, zi_sem.at[3])

    def far_block(piece, j, store, load):
        kind = 0 if piece == 0 else 1
        rows = pl.ds(pl.multiple_of(j * DB, DB), DB)
        left = pltpu.make_async_copy(far_lt.at[kind, :, rows], far_l, zi_sem.at[2])
        left.start()
        z_block(piece, j, hold)
        if load is not None:
            load.wait()
        left.wait()

        def tile(t, _):
            at = lanes(t, ntile)
            store(
                at,
                z_acc[:, at] + dot(far_l[0], far_r[0, :, at]) + dot(far_l[1], far_r[1, :, at]),
            )
            return 0

        lax.fori_loop(0, I // ntile, tile, 0)

    def z_one(piece, j, up):
        index = jnp.where(j < s, j, j - 1)
        def store(at, value):
            z_send[piece % 2, index, :, at] = value.astype(BF16)

        z_block(piece, j, store)
        z_copy(piece, j, up).start()
        return 0

    def z_first(piece):
        @pl.when(is_first)
        def _():
            lax.fori_loop(0, n_seq - 1, lambda i, _: z_one(piece, n_seq - 1 - i, True), 0)

    def z_last(piece, part):
        low, high = (n_seq - 1) * part // 3, (n_seq - 1) * (part + 1) // 3

        @pl.when(is_last)
        def _():
            lax.fori_loop(low, high, lambda i, _: z_one(piece, i, False), 0)

    def z_sent(piece, index):
        pltpu.make_async_remote_copy(
            src_ref=z_send.at[piece % 2, index],
            dst_ref=z_land.at[piece, 0],
            send_sem=zs_sem.at[piece * (n_seq - 1) + index],
            recv_sem=zr_sem.at[piece * (n_seq + 1)],
            device_id=next_dev,
            device_id_type=MESH,
        ).wait_send()

    def z_forward(l, piece, up, first, part=None):
        mine = inside & (low_half if up == first else jnp.logical_not(low_half))
        count = n_seq - 1 - s if up else s
        begin, end = 0, count
        if part is not None:
            begin, end = (0, count // 2) if part == 0 else (count // 2, count)

        def one(i, _, far):
            j = n_seq - 1 - i if up else i
            index = jnp.where(j < s, j, j - 1)
            if piece == 2:
                z_sent(0, index)
            if far:

                def store(at, value):
                    z_send[piece % 2, index, :, at] = value.astype(BF16)

                far_block(piece, j, store, None)
            else:
                load = z_arrived(piece, j, 0)
                load.start()
                z_block(piece, j, hold)
                load.wait()
                z_send[piece % 2, index] = (z_acc[...] + z_in[0].astype(F32)).astype(BF16)
            z_copy(piece, j, up).start()
            return 0

        use_far = far_up(l, piece) if up else far_down(l, piece)
        near = s == 1 if up else s == n_seq - 2
        if first and use_far:

            @pl.when(mine & near)
            def _():
                if not part:
                    if piece < 2:
                        far[l][0][piece].wait_recv()
                    far[l][1][piece].wait_recv()
                load = far_load(piece)
                load.start()
                load.wait()
                lax.fori_loop(begin, end, functools.partial(one, far=True), 0)

            if n_seq > 4:

                @pl.when(mine & jnp.logical_not(near))
                def _():
                    lax.fori_loop(begin, end, functools.partial(one, far=False), 0)

        else:

            @pl.when(mine)
            def _():
                lax.fori_loop(begin, end, functools.partial(one, far=False), 0)

    def z_final(l, piece):
        by_low, by_high = far_up(l, piece), far_down(l, piece)
        from_low = s >= (2 if by_low else 1)
        from_high = s < n_seq - (2 if by_high else 1)
        near = ((s == 1) & by_low) | ((s == n_seq - 2) & by_high)

        @pl.when(from_low)
        def _():
            z_arrived(piece, s, 0).start()

        @pl.when(from_high)
        def _():
            z_arrived(piece, n_seq, 1).start()

        if by_low or by_high:

            @pl.when(near)
            def _():
                load = far_load(piece)
                load.start()
                far_block(piece, s, hold, load)

            @pl.when(jnp.logical_not(near))
            def _():
                z_block(piece, s, hold)

        else:
            z_block(piece, s, hold)

        @pl.when(from_low)
        def _():
            pltpu.make_async_copy(z_land.at[piece, s], z_in.at[0], zi_sem.at[0]).wait()
            z_acc[...] += z_in[0].astype(F32)

        @pl.when(from_high)
        def _():
            pltpu.make_async_copy(z_land.at[piece, n_seq], z_in.at[1], zi_sem.at[1]).wait()
            z_acc[...] += z_in[1].astype(F32)

        if piece == 0 and DB % LANES == 0:
            for t in range(I // ntile):
                at = lanes(t, ntile)
                z_turn[at, :] = jnp.transpose(z_acc[:, at])
        z_save(piece).start()
        if piece == 1 or (piece == 0 and DB % LANES):
            z_saved(piece)

    def z_save(piece):
        if piece == 0 and DB % LANES == 0:
            return pltpu.make_async_copy(z_turn, gw_out, zi_sem.at[4])
        target = gw_out if piece == 0 else gw_xz.at[2 - piece]
        return pltpu.make_async_copy(z_acc, target, zi_sem.at[5])

    def z_saved(piece):
        z_save(piece).wait()

    lane_low = lax.broadcasted_iota(jnp.int32, (T, LANES), 1) < head_size
    later = row_i >= col_i
    earlier = col_i >= row_i

    def spread_heads(l):
        for p in range(pairs):
            at = lanes(p)
            dte[:, at] = jnp.where(
                lane_low, dtv[l, :, 2 * p : 2 * p + 1], dtv[l, :, 2 * p + 1 : 2 * p + 2]
            )
            cume[:, at] = jnp.where(
                lane_low, cum[l, :, 2 * p : 2 * p + 1], cum[l, :, 2 * p + 1 : 2 * p + 2]
            )

    def steps(l):
        def one(p, _):
            at = lanes(p)
            acc = cume[:, at]
            stepped = dte[:, at] * act[l, :, at]
            xtb[:, at] = stepped.astype(BF16)
            xtl[:, at] = (stepped * jnp.exp(acc[T - 1 : T] - acc)).astype(BF16)
            return 0

        lax.fori_loop(0, pairs, one, 0)

    def conv_sum(l, at, v):
        total = prm[l, 5:6, at] + prm[l, 4:5, at] * v[EDGE:]
        moved = []
        for shift in range(1, 4):
            moved.append(pltpu.roll(v, shift, 0)[EDGE:])
            total = total + prm[l, 4 - shift : 5 - shift, at] * moved[-1]
        return total, [v[EDGE:]] + moved

    def forward(l, gap_norm, gap_chain):
        weights_ready(l, [0])
        gain = prm[l, 0:1, :]

        def norm_rows(i, _):
            rows = pl.ds(pl.multiple_of(i * 32, 32), 32)
            v = hb[l, rows, :].astype(F32)
            rstd = lax.rsqrt(jnp.mean(v * v, axis=1, keepdims=True) + EPSILON)
            nm[rows, :] = (v * rstd * gain).astype(BF16)
            return 0

        lax.fori_loop(0, T // 32, norm_rows, 0)

        gap_norm()
        weights_ready(l, [1, 2, 3])

        def project_x(j, _):
            xin[l, EDGE:, lanes(j, ntile)] = dot(
                nm[...], wxz[l, 0, :, lanes(j, ntile)]
            ).astype(BF16)
            return 0

        lax.fori_loop(0, I // ntile, project_x, 0)
        xin[l, EDGE:, I:] = dot(nm[...], wbc[l]).astype(BF16)

        edge = links.remote(
            xin.at[l, pl.ds(T, EDGE)], xin.at[l, pl.ds(0, EDGE)], next_dev, has_next
        )
        start_if(has_next, edge)

        dt_raw = dot_nt(nm[...], wdt[l])
        hp0 = prm[l, 6:7, I : I + LANES]
        hp1 = prm[l, 6:7, I + LANES : I + 2 * LANES]
        pre_dt = dt_raw + hp0
        sgdt[l] = lax.logistic(pre_dt)
        step = jnp.maximum(pre_dt, 0.0) + jnp.log1p(jnp.exp(-jnp.abs(pre_dt)))
        dtv[l] = step
        cum[l] = exact_dot(tri[...], -jnp.exp(hp1) * step)
        cumT[l] = jnp.transpose(cum[l])

        weights_ready(l, [4])

        def project_z(j, _):
            z[l, :, lanes(j, ntile)] = dot(nm[...], wxz[l, 1, :, lanes(j, ntile)])
            return 0

        lax.fori_loop(0, I // ntile, project_z, 0)

        @pl.when(is_first)
        def _():
            xin[l, :EDGE, :] = jnp.zeros((EDGE, XB), BF16)

        wait_if(has_prev, edge)

        def conv(j, _):
            at = lanes(j)
            total, _ = conv_sum(l, at, xin[l, :, at].astype(F32))
            act[l, :, at] = total * lax.logistic(total)
            return 0

        lax.fori_loop(0, XB // LANES, conv, 0)

        mat_b = act[l, :, I : I + N]
        mat_c = act[l, :, I + N :]
        Bb[l] = mat_b.astype(BF16)
        Cb[l] = mat_c.astype(BF16)
        BT[l] = jnp.transpose(mat_b).astype(BF16)
        CT[l] = jnp.transpose(mat_c).astype(BF16)
        spread_heads(l)
        steps(l)

        def local_state(j, _):
            st_loc[l, :, lanes(j, ntile)] = dot(BT[l], xtl[:, lanes(j, ntile)])
            return 0

        lax.fori_loop(0, I // ntile, local_state, 0)
        begin, finish_chain = chain(
            l, True, st_loc.at[l], jnp.exp(cume[T - 1 : T, :]), s_ent.at[l]
        )
        begin()

        cb = dot_nt(Cb[l], Bb[l])

        def intra(p, _):
            at = lanes(p)
            wide = cume[:, at]
            values = xtb[:, at]
            total = jnp.zeros((T, LANES), F32)
            for half in range(2):
                column = wide[:, half * head_size : half * head_size + 1]
                row = cumT[l, pl.ds(2 * p + half, 1), :]
                decay = jnp.where(later, jnp.exp(jnp.minimum(column - row, 0.0)), 0.0)
                mix = (cb * decay).astype(BF16)
                kept = jnp.where(lane_low == (half == 0), values, jnp.zeros_like(values))
                total = total + dot(mix, kept)
            y0[l, :, at] = total
            return 0

        lax.fori_loop(0, pairs, intra, 0)
        gap_chain()
        finish_chain()

        def gate(p, ssq):
            at = lanes(p)
            carried = dot(Cb[l], s_ent[l, :, at].astype(BF16))
            y = y0[l, :, at] + jnp.exp(cume[:, at]) * carried
            y0[l, :, at] = y
            full = y + prm[l, 7:8, at] * act[l, :, at]
            gate_in = z[l, :, at]
            value = full * (gate_in * lax.logistic(gate_in))
            dye[:, at] = (value * prm[l, 6:7, at]).astype(BF16)
            return ssq + value * value

        ssq = lax.fori_loop(0, pairs, gate, jnp.zeros((T, LANES), F32))
        return exchange_rows(ssq, l)

    def project_branch(l):
        if l == 0:
            weights_ready(l, [5])
        rs_start, rs_part = reduce_rows(l)

        def project_out(j, _):
            rs_send[l, :, lanes(j, ntile)] = dot(dye[...], wo[l, :, lanes(j, ntile)]).astype(BF16)
            return 0

        for q in range(parts_rs):
            lax.fori_loop(q * RW // ntile, (q + 1) * RW // ntile, project_out, 0)
            rs_start(q)
        return rs_part

    def gated(l, at):
        gate_in = z[l, :, at]
        return (y0[l, :, at] + prm[l, 7:8, at] * act[l, :, at]) * (gate_in * lax.logistic(gate_in))

    def scale_branch(l, finish_rows):
        qb[l] = lax.rsqrt(finish_rows() / inner_total + EPSILON)

        def scaled(p, _):
            at = lanes(p)
            us[l, :, at] = (gated(l, at) * qb[l] * prm[l, 6:7, at]).astype(BF16)
            return 0

        lax.fori_loop(0, pairs, scaled, 0)
        return collect(l, us.at[l], rhs.at[0, c])

    def finish_branch(l, rs_part, put):
        q_own = qb[l, own_rows, :][:, :1]
        for q in range(parts_rs):
            at = pl.ds(q * RW, RW)
            rows = hb[l, own_rows, at].astype(F32) + q_own * rs_part(q)
            put(q, rows.astype(BF16))

    def backward(l, gap_dot, gap_chain, gap_after, gap_join, gap_rs):
        hp1 = prm[l, 6:7, I + LANES : I + 2 * LANES]

        def start_du(j, acc):
            at = lanes(j, ntile)
            got = dot_nt(eb[l], wo[l, at, :])
            du[:, at] = got
            value = got * gated(l, at)
            weighted = value * prm[l, 6:7, at]
            return acc + weighted[:, :LANES] + weighted[:, LANES:]

        if l == 1:
            weights_ready(l, [5])
        acc = lax.fori_loop(0, I // ntile, start_du, jnp.zeros((T, LANES), F32))
        finish_rows = exchange_rows(acc, 2 + l)
        if l == 0:
            spread_heads(l)
            steps(l)
        gap_dot()
        dot_all = finish_rows()

        def through_gate(p, _):
            at = lanes(p)
            q = qb[l]
            gate_in = z[l, :, at]
            sig = lax.logistic(gate_in)
            silu = gate_in * sig
            x_now = act[l, :, at]
            full = y0[l, :, at] + prm[l, 7:8, at] * x_now
            small[l, 6:7, at] = jnp.sum(du[:, at] * full * silu * q, axis=0, keepdims=True)
            dg = q * (du[:, at] * prm[l, 6:7, at]) - full * silu * (q * q * q) * (
                dot_all / inner_total
            )
            d_y = dg * silu
            gp[l, :, lanes(p + pairs)] = (
                dg * full * sig * (1.0 + gate_in * (1.0 - sig))
            ).astype(BF16)
            small[l, 7:8, at] = jnp.sum(d_y * x_now, axis=0, keepdims=True)
            dy[:, at] = d_y
            dyb[:, at] = d_y.astype(BF16)
            dye[:, at] = (d_y * jnp.exp(cume[:, at])).astype(BF16)
            return 0

        lax.fori_loop(0, pairs, through_gate, 0)

        def local_state(j, _):
            dst_loc[:, lanes(j, ntile)] = dot(CT[l], dye[:, lanes(j, ntile)])
            return 0

        lax.fori_loop(0, I // ntile, local_state, 0)
        begin, finish_chain = chain(
            2 + l, False, dst_loc, jnp.exp(cume[T - 1 : T, :]), gin
        )
        begin()
        ready_z = collect(l, gp.at[l, :, pl.ds(I, I)], rhs.at[1, c])

        cbt = dot_nt(Bb[l], Cb[l])
        dcbt[...] = jnp.zeros_like(dcbt)

        def intra(p, _):
            at = lanes(p)
            wide = cume[:, at]
            values = xtb[:, at]
            grads = dyb[:, at]
            total = jnp.zeros((T, LANES), F32)
            for half in range(2):
                column = wide[:, half * head_size : half * head_size + 1]
                row = cumT[l, pl.ds(2 * p + half, 1), :]
                decay = jnp.where(earlier, jnp.exp(jnp.minimum(row - column, 0.0)), 0.0)
                mix = (cbt * decay).astype(BF16)
                kept = jnp.where(lane_low == (half == 0), grads, jnp.zeros_like(grads))
                total = total + dot(mix, kept)
                dcbt[...] += dot_nt(values, kept) * decay
            du[:, at] = total
            return 0

        lax.fori_loop(0, pairs, intra, 0)
        gap_chain(ready_z)
        finish_chain()
        gap_after()

        def join(p, carry):
            sum_v, sum_w = carry
            at = lanes(p)
            into = gin[:, at]
            acc = cume[:, at]
            end = acc[T - 1 : T]
            got = du[:, at] + jnp.exp(end - acc) * dot(Bb[l], into.astype(BF16))
            x_now = act[l, :, at]
            d_y = dy[:, at]
            leaving = s_ent[l, :, at] * jnp.exp(end) + st_loc[l, :, at]
            final = jnp.sum(into * leaving, axis=0, keepdims=True)
            v = dyb[:, at].astype(F32) * y0[l, :, at] - xtb[:, at].astype(F32) * got
            is_end = lax.broadcasted_iota(jnp.int32, (T, LANES), 0) == T - 1
            v = v + jnp.where(is_end, final, 0.0)
            dact[:T, at] = dte[:, at] * got + prm[l, 7:8, at] * d_y
            picks = et[at, :]
            return (sum_v + split_dot(v, picks), sum_w + split_dot(x_now * got, picks))

        zero = jnp.zeros((T, LANES), F32)
        sum_v, sum_w = lax.fori_loop(0, pairs, join, (zero, zero))

        dcb_low = dcbt[...].astype(BF16)
        gin_low = gin[...].astype(BF16)
        ent_low = s_ent[l].astype(BF16)
        dact[:T, I : I + N] = dot(dcb_low, Cb[l]) + dot_nt(xtl[...], gin_low)
        dact[:T, I + N :] = dot_tn(dcb_low, Bb[l]) + dot_nt(dye[...], ent_low)

        def conv_pre(j, _):
            at = lanes(j)
            total, moved = conv_sum(l, at, xin[l, :, at].astype(F32))
            sig = lax.logistic(total)
            got = dact[:T, at] * (sig * (1.0 + total * (1.0 - sig)))
            dact[:T, at] = got
            edge_send[l, :, at] = got[:EDGE].astype(BF16)
            small[l, 5:6, at] = jnp.sum(got, axis=0, keepdims=True)
            for shift in range(4):
                small[l, 4 - shift : 5 - shift, at] = jnp.sum(
                    got * moved[shift], axis=0, keepdims=True
                )
            return 0

        lax.fori_loop(0, XB // LANES, conv_pre, 0)
        edge = links.remote(edge_send.at[l], edge_recv.at[l], prev_dev, has_prev)
        start_if(has_prev, edge)

        d_log = lax.dot_general(
            tri[...], sum_v, (((0,), (0,)), ((), ())),
            precision=lax.Precision.HIGHEST, preferred_element_type=F32,
        )
        rate = -jnp.exp(hp1)
        d_raw = (sum_w + d_log * rate) * sgdt[l]
        small[l, 6:7, I : I + LANES] = jnp.sum(d_raw, axis=0, keepdims=True)
        small[l, 6:7, I + LANES : I + 2 * LANES] = jnp.sum(
            d_log * rate * dtv[l], axis=0, keepdims=True
        )
        d_raw = jnp.where(lax.broadcasted_iota(jnp.int32, (T, LANES), 1) < heads, d_raw, 0.0)
        gp[l, :, 2 * I + 2 * N :] = d_raw.astype(BF16)
        dt_rows = bc_rows.shape[1] - Q2
        bc_rows[l, Q2:, :] = jnp.transpose(d_raw)[:dt_rows].astype(BF16)
        gap_join()

        @pl.when(is_last)
        def _():
            dact[T:, :] = jnp.zeros((EDGE, XB), F32)

        @pl.when(has_next)
        def _():
            edge.wait_recv()
            dact[T:, :] = edge_recv[l].astype(F32)

        def conv_in(j, _):
            at = lanes(j)
            v = dact[:, at]
            total = prm[l, 4:5, at] * v[:T]
            for shift in range(1, 4):
                moved = pltpu.roll(v, T + EDGE - shift, 0)
                total = total + prm[l, 4 - shift : 5 - shift, at] * moved[:T]
            dact[:T, at] = total
            return 0

        lax.fori_loop(0, XB // LANES, conv_in, 0)
        gp[l, :, :I] = dact[:T, :I].astype(BF16)
        gp[l, :, 2 * I : 2 * I + 2 * N] = dact[:T, I:].astype(BF16)

        def normed_all(j, _):
            at = lanes(j, ntile)
            total = dot_nt(gp[l, :, I : 2 * I], wxz[l, 1, at, :])
            total = total + dot_nt(gp[l, :, :I], wxz[l, 0, at, :])
            total = total + dot_nt(gp[l, :, 2 * I : 2 * I + 2 * N], wbc[l, at, :])
            total = total + dot(gp[l, :, 2 * I + 2 * N :], wdt[l, :, at])
            rs_send[1 - l, :, at] = total.astype(BF16)
            return 0

        for copy in rs_copies[1 - l]:
            copy.wait_send()
        rs_start, rs_part = reduce_rows(1 - l)
        for q in range(parts_rs):
            lax.fori_loop(q * RW // ntile, (q + 1) * RW // ntile, normed_all, 0)
            rs_start(q)
        ready_x = collect(l, gp.at[l, :, pl.ds(0, I)], rhs.at[2, c])
        gap_rs(ready_x)
        got = jnp.concatenate([rs_part(q) for q in range(parts_rs)], axis=1)
        v = hb[l, own_rows, :].astype(F32)
        rstd = lax.rsqrt(jnp.mean(v * v, axis=1, keepdims=True) + EPSILON)
        small[l, 0:1, :] = jnp.sum(got * v * rstd, axis=0, keepdims=True)
        hat = got * prm[l, 0:1, :]
        inner = jnp.sum(hat * v, axis=1, keepdims=True)
        return (
            rstd * hat - v * (rstd * rstd * rstd) * inner / D
            + eb[l, own_rows, :].astype(F32)
        )

    def bc_start(l):
        copies = []
        bc_t[l] = jnp.transpose(dact[:T, I:]).astype(BF16)
        for d, peer in enumerate(head_peers):
            rows = pl.ds(pl.multiple_of(peer_at[d] * Q2, Q2), Q2)
            copy = links.remote(bc_t.at[l, rows], bc_recv.at[l, d], peer)
            copy.start()
            copies.append(copy)
        return copies

    def bc_mid(l, copies):
        total = bc_t[l, pl.ds(pl.multiple_of(k * Q2, Q2), Q2), :].astype(F32)
        for d, copy in enumerate(copies):
            copy.wait_recv()
            total = total + bc_recv[l, d].astype(F32)
        bc_rows[l, :Q2, :] = total.astype(BF16)
        return collect(l, bc_rows.at[l], bc_rhs.at[c])

    def bc_block(j):
        rows = pl.ds(pl.multiple_of(j * DB, DB), DB)
        return dot_nt(bc_rhs[0], lt[1, 0, rows, :]) + dot_nt(bc_rhs[1], lt[1, 1, rows, :])

    def bc_copies(l):
        return [
            links.remote(bc_send.at[d], bc_land.at[d], peer, c == l)
            for d, peer in enumerate(seq_peers)
        ]

    def bc_out_start(ready, copies):
        ready()
        for d, copy in enumerate(copies):
            bc_send[d] = bc_block(lax.rem(s + d + 1, n_seq)).astype(BF16)
            copy.start()

    def bc_gather_copies(l):
        return [
            links.remote(bc_all.at[k], bc_all.at[k], peer, c == l) for peer in head_peers
        ]

    def bc_sum(copies, gathers):
        total = bc_block(s)
        for d, copy in enumerate(copies):
            copy.wait_recv()
            total = total + bc_land[d].astype(F32)
        bc_all[k] = total[:Q2]
        for h in range(heads):
            gw_dt[h] = total[Q2 + h : Q2 + h + 1]
        for copy in gathers:
            copy.start()

    def bc_finish(gathers):
        for copy in gathers:
            copy.wait_recv()
        whole = jnp.concatenate([bc_all[i] for i in range(n_head)], axis=0)
        gw_bc[...] = jnp.transpose(whole) if DB % LANES == 0 else whole

    def small_start(l):
        copy = links.remote(small.at[l], sm_o, other, c != l)
        start_if(c != l, copy)
        heads_to = [
            links.remote(sm_t, sm_h.at[d], peer, c == l) for d, peer in enumerate(head_peers)
        ]
        seqs_to = [
            links.remote(sm_u, sm_z.at[d], peer, c == l) for d, peer in enumerate(seq_peers)
        ]
        return copy, heads_to, seqs_to

    def small_heads(l, copies):
        copies[0].wait_recv()
        sm_t[...] = small[l] + sm_o[...]
        for copy in copies[1]:
            copy.start()

    def small_seqs(copies):
        sm_u[...] = sm_t[...]
        for d, copy in enumerate(copies[1]):
            copy.wait_recv()
            sm_u[0:1, :] += sm_h[d, 0:1, :]
            sm_u[1:6, I : I + 2 * N] += sm_h[d, 1:6, I : I + 2 * N]
        for copy in copies[2]:
            copy.start()

    def small_finish(copies):
        total = sm_u[...]
        for d, copy in enumerate(copies[2]):
            copy.wait_recv()
            total = total + sm_z[d]
        g_gain[...] = total[0:1]
        for r in range(5):
            g_conv_x[r] = total[1 + r : 2 + r, :I]
            g_conv_bc[r] = total[1 + r : 2 + r, I : I + 2 * N]
        g_out[...] = total[6:7, :I]
        g_head[0] = total[6:7, I : I + heads]
        g_head[1] = total[6:7, I + LANES : I + LANES + heads]
        g_head[2] = split_dot(total[:, :I], et[...])[7:8, :heads]

    def deliver(kind):
        copy = links.remote(end_send, ends.at[c], other, c != kind)

        def put(q, rows):
            @pl.when(c == kind)
            def _():
                ends[c, :, pl.ds(q * RW, RW)] = rows.astype(F32)

            @pl.when(c != kind)
            def _():
                end_send[:, pl.ds(q * RW, RW)] = rows.astype(F32)
                if q == parts_rs - 1:
                    copy.start()

        def finish():
            wait_if(c == kind, copy)

        return put, finish

    on0, on1 = pl.when(c == 0), pl.when(c == 1)
    end0, end1 = pl.when(is_end & (c == 0)), pl.when(is_end & (c == 1))
    first0, last0 = pl.when(is_first & (c == 0)), pl.when(is_last & (c == 0))
    first1, last1 = pl.when(is_first & (c == 1)), pl.when(is_last & (c == 1))
    far = (far_copies(0, (1,), (1, 2)), far_copies(1, (0, 1), (0, 1, 2)))
    got = {}

    def up1(l, piece):
        z_forward(l, piece, True, True)

    def up2(l, piece):
        z_forward(l, piece, True, False)

    def down1(l, piece, part=None):
        z_forward(l, piece, False, True, part)

    def down2(l, piece):
        z_forward(l, piece, False, False)

    def nothing():
        pass

    run_e1, ready_e1 = collect_transposed(1, 0, eb.at[1])
    run_n0, ready_n0 = collect_transposed(0, 1, nm)
    run_n1, ready_n1 = collect_transposed(1, 1, nm)

    def send_e1():
        @on1
        def _():
            ready_e1()
            far[1][0][0].start()

    def send_n0():
        @on0
        def _():
            ready_n0()
            far[0][0][1].start()

    def gap():
        run_n0()

        @pl.when(is_first)
        def _():
            send_n0()

        load_e.wait()
        run_e1()

        @pl.when(is_last)
        def _():
            send_e1()

    def gap_rs():
        @pl.when(is_last)
        def _():
            send_n0()

        @pl.when(inside)
        def _():
            @on0
            def _():
                ready_n0()

        @pl.when(s < n_seq - 1)
        def _():
            @on1
            def _():
                ready_e1()

    put, finish_gather = gather_rows(hb.at[1])
    finish_q = forward(0, nothing, gap)
    rs_part = project_branch(0)
    ready_u0 = scale_branch(0, finish_q)
    gap_rs()
    finish_branch(0, rs_part, put)
    finish_gather()

    def gap():
        @on1
        def _():
            ready_n1()

        @end1
        def _():
            far[1][0][1].start()

    put, finish_out = deliver(1)
    finish_q1 = forward(1, run_n1, gap)

    def gap_dot():
        got["rs1"] = project_branch(1)
        ready_u1 = scale_branch(1, finish_q1)

        @on1
        def _():
            ready_u1()

        @on1
        def _():
            z_first(0)

    def gap_chain(ready):
        @on1
        def _():
            ready()

        @first1
        def _():
            far[1][1][1].start()

    def gap_join():
        @last1
        def _():
            far[1][1][0].start()
            far[1][1][1].start()

        finish_branch(1, got["rs1"], put)

        @on1
        def _():
            up1(1, 0)

    def gap_rs(ready):
        got["bc1"] = bc_start(1)

        @on1
        def _():
            ready()

        @end1
        def _():
            far[1][1][2].start()

        @on1
        def _():
            up1(1, 1)
            down1(1, 0)

    rows = backward(1, gap_dot, gap_chain, nothing, gap_join, gap_rs)
    put, finish_gather = gather_rows(eb.at[0])
    for q in range(parts_rs):
        put(q, rows[:, q * RW : (q + 1) * RW].astype(BF16))
    small1 = small_start(1)
    ready_bc1 = bc_mid(1, got["bc1"])
    bc_to1, bc_g1 = bc_copies(1), bc_gather_copies(1)

    @on1
    def _():
        down1(1, 1)
        up1(1, 2)
        up2(1, 0)
        down1(1, 2, 0)

    finish_gather()

    run_e0, ready_e0 = collect_transposed(0, 0, eb.at[0])

    def gap_dot():
        run_e0()

        @on1
        def _():
            down2(1, 0)
            small_heads(1, small1)

        @on0
        def _():
            ready_u0()
            ready_e0()
            z_first(0)
            z_last(0, 0)

    def gap_chain(ready):
        @on1
        def _():
            up2(1, 1)
            small_seqs(small1)

        @on0
        def _():
            z_last(0, 1)
            ready()

        @first0
        def _():
            far[0][1][1].start()

    def gap_after():
        @on1
        def _():
            down1(1, 2, 1)

    def gap_join():
        @on0
        def _():
            z_last(0, 2)

        @last0
        def _():
            far[0][1][1].start()

        @on0
        def _():
            up1(0, 0)

    def gap_rs(ready):
        got["bc0"] = bc_start(0)

        @on0
        def _():
            ready()

        @end0
        def _():
            far[0][1][2].start()

        @on0
        def _():
            up1(0, 1)

        @on1
        def _():
            down2(1, 1)
            up2(1, 2)
            bc_out_start(ready_bc1, bc_to1)
            z_final(1, 0)

    rows = backward(0, gap_dot, gap_chain, gap_after, gap_join, gap_rs)
    put, finish_in = deliver(0)
    for q in range(parts_rs):
        put(q, rows[:, q * RW : (q + 1) * RW])
    small0 = small_start(0)
    ready_bc0 = bc_mid(0, got["bc0"])
    bc_to0, bc_g0 = bc_copies(0), bc_gather_copies(0)

    @on1
    def _():
        small_finish(small1)
        bc_sum(bc_to1, bc_g1)
        z_final(1, 1)
        down2(1, 2)
        bc_finish(bc_g1)
        z_final(1, 2)

    @on0
    def _():
        bc_out_start(ready_bc0, bc_to0)
        down1(0, 0)
        up1(0, 2)
        small_heads(0, small0)
        up2(0, 0)
        down1(0, 1)
        down2(0, 0)
        up2(0, 1)
        down1(0, 2)
        z_final(0, 0)
        small_seqs(small0)
        down2(0, 1)
        bc_sum(bc_to0, bc_g0)
        z_final(0, 1)
        up2(0, 2)
        down2(0, 2)
        small_finish(small0)
        bc_finish(bc_g0)
        z_final(0, 2)

    if DB % LANES == 0:
        z_saved(0)
    z_saved(2)
    finish_out()
    finish_in()
    save = links.local(ends, ends_out)
    save.start()
    save.wait()

    @pl.when(inside)
    def _():
        for i in range(n_seq - 1):
            z_sent(1, i)
            z_sent(2, i)

    @pl.when(is_first | (is_last & (c == 0)))
    def _():
        for i in range(n_seq - 1):
            z_sent(0, i)

    for l, copy in lt_sends:

        @pl.when(c != l)
        def _():
            copy.wait_send()

    for slot in range(2):
        for copy in rs_copies[slot]:
            copy.wait_send()
    links.drain()


def run_layers(tokens, cotangent, w_xz, w_bc, w_dt, w_out, in_gain, in_conv_x, in_conv_bc, in_head, in_out):
    n_seq, n_head = lax.axis_size("seq"), lax.axis_size("head")
    _, T, D = tokens.shape
    I = w_xz.shape[2]
    N = w_bc.shape[1] // 2
    heads = in_head.shape[2]
    XB = I + 2 * N
    G = 2 * I + 2 * N + LANES
    Q = T // n_head
    DB = D // n_seq
    BR = 2 * N // n_head + (heads + 15) // 16 * 16
    sems = 160 + 4 * (n_seq + n_head)
    S = jax.ShapeDtypeStruct
    V = pltpu.VMEM
    dma = pltpu.SemaphoreType.DMA
    vm = pl.BlockSpec(memory_space=pltpu.VMEM)
    hbm = pl.BlockSpec(memory_space=pl.ANY)
    scratch = [
        V((2, 2, D, I), BF16), V((2, D, 2 * N), BF16), V((2, LANES, D), BF16), V((2, I, D), BF16),
        V((2, 8, D), F32), V((2, T, D), BF16), V((2, T, D), BF16), V((T, D), BF16),
        V((2, T + EDGE, XB), BF16), V((2, T, I), F32), V((2, T, XB), F32),
        V((T, I), F32), V((T, I), F32), V((2, T, I), F32),
        V((2, T, LANES), F32), V((2, T, LANES), F32), V((2, T, LANES), F32), V((2, LANES, T), F32),
        V((2, N, T), BF16), V((2, N, T), BF16), V((2, T, N), BF16), V((2, T, N), BF16),
        V((2, N, I), F32), V((2, N, I), F32), V((T, I), BF16), V((T, I), BF16),
        V((2, T, LANES), F32),
        V((T, I), F32), V((T, I), F32), V((T, I), BF16), V((T, I), BF16),
        V((N, I), F32), V((N, I), F32), V((T + EDGE, XB), F32),
        V((T, T), F32), V((2, T, G), BF16), V((2, T, I), BF16), V((2, 8, D), F32),
        V((4, 8, T), F32), V((4, n_head - 1, 8, T), F32),
        V((2, T, D), BF16), V((2, n_head - 1, Q, D), BF16),
        V((4, 6, N, I // 6), BF16), V((4, 6, N, I // 6), BF16),
        V((2, EDGE, XB), BF16), V((2, EDGE, XB), BF16),
        V((Q, D), F32), V((2, Q, D), F32), V((I, LANES), BF16), V((T, T), F32),
        V((2, 2, D, T), BF16), V((D, T), BF16), V((3, 2, T, I), BF16),
        V((2, n_seq - 1, DB, I), BF16), V((2, DB, I), BF16), V((DB, I), F32), V((I, DB), F32),
        V((2, DB, T), BF16), V((2, T, I), BF16),
        V((2, n_head - 1, 2 * N // n_head, T), BF16), V((2, 2 * N, T), BF16), V((2, BR, T), BF16),
        V((2, BR, T), BF16), V((n_seq - 1, BR, DB), BF16), V((n_seq - 1, BR, DB), BF16),
        V((n_head, 2 * N // n_head, DB), F32),
        V((8, D), F32), V((8, D), F32), V((n_head - 1, 8, D), F32), V((8, D), F32),
        V((n_seq - 1, 8, D), F32),
        dma((24,)), dma((sems,)), dma((sems,)),
        dma((3 * (n_seq - 1),)), dma((3 * (n_seq + 1),)), dma((6,)),
    ]
    dims = (n_seq, n_head, T, D, I, N, heads)
    return pl.pallas_call(
        functools.partial(layer_kernel, dims),
        out_shape=(
            S((2, Q, D), F32), S((I, DB) if DB % LANES == 0 else (DB, I), F32), S((2, DB, I), F32),
            S((DB, 2 * N) if DB % LANES == 0 else (2 * N, DB), F32), S((heads, 1, DB), F32),
            S((1, D), F32), S((5, 1, I), F32), S((5, 1, 2 * N), F32), S((3, 1, heads), F32),
            S((1, I), F32),
            S((3, n_seq + 1, DB, I), BF16), S((2, 2, D, T), BF16), S((3, 2, T, I), BF16),
        ),
        in_specs=[hbm] * 6 + [vm] * 5,
        out_specs=(hbm, hbm, hbm, vm, vm, vm, vm, vm, vm, vm, hbm, hbm, hbm),
        scratch_shapes=scratch,
        compiler_params=pltpu.CompilerParams(
            collective_id=0, has_side_effects=True, vmem_limit_bytes=63 * 2**20
        ),
        name="layers",
    )(
        tokens, cotangent, w_xz, w_bc, w_dt, w_out, in_gain, in_conv_x, in_conv_bc, in_head, in_out
    )[:10]


def body(
    tokens, cotangent, norm_gain, w_xz, w_bc, w_dt, conv_x, conv_bc, head_params, out_gain, w_out
):
    heads = w_dt.shape[2]
    dt_rows = jnp.pad(w_dt[0].T, ((0, -heads % EDGE), (0, 0)))
    ends, gw_out, gw_xz, gw_bc, gw_dt, g_gain, g_conv_x, g_conv_bc, g_head, g_out = run_layers(
        tokens,
        cotangent,
        jnp.swapaxes(w_xz[0], 0, 1),
        w_bc[0],
        dt_rows,
        w_out[0],
        norm_gain,
        jnp.swapaxes(conv_x, 0, 1),
        jnp.swapaxes(conv_bc, 0, 1),
        jnp.swapaxes(head_params, 0, 1),
        out_gain,
    )
    if gw_bc.shape[1] != w_bc.shape[2]:
        gw_bc = gw_bc.T
        gw_out = gw_out.T
    return (
        ends[None],
        g_gain,
        jnp.swapaxes(gw_xz, 0, 1)[None],
        gw_bc[None],
        jnp.transpose(gw_dt, (1, 2, 0)),
        jnp.swapaxes(g_conv_x, 0, 1),
        jnp.swapaxes(g_conv_bc, 0, 1),
        jnp.swapaxes(g_head, 0, 1),
        g_out,
        gw_out[None],
    )


def solution(mesh):
    placed = (
        P(None, "seq", None),
        P(None, "seq", None),
        P("section", None),
        P("section", None, None, "head"),
        P("section", None, None),
        P("section", None, "head"),
        P("section", None, "head"),
        P("section", None, None),
        P("section", None, "head"),
        P("section", "head"),
        P("section", "head", None),
    )
    return jax.shard_map(
        body,
        mesh=mesh,
        in_specs=placed,
        out_specs=(
            P("section", None, ("seq", "head"), None),
            P("section", None),
            P("section", "seq", None, "head"),
            P("section", "seq", None),
            P("section", "seq", "head"),
            P("section", None, "head"),
            P("section", None, None),
            P("section", None, "head"),
            P("section", "head"),
            P("section", "head", "seq"),
        ),
        check_vma=False,
    )
```

```python
import functools

import jax
import jax.numpy as jnp
from jax import lax
from jax.experimental import pallas as pl
from jax.experimental.pallas import tpu as pltpu
from jax.sharding import PartitionSpec as P

EPSILON = 1e-05
MESH = pl.DeviceIdType.MESH
LANES = 128
EDGE = 16
F32 = jnp.float32
BF16 = jnp.bfloat16


def dot(a, b):
    return lax.dot_general(a, b, (((1,), (0,)), ((), ())), preferred_element_type=F32)


def dot_nt(a, b):
    return lax.dot_general(a, b, (((1,), (1,)), ((), ())), preferred_element_type=F32)


def dot_tn(a, b):
    return lax.dot_general(a, b, (((0,), (0,)), ((), ())), preferred_element_type=F32)


def exact_dot(a, b):
    return lax.dot_general(
        a, b, (((1,), (0,)), ((), ())), precision=lax.Precision.HIGHEST, preferred_element_type=F32
    )


def split_dot(a, b):
    high = a.astype(BF16)
    return dot(high, b) + dot((a - high.astype(F32)).astype(BF16), b)


class Links:
    def __init__(self, local_sem, send_sem, recv_sem):
        self.local_sem, self.send_sem, self.recv_sem = local_sem, send_sem, recv_sem
        self.local_count = 0
        self.count = 0
        self.pending = []

    def local(self, src, dst):
        index = self.local_count
        assert index < self.local_sem.shape[0]
        self.local_count += 1
        return pltpu.make_async_copy(src, dst, self.local_sem.at[index])

    def remote(self, src, dst, peer, when=None):
        index = self.count
        assert index < self.send_sem.shape[0]
        self.count += 1
        copy = pltpu.make_async_remote_copy(
            src_ref=src,
            dst_ref=dst,
            send_sem=self.send_sem.at[index],
            recv_sem=self.recv_sem.at[index],
            device_id=peer,
            device_id_type=MESH,
        )
        self.pending.append((copy, when))
        return copy

    def drain(self):
        for copy, when in self.pending:
            if when is None:
                copy.wait_send()
            else:

                @pl.when(when)
                def _():
                    copy.wait_send()


def wait_if(condition, copy):
    @pl.when(condition)
    def _():
        copy.wait_recv()


def start_if(condition, copy):
    @pl.when(condition)
    def _():
        copy.start()


def lanes(i, width=LANES):
    if isinstance(i, int):
        return pl.ds(i * width, width)
    return pl.ds(pl.multiple_of(i * width, width), width)


def layer_kernel(dims, *refs):
    (n_seq, n_head, T, D, I, N, heads) = dims
    (
        tokens, cotangent, w_xz, w_bc, w_dt, w_out, in_gain, in_conv_x, in_conv_bc, in_head, in_out,
        ends_out, gw_out, gw_xz, gw_bc, gw_dt, g_gain, g_conv_x, g_conv_bc, g_head, g_out, z_land, far_lt, far_rhs,
        wxz, wbc, wdt, wo, prm, hb, eb, nm, xin, z, act, dte, cume, y0,
        sgdt, dtv, cum, cumT, CT, BT, Bb, Cb, st_loc, s_ent, xtb, xtl, qb,
        du, dy, dyb, dye, dst_loc, gin, dact, dcbt, gp, us, small,
        row_send, row_recv, rs_send, rs_recv, ch_send, ch_recv, edge_send, edge_recv,
        end_send, ends, et, tri,
        lt, lt_send, rhs, z_send, z_in, z_acc, z_turn, far_l, far_r, bc_recv, bc_t, bc_rows, bc_rhs, bc_send, bc_land, bc_all,
        sm_o, sm_t, sm_h, sm_u, sm_z,
        local_sem, send_sem, recv_sem, zs_sem, zr_sem, zi_sem,
    ) = refs
    c = lax.axis_index("section")
    s = lax.axis_index("seq")
    k = lax.axis_index("head")
    links = Links(local_sem, send_sem, recv_sem)
    Q = T // n_head
    XB = I + 2 * N
    DB = D // n_seq
    pairs = I // LANES
    head_size = I // heads
    is_first = s == 0
    is_last = s == n_seq - 1
    has_prev = s > 0
    has_next = s < n_seq - 1
    other = {"section": 1 - c}
    prev_dev = {"seq": jnp.maximum(s - 1, 0)}
    next_dev = {"seq": jnp.minimum(s + 1, n_seq - 1)}
    if n_head == 4:
        peer_at = [3 - k, k + 1 - 2 * lax.rem(k, 2), lax.rem(k + 2, 4)]
    else:
        peer_at = [lax.rem(k + d, n_head) for d in range(1, n_head)]
    head_peers = [{"head": at} for at in peer_at]
    seq_peers = [{"seq": lax.rem(s + d, n_seq)} for d in range(1, n_seq)]
    own_rows = pl.ds(pl.multiple_of(k * Q, Q), Q)
    chunks = 6
    CW = I // chunks
    ntile = 256
    inner_total = I * n_head
    Q2 = 2 * N // n_head
    rs_copies = {}
    parts_rs = 3
    RW = D // parts_rs

    barrier = pltpu.get_barrier_semaphore()
    for peer in [other] + head_peers + seq_peers:
        pl.semaphore_signal(barrier, inc=1, device_id=peer, device_id_type=MESH)

    load_h = links.local(tokens.at[c], hb.at[0])
    load_e = links.local(cotangent.at[c], eb.at[1])
    load_h.start()
    parts = (
        (w_xz.at[0], wxz.at[c, 0]),
        (w_bc, wbc.at[c]),
        (w_dt, wdt.at[c]),
        (w_xz.at[1], wxz.at[c, 1]),
        (w_out, wo.at[c]),
    )
    mine = [links.local(src, dst) for src, dst in parts]
    for copy in mine:
        copy.start()
    load_e.start()
    pl.semaphore_wait(barrier, n_head + n_seq - 1)
    low_row = lax.broadcasted_iota(jnp.int32, (1, LANES), 1) < head_size
    prm[c] = jnp.zeros((8, D), F32)
    prm[c, 0:1, :] = in_gain[...]
    for r in range(5):
        prm[c, 1 + r : 2 + r, :I] = in_conv_x[r]
        prm[c, 1 + r : 2 + r, I : I + 2 * N] = in_conv_bc[r]
    prm[c, 6:7, :I] = in_out[...]
    prm[c, 6:7, I : I + heads] = in_head[0]
    prm[c, 6:7, I + LANES : I + LANES + heads] = in_head[1]
    skips = in_head[2]
    for p in range(pairs):
        prm[c, 7:8, lanes(p)] = jnp.where(
            low_row, skips[:, 2 * p : 2 * p + 1], skips[:, 2 * p + 1 : 2 * p + 2]
        )
    theirs = [links.remote(prm.at[c], prm.at[c], other)]
    theirs += [links.remote(src, dst, other) for src, dst in parts]
    for copy in theirs:
        copy.start()

    def weights_ready(layer, which):
        @pl.when(c == layer)
        def _():
            for i in which:
                if i:
                    mine[i - 1].wait()

        @pl.when(c != layer)
        def _():
            for i in which:
                theirs[i].wait_recv()

    row_i = lax.broadcasted_iota(jnp.int32, (T, T), 0)
    col_i = lax.broadcasted_iota(jnp.int32, (T, T), 1)
    tri[...] = jnp.where(row_i >= col_i, 1.0, 0.0)
    er = lax.broadcasted_iota(jnp.int32, (I, LANES), 0)
    ec = lax.broadcasted_iota(jnp.int32, (I, LANES), 1)
    et[...] = jnp.where(
        (er >= ec * head_size) & (er < (ec + 1) * head_size), 1.0, 0.0
    ).astype(BF16)
    small[...] = jnp.zeros_like(small)
    load_h.wait()

    def exchange_rows(total_cols, slot):
        summed = jnp.sum(total_cols, axis=1, keepdims=True)
        as_row = jnp.transpose(jnp.broadcast_to(summed, (T, LANES)))[:8]
        row_send[slot] = as_row
        copies = []
        for d, peer in enumerate(head_peers):
            copy = links.remote(row_send.at[slot], row_recv.at[slot, d], peer)
            copy.start()
            copies.append(copy)

        def finish():
            total = row_send[slot]
            for d, copy in enumerate(copies):
                copy.wait_recv()
                total = total + row_recv[slot, d]
            wide = jnp.broadcast_to(total[:1], (LANES, T))
            return jnp.transpose(wide)

        return finish

    def reduce_rows(slot):
        copies = []
        for q in range(parts_rs):
            at = pl.ds(q * RW, RW)
            row = []
            for d, peer in enumerate(head_peers):
                rows = pl.ds(pl.multiple_of(peer_at[d] * Q, Q), Q)
                row.append(
                    links.remote(rs_send.at[slot, rows, at], rs_recv.at[slot, d, :, at], peer)
                )
                links.pending.pop()
            copies.append(row)
        rs_copies[slot] = [copy for row in copies for copy in row]

        def send(q):
            for copy in copies[q]:
                copy.start()

        def part(q):
            at = pl.ds(q * RW, RW)
            total = rs_send[slot, own_rows, at].astype(F32)
            for d, copy in enumerate(copies[q]):
                copy.wait_recv()
                total = total + rs_recv[slot, d, :, at].astype(F32)
            return total

        return send, part

    def gather_rows(target):
        copies = []
        for q in range(parts_rs):
            at = target.at[own_rows, pl.ds(q * RW, RW)]
            copies.append([links.remote(at, at, peer) for peer in head_peers])

        def send(q, rows):
            target[own_rows, pl.ds(q * RW, RW)] = rows
            for copy in copies[q]:
                copy.start()

        def finish():
            for row in copies:
                for copy in row:
                    copy.wait_recv()

        return send, finish

    def chain(slot, forward, local, dec_row, into):
        starts, goes_on = (is_first, has_next) if forward else (is_last, has_prev)
        receives = has_prev if forward else has_next
        peer = next_dev if forward else prev_dev
        copies = []
        for j in range(chunks):
            copies.append(
                links.remote(ch_send.at[slot, j], ch_recv.at[slot, j], peer, goes_on)
            )

        def begin():
            @pl.when(starts)
            def _():
                for j in range(chunks):
                    ch_send[slot, j] = local[:, lanes(j, CW)].astype(BF16)
                    start_if(goes_on, copies[j])

        def finish():
            @pl.when(starts)
            def _():
                into[...] = jnp.zeros_like(into)

            @pl.when(receives)
            def _():
                for j in range(chunks):
                    copies[j].wait_recv()
                    at = lanes(j, CW)
                    arrived = ch_recv[slot, j].astype(F32)
                    into[:, at] = arrived

                    @pl.when(goes_on)
                    def _():
                        ch_send[slot, j] = (
                            arrived * dec_row[:, j * CW : (j + 1) * CW] + local[:, at]
                        ).astype(BF16)
                        copies[j].start()

        return begin, finish

    def collect(l, src, dst):
        near = links.local(src, dst)
        far = links.remote(src, dst, other, c != l)

        @pl.when(c == l)
        def _():
            near.start()

        @pl.when(c != l)
        def _():
            far.start()

        def ready():
            near.wait()
            far.wait_recv()

        return ready

    lt_sends = []

    def collect_transposed(l, kind, src):
        far = links.remote(lt_send, lt.at[kind, c], other, c != l)
        links.pending.pop()
        before = [copy for layer, copy in lt_sends if layer == l]
        lt_sends[:] = [item for item in lt_sends if item[0] != l] + [(l, far)]

        def run():
            @pl.when(c == l)
            def _():
                def turn(t, _):
                    lt[kind, c, lanes(t), :] = jnp.transpose(src[:, lanes(t)].astype(F32)).astype(BF16)
                    return 0

                lax.fori_loop(0, D // LANES, turn, 0)

            @pl.when(c != l)
            def _():
                for copy in before:
                    copy.wait_send()

                def turn(t, _):
                    lt_send[lanes(t), :] = jnp.transpose(src[:, lanes(t)].astype(F32)).astype(BF16)
                    return 0

                lax.fori_loop(0, D // LANES, turn, 0)
                far.start()

        def ready():
            far.wait_recv()

        return run, ready

    low_half = s < n_seq // 2
    is_end = is_first | is_last
    inside = has_prev & has_next
    inward = {"seq": jnp.where(is_first, 1, jnp.where(is_last, n_seq - 2, s))}

    def far_copies(l, kinds, pieces):
        def one(a, there, i):
            ends = is_end if far_up(l, i) else is_last
            return links.remote(a.at[i], there.at[i], inward, ends & (c == l))

        return (
            {i: one(lt, far_lt, i) for i in kinds},
            {i: one(rhs, far_rhs, i) for i in pieces},
        )

    def far_up(l, piece):
        return piece > 0

    def far_down(l, piece):
        return l == 1 or piece > 0

    def z_copy(piece, j, up):
        if up:
            slot, peer = j, next_dev
        else:
            slot, peer = jnp.where(j == s - 1, n_seq, j), prev_dev
        index = jnp.where(j < s, j, j - 1)
        return pltpu.make_async_remote_copy(
            src_ref=z_send.at[piece % 2, index],
            dst_ref=z_land.at[piece, slot],
            send_sem=zs_sem.at[piece * (n_seq - 1) + index],
            recv_sem=zr_sem.at[piece * (n_seq + 1) + slot],
            device_id=peer,
            device_id_type=MESH,
        )

    def z_arrived(piece, slot, into):
        pltpu.make_async_remote_copy(
            src_ref=z_send.at[piece % 2, 0],
            dst_ref=z_land.at[piece, slot],
            send_sem=zs_sem.at[piece * (n_seq - 1)],
            recv_sem=zr_sem.at[piece * (n_seq + 1) + slot],
            device_id=prev_dev,
            device_id_type=MESH,
        ).wait_recv()
        return pltpu.make_async_copy(z_land.at[piece, slot], z_in.at[into], zi_sem.at[into])

    def z_block(piece, j, store):
        kind = 0 if piece == 0 else 1
        rows = pl.ds(pl.multiple_of(j * DB, DB), DB)

        def tile(t, _):
            at = lanes(t, ntile)
            store(
                at,
                dot(lt[kind, 0, rows, :], rhs[piece, 0, :, at])
                + dot(lt[kind, 1, rows, :], rhs[piece, 1, :, at]),
            )
            return 0

        lax.fori_loop(0, I // ntile, tile, 0)

    def hold(at, value):
        z_acc[:, at] = value

    def far_load(piece):
        return pltpu.make_async_copy(far_rhs.at[piece], far_r, zi_sem.at[3])

    def far_block(piece, j, store, load):
        kind = 0 if piece == 0 else 1
        rows = pl.ds(pl.multiple_of(j * DB, DB), DB)
        left = pltpu.make_async_copy(far_lt.at[kind, :, rows], far_l, zi_sem.at[2])
        left.start()
        z_block(piece, j, hold)
        if load is not None:
            load.wait()
        left.wait()

        def tile(t, _):
            at = lanes(t, ntile)
            store(
                at,
                z_acc[:, at] + dot(far_l[0], far_r[0, :, at]) + dot(far_l[1], far_r[1, :, at]),
            )
            return 0

        lax.fori_loop(0, I // ntile, tile, 0)

    def z_one(piece, j, up):
        index = jnp.where(j < s, j, j - 1)
        def store(at, value):
            z_send[piece % 2, index, :, at] = value.astype(BF16)

        z_block(piece, j, store)
        z_copy(piece, j, up).start()
        return 0

    def z_first(piece):
        @pl.when(is_first)
        def _():
            lax.fori_loop(0, n_seq - 1, lambda i, _: z_one(piece, n_seq - 1 - i, True), 0)

    def z_last(piece, part):
        low, high = (n_seq - 1) * part // 3, (n_seq - 1) * (part + 1) // 3

        @pl.when(is_last)
        def _():
            lax.fori_loop(low, high, lambda i, _: z_one(piece, i, False), 0)

    def z_sent(piece, index):
        pltpu.make_async_remote_copy(
            src_ref=z_send.at[piece % 2, index],
            dst_ref=z_land.at[piece, 0],
            send_sem=zs_sem.at[piece * (n_seq - 1) + index],
            recv_sem=zr_sem.at[piece * (n_seq + 1)],
            device_id=next_dev,
            device_id_type=MESH,
        ).wait_send()

    def z_forward(l, piece, up, first, part=None):
        mine = inside & (low_half if up == first else jnp.logical_not(low_half))
        count = n_seq - 1 - s if up else s
        begin, end = 0, count
        if part is not None:
            begin, end = (0, count // 2) if part == 0 else (count // 2, count)

        def one(i, _, far):
            j = n_seq - 1 - i if up else i
            index = jnp.where(j < s, j, j - 1)
            if piece == 2:
                z_sent(0, index)
            if far:

                def store(at, value):
                    z_send[piece % 2, index, :, at] = value.astype(BF16)

                far_block(piece, j, store, None)
            else:
                load = z_arrived(piece, j, 0)
                load.start()
                z_block(piece, j, hold)
                load.wait()
                z_send[piece % 2, index] = (z_acc[...] + z_in[0].astype(F32)).astype(BF16)
            z_copy(piece, j, up).start()
            return 0

        use_far = far_up(l, piece) if up else far_down(l, piece)
        near = s == 1 if up else s == n_seq - 2
        if first and use_far:

            @pl.when(mine & near)
            def _():
                if not part:
                    if piece < 2:
                        far[l][0][piece].wait_recv()
                    far[l][1][piece].wait_recv()
                load = far_load(piece)
                load.start()
                load.wait()
                lax.fori_loop(begin, end, functools.partial(one, far=True), 0)

            if n_seq > 4:

                @pl.when(mine & jnp.logical_not(near))
                def _():
                    lax.fori_loop(begin, end, functools.partial(one, far=False), 0)

        else:

            @pl.when(mine)
            def _():
                lax.fori_loop(begin, end, functools.partial(one, far=False), 0)

    def z_final(l, piece):
        by_low, by_high = far_up(l, piece), far_down(l, piece)
        from_low = s >= (2 if by_low else 1)
        from_high = s < n_seq - (2 if by_high else 1)
        near = ((s == 1) & by_low) | ((s == n_seq - 2) & by_high)

        @pl.when(from_low)
        def _():
            z_arrived(piece, s, 0).start()

        @pl.when(from_high)
        def _():
            z_arrived(piece, n_seq, 1).start()

        if by_low or by_high:

            @pl.when(near)
            def _():
                load = far_load(piece)
                load.start()
                far_block(piece, s, hold, load)

            @pl.when(jnp.logical_not(near))
            def _():
                z_block(piece, s, hold)

        else:
            z_block(piece, s, hold)

        @pl.when(from_low)
        def _():
            pltpu.make_async_copy(z_land.at[piece, s], z_in.at[0], zi_sem.at[0]).wait()
            z_acc[...] += z_in[0].astype(F32)

        @pl.when(from_high)
        def _():
            pltpu.make_async_copy(z_land.at[piece, n_seq], z_in.at[1], zi_sem.at[1]).wait()
            z_acc[...] += z_in[1].astype(F32)

        if piece == 0 and DB % LANES == 0:
            for t in range(I // ntile):
                at = lanes(t, ntile)
                z_turn[at, :] = jnp.transpose(z_acc[:, at])
        z_save(piece).start()
        if piece == 1 or (piece == 0 and DB % LANES):
            z_saved(piece)

    def z_save(piece):
        if piece == 0 and DB % LANES == 0:
            return pltpu.make_async_copy(z_turn, gw_out, zi_sem.at[4])
        target = gw_out if piece == 0 else gw_xz.at[2 - piece]
        return pltpu.make_async_copy(z_acc, target, zi_sem.at[5])

    def z_saved(piece):
        z_save(piece).wait()

    lane_low = lax.broadcasted_iota(jnp.int32, (T, LANES), 1) < head_size
    later = row_i >= col_i
    earlier = col_i >= row_i

    def spread_heads(l):
        for p in range(pairs):
            at = lanes(p)
            dte[:, at] = jnp.where(
                lane_low, dtv[l, :, 2 * p : 2 * p + 1], dtv[l, :, 2 * p + 1 : 2 * p + 2]
            )
            cume[:, at] = jnp.where(
                lane_low, cum[l, :, 2 * p : 2 * p + 1], cum[l, :, 2 * p + 1 : 2 * p + 2]
            )

    def steps(l):
        def one(p, _):
            at = lanes(p)
            acc = cume[:, at]
            stepped = dte[:, at] * act[l, :, at]
            xtb[:, at] = stepped.astype(BF16)
            xtl[:, at] = (stepped * jnp.exp(acc[T - 1 : T] - acc)).astype(BF16)
            return 0

        lax.fori_loop(0, pairs, one, 0)

    def conv_sum(l, at, v):
        total = prm[l, 5:6, at] + prm[l, 4:5, at] * v[EDGE:]
        moved = []
        for shift in range(1, 4):
            moved.append(pltpu.roll(v, shift, 0)[EDGE:])
            total = total + prm[l, 4 - shift : 5 - shift, at] * moved[-1]
        return total, [v[EDGE:]] + moved

    def forward(l, gap_norm, gap_chain):
        weights_ready(l, [0])
        gain = prm[l, 0:1, :]

        def norm_rows(i, _):
            rows = pl.ds(pl.multiple_of(i * 32, 32), 32)
            v = hb[l, rows, :].astype(F32)
            rstd = lax.rsqrt(jnp.mean(v * v, axis=1, keepdims=True) + EPSILON)
            nm[rows, :] = (v * rstd * gain).astype(BF16)
            return 0

        lax.fori_loop(0, T // 32, norm_rows, 0)

        gap_norm()
        weights_ready(l, [1, 2, 3])

        def project_x(j, _):
            xin[l, EDGE:, lanes(j, ntile)] = dot(
                nm[...], wxz[l, 0, :, lanes(j, ntile)]
            ).astype(BF16)
            return 0

        lax.fori_loop(0, I // ntile, project_x, 0)
        xin[l, EDGE:, I:] = dot(nm[...], wbc[l]).astype(BF16)

        edge = links.remote(
            xin.at[l, pl.ds(T, EDGE)], xin.at[l, pl.ds(0, EDGE)], next_dev, has_next
        )
        start_if(has_next, edge)

        dt_raw = dot_nt(nm[...], wdt[l])
        hp0 = prm[l, 6:7, I : I + LANES]
        hp1 = prm[l, 6:7, I + LANES : I + 2 * LANES]
        pre_dt = dt_raw + hp0
        sgdt[l] = lax.logistic(pre_dt)
        step = jnp.maximum(pre_dt, 0.0) + jnp.log1p(jnp.exp(-jnp.abs(pre_dt)))
        dtv[l] = step
        cum[l] = exact_dot(tri[...], -jnp.exp(hp1) * step)
        cumT[l] = jnp.transpose(cum[l])

        weights_ready(l, [4])

        def project_z(j, _):
            z[l, :, lanes(j, ntile)] = dot(nm[...], wxz[l, 1, :, lanes(j, ntile)])
            return 0

        lax.fori_loop(0, I // ntile, project_z, 0)

        @pl.when(is_first)
        def _():
            xin[l, :EDGE, :] = jnp.zeros((EDGE, XB), BF16)

        wait_if(has_prev, edge)

        def conv(j, _):
            at = lanes(j)
            total, _ = conv_sum(l, at, xin[l, :, at].astype(F32))
            act[l, :, at] = total * lax.logistic(total)
            return 0

        lax.fori_loop(0, XB // LANES, conv, 0)

        mat_b = act[l, :, I : I + N]
        mat_c = act[l, :, I + N :]
        Bb[l] = mat_b.astype(BF16)
        Cb[l] = mat_c.astype(BF16)
        BT[l] = jnp.transpose(mat_b).astype(BF16)
        CT[l] = jnp.transpose(mat_c).astype(BF16)
        spread_heads(l)
        steps(l)

        def local_state(j, _):
            st_loc[l, :, lanes(j, ntile)] = dot(BT[l], xtl[:, lanes(j, ntile)])
            return 0

        lax.fori_loop(0, I // ntile, local_state, 0)
        begin, finish_chain = chain(
            l, True, st_loc.at[l], jnp.exp(cume[T - 1 : T, :]), s_ent.at[l]
        )
        begin()

        cb = dot_nt(Cb[l], Bb[l])

        def intra(p, _):
            at = lanes(p)
            wide = cume[:, at]
            values = xtb[:, at]
            total = jnp.zeros((T, LANES), F32)
            for half in range(2):
                column = wide[:, half * head_size : half * head_size + 1]
                row = cumT[l, pl.ds(2 * p + half, 1), :]
                decay = jnp.where(later, jnp.exp(jnp.minimum(column - row, 0.0)), 0.0)
                mix = (cb * decay).astype(BF16)
                kept = jnp.where(lane_low == (half == 0), values, jnp.zeros_like(values))
                total = total + dot(mix, kept)
            y0[l, :, at] = total
            return 0

        lax.fori_loop(0, pairs, intra, 0)
        gap_chain()
        finish_chain()

        def gate(p, ssq):
            at = lanes(p)
            carried = dot(Cb[l], s_ent[l, :, at].astype(BF16))
            y = y0[l, :, at] + jnp.exp(cume[:, at]) * carried
            y0[l, :, at] = y
            full = y + prm[l, 7:8, at] * act[l, :, at]
            gate_in = z[l, :, at]
            value = full * (gate_in * lax.logistic(gate_in))
            dye[:, at] = (value * prm[l, 6:7, at]).astype(BF16)
            return ssq + value * value

        ssq = lax.fori_loop(0, pairs, gate, jnp.zeros((T, LANES), F32))
        return exchange_rows(ssq, l)

    def project_branch(l):
        if l == 0:
            weights_ready(l, [5])
        rs_start, rs_part = reduce_rows(l)

        def project_out(j, _):
            rs_send[l, :, lanes(j, ntile)] = dot(dye[...], wo[l, :, lanes(j, ntile)]).astype(BF16)
            return 0

        for q in range(parts_rs):
            lax.fori_loop(q * RW // ntile, (q + 1) * RW // ntile, project_out, 0)
            rs_start(q)
        return rs_part

    def gated(l, at):
        gate_in = z[l, :, at]
        return (y0[l, :, at] + prm[l, 7:8, at] * act[l, :, at]) * (gate_in * lax.logistic(gate_in))

    def scale_branch(l, finish_rows):
        qb[l] = lax.rsqrt(finish_rows() / inner_total + EPSILON)

        def scaled(p, _):
            at = lanes(p)
            us[l, :, at] = (gated(l, at) * qb[l] * prm[l, 6:7, at]).astype(BF16)
            return 0

        lax.fori_loop(0, pairs, scaled, 0)
        return collect(l, us.at[l], rhs.at[0, c])

    def finish_branch(l, rs_part, put):
        q_own = qb[l, own_rows, :][:, :1]
        for q in range(parts_rs):
            at = pl.ds(q * RW, RW)
            rows = hb[l, own_rows, at].astype(F32) + q_own * rs_part(q)
            put(q, rows.astype(BF16))

    def backward(l, gap_dot, gap_chain, gap_after, gap_join, gap_rs):
        hp1 = prm[l, 6:7, I + LANES : I + 2 * LANES]

        def start_du(j, acc):
            at = lanes(j, ntile)
            got = dot_nt(eb[l], wo[l, at, :])
            du[:, at] = got
            value = got * gated(l, at)
            weighted = value * prm[l, 6:7, at]
            return acc + weighted[:, :LANES] + weighted[:, LANES:]

        if l == 1:
            weights_ready(l, [5])
        acc = lax.fori_loop(0, I // ntile, start_du, jnp.zeros((T, LANES), F32))
        finish_rows = exchange_rows(acc, 2 + l)
        if l == 0:
            spread_heads(l)
            steps(l)
        gap_dot()
        dot_all = finish_rows()

        def through_gate(p, _):
            at = lanes(p)
            q = qb[l]
            gate_in = z[l, :, at]
            sig = lax.logistic(gate_in)
            silu = gate_in * sig
            x_now = act[l, :, at]
            full = y0[l, :, at] + prm[l, 7:8, at] * x_now
            small[l, 6:7, at] = jnp.sum(du[:, at] * full * silu * q, axis=0, keepdims=True)
            dg = q * (du[:, at] * prm[l, 6:7, at]) - full * silu * (q * q * q) * (
                dot_all / inner_total
            )
            d_y = dg * silu
            gp[l, :, lanes(p + pairs)] = (
                dg * full * sig * (1.0 + gate_in * (1.0 - sig))
            ).astype(BF16)
            small[l, 7:8, at] = jnp.sum(d_y * x_now, axis=0, keepdims=True)
            dy[:, at] = d_y
            dyb[:, at] = d_y.astype(BF16)
            dye[:, at] = (d_y * jnp.exp(cume[:, at])).astype(BF16)
            return 0

        lax.fori_loop(0, pairs, through_gate, 0)

        def local_state(j, _):
            dst_loc[:, lanes(j, ntile)] = dot(CT[l], dye[:, lanes(j, ntile)])
            return 0

        lax.fori_loop(0, I // ntile, local_state, 0)
        begin, finish_chain = chain(
            2 + l, False, dst_loc, jnp.exp(cume[T - 1 : T, :]), gin
        )
        begin()
        ready_z = collect(l, gp.at[l, :, pl.ds(I, I)], rhs.at[1, c])

        cbt = dot_nt(Bb[l], Cb[l])
        dcbt[...] = jnp.zeros_like(dcbt)

        def intra(p, _):
            at = lanes(p)
            wide = cume[:, at]
            values = xtb[:, at]
            grads = dyb[:, at]
            total = jnp.zeros((T, LANES), F32)
            for half in range(2):
                column = wide[:, half * head_size : half * head_size + 1]
                row = cumT[l, pl.ds(2 * p + half, 1), :]
                decay = jnp.where(earlier, jnp.exp(jnp.minimum(row - column, 0.0)), 0.0)
                mix = (cbt * decay).astype(BF16)
                kept = jnp.where(lane_low == (half == 0), grads, jnp.zeros_like(grads))
                total = total + dot(mix, kept)
                dcbt[...] += dot_nt(values, kept) * decay
            du[:, at] = total
            return 0

        lax.fori_loop(0, pairs, intra, 0)
        gap_chain(ready_z)
        finish_chain()
        gap_after()

        def join(p, carry):
            sum_v, sum_w = carry
            at = lanes(p)
            into = gin[:, at]
            acc = cume[:, at]
            end = acc[T - 1 : T]
            got = du[:, at] + jnp.exp(end - acc) * dot(Bb[l], into.astype(BF16))
            x_now = act[l, :, at]
            d_y = dy[:, at]
            leaving = s_ent[l, :, at] * jnp.exp(end) + st_loc[l, :, at]
            final = jnp.sum(into * leaving, axis=0, keepdims=True)
            v = dyb[:, at].astype(F32) * y0[l, :, at] - xtb[:, at].astype(F32) * got
            is_end = lax.broadcasted_iota(jnp.int32, (T, LANES), 0) == T - 1
            v = v + jnp.where(is_end, final, 0.0)
            dact[:T, at] = dte[:, at] * got + prm[l, 7:8, at] * d_y
            picks = et[at, :]
            return (sum_v + split_dot(v, picks), sum_w + split_dot(x_now * got, picks))

        zero = jnp.zeros((T, LANES), F32)
        sum_v, sum_w = lax.fori_loop(0, pairs, join, (zero, zero))

        dcb_low = dcbt[...].astype(BF16)
        gin_low = gin[...].astype(BF16)
        ent_low = s_ent[l].astype(BF16)
        dact[:T, I : I + N] = dot(dcb_low, Cb[l]) + dot_nt(xtl[...], gin_low)
        dact[:T, I + N :] = dot_tn(dcb_low, Bb[l]) + dot_nt(dye[...], ent_low)

        def conv_pre(j, _):
            at = lanes(j)
            total, moved = conv_sum(l, at, xin[l, :, at].astype(F32))
            sig = lax.logistic(total)
            got = dact[:T, at] * (sig * (1.0 + total * (1.0 - sig)))
            dact[:T, at] = got
            edge_send[l, :, at] = got[:EDGE].astype(BF16)
            small[l, 5:6, at] = jnp.sum(got, axis=0, keepdims=True)
            for shift in range(4):
                small[l, 4 - shift : 5 - shift, at] = jnp.sum(
                    got * moved[shift], axis=0, keepdims=True
                )
            return 0

        lax.fori_loop(0, XB // LANES, conv_pre, 0)
        edge = links.remote(edge_send.at[l], edge_recv.at[l], prev_dev, has_prev)
        start_if(has_prev, edge)

        d_log = lax.dot_general(
            tri[...], sum_v, (((0,), (0,)), ((), ())),
            precision=lax.Precision.HIGHEST, preferred_element_type=F32,
        )
        rate = -jnp.exp(hp1)
        d_raw = (sum_w + d_log * rate) * sgdt[l]
        small[l, 6:7, I : I + LANES] = jnp.sum(d_raw, axis=0, keepdims=True)
        small[l, 6:7, I + LANES : I + 2 * LANES] = jnp.sum(
            d_log * rate * dtv[l], axis=0, keepdims=True
        )
        d_raw = jnp.where(lax.broadcasted_iota(jnp.int32, (T, LANES), 1) < heads, d_raw, 0.0)
        gp[l, :, 2 * I + 2 * N :] = d_raw.astype(BF16)
        dt_rows = bc_rows.shape[1] - Q2
        bc_rows[l, Q2:, :] = jnp.transpose(d_raw)[:dt_rows].astype(BF16)
        gap_join()

        @pl.when(is_last)
        def _():
            dact[T:, :] = jnp.zeros((EDGE, XB), F32)

        @pl.when(has_next)
        def _():
            edge.wait_recv()
            dact[T:, :] = edge_recv[l].astype(F32)

        def conv_in(j, _):
            at = lanes(j)
            v = dact[:, at]
            total = prm[l, 4:5, at] * v[:T]
            for shift in range(1, 4):
                moved = pltpu.roll(v, T + EDGE - shift, 0)
                total = total + prm[l, 4 - shift : 5 - shift, at] * moved[:T]
            dact[:T, at] = total
            return 0

        lax.fori_loop(0, XB // LANES, conv_in, 0)
        gp[l, :, :I] = dact[:T, :I].astype(BF16)
        gp[l, :, 2 * I : 2 * I + 2 * N] = dact[:T, I:].astype(BF16)

        def normed_all(j, _):
            at = lanes(j, ntile)
            total = dot_nt(gp[l, :, I : 2 * I], wxz[l, 1, at, :])
            total = total + dot_nt(gp[l, :, :I], wxz[l, 0, at, :])
            total = total + dot_nt(gp[l, :, 2 * I : 2 * I + 2 * N], wbc[l, at, :])
            total = total + dot(gp[l, :, 2 * I + 2 * N :], wdt[l, :, at])
            rs_send[1 - l, :, at] = total.astype(BF16)
            return 0

        for copy in rs_copies[1 - l]:
            copy.wait_send()
        rs_start, rs_part = reduce_rows(1 - l)
        for q in range(parts_rs):
            lax.fori_loop(q * RW // ntile, (q + 1) * RW // ntile, normed_all, 0)
            rs_start(q)
        ready_x = collect(l, gp.at[l, :, pl.ds(0, I)], rhs.at[2, c])
        gap_rs(ready_x)
        got = jnp.concatenate([rs_part(q) for q in range(parts_rs)], axis=1)
        v = hb[l, own_rows, :].astype(F32)
        rstd = lax.rsqrt(jnp.mean(v * v, axis=1, keepdims=True) + EPSILON)
        small[l, 0:1, :] = jnp.sum(got * v * rstd, axis=0, keepdims=True)
        hat = got * prm[l, 0:1, :]
        inner = jnp.sum(hat * v, axis=1, keepdims=True)
        return (
            rstd * hat - v * (rstd * rstd * rstd) * inner / D
            + eb[l, own_rows, :].astype(F32)
        )

    def bc_start(l):
        copies = []
        bc_t[l] = jnp.transpose(dact[:T, I:]).astype(BF16)
        for d, peer in enumerate(head_peers):
            rows = pl.ds(pl.multiple_of(peer_at[d] * Q2, Q2), Q2)
            copy = links.remote(bc_t.at[l, rows], bc_recv.at[l, d], peer)
            copy.start()
            copies.append(copy)
        return copies

    def bc_mid(l, copies):
        total = bc_t[l, pl.ds(pl.multiple_of(k * Q2, Q2), Q2), :].astype(F32)
        for d, copy in enumerate(copies):
            copy.wait_recv()
            total = total + bc_recv[l, d].astype(F32)
        bc_rows[l, :Q2, :] = total.astype(BF16)
        return collect(l, bc_rows.at[l], bc_rhs.at[c])

    def bc_block(j):
        rows = pl.ds(pl.multiple_of(j * DB, DB), DB)
        return dot_nt(bc_rhs[0], lt[1, 0, rows, :]) + dot_nt(bc_rhs[1], lt[1, 1, rows, :])

    def bc_copies(l):
        return [
            links.remote(bc_send.at[d], bc_land.at[d], peer, c == l)
            for d, peer in enumerate(seq_peers)
        ]

    def bc_out_start(ready, copies):
        ready()
        for d, copy in enumerate(copies):
            bc_send[d] = bc_block(lax.rem(s + d + 1, n_seq)).astype(BF16)
            copy.start()

    def bc_gather_copies(l):
        return [
            links.remote(bc_all.at[k], bc_all.at[k], peer, c == l) for peer in head_peers
        ]

    def bc_sum(copies, gathers):
        total = bc_block(s)
        for d, copy in enumerate(copies):
            copy.wait_recv()
            total = total + bc_land[d].astype(F32)
        bc_all[k] = total[:Q2]
        for h in range(heads):
            gw_dt[h] = total[Q2 + h : Q2 + h + 1]
        for copy in gathers:
            copy.start()

    def bc_finish(gathers):
        for copy in gathers:
            copy.wait_recv()
        whole = jnp.concatenate([bc_all[i] for i in range(n_head)], axis=0)
        gw_bc[...] = jnp.transpose(whole) if DB % LANES == 0 else whole

    def small_start(l):
        copy = links.remote(small.at[l], sm_o, other, c != l)
        start_if(c != l, copy)
        heads_to = [
            links.remote(sm_t, sm_h.at[d], peer, c == l) for d, peer in enumerate(head_peers)
        ]
        seqs_to = [
            links.remote(sm_u, sm_z.at[d], peer, c == l) for d, peer in enumerate(seq_peers)
        ]
        return copy, heads_to, seqs_to

    def small_heads(l, copies):
        copies[0].wait_recv()
        sm_t[...] = small[l] + sm_o[...]
        for copy in copies[1]:
            copy.start()

    def small_seqs(copies):
        sm_u[...] = sm_t[...]
        for d, copy in enumerate(copies[1]):
            copy.wait_recv()
            sm_u[0:1, :] += sm_h[d, 0:1, :]
            sm_u[1:6, I : I + 2 * N] += sm_h[d, 1:6, I : I + 2 * N]
        for copy in copies[2]:
            copy.start()

    def small_finish(copies):
        total = sm_u[...]
        for d, copy in enumerate(copies[2]):
            copy.wait_recv()
            total = total + sm_z[d]
        g_gain[...] = total[0:1]
        for r in range(5):
            g_conv_x[r] = total[1 + r : 2 + r, :I]
            g_conv_bc[r] = total[1 + r : 2 + r, I : I + 2 * N]
        g_out[...] = total[6:7, :I]
        g_head[0] = total[6:7, I : I + heads]
        g_head[1] = total[6:7, I + LANES : I + LANES + heads]
        g_head[2] = split_dot(total[:, :I], et[...])[7:8, :heads]

    def deliver(kind):
        copy = links.remote(end_send, ends.at[c], other, c != kind)

        def put(q, rows):
            @pl.when(c == kind)
            def _():
                ends[c, :, pl.ds(q * RW, RW)] = rows.astype(F32)

            @pl.when(c != kind)
            def _():
                end_send[:, pl.ds(q * RW, RW)] = rows.astype(F32)
                if q == parts_rs - 1:
                    copy.start()

        def finish():
            wait_if(c == kind, copy)

        return put, finish

    on0, on1 = pl.when(c == 0), pl.when(c == 1)
    end0, end1 = pl.when(is_end & (c == 0)), pl.when(is_end & (c == 1))
    first0, last0 = pl.when(is_first & (c == 0)), pl.when(is_last & (c == 0))
    first1, last1 = pl.when(is_first & (c == 1)), pl.when(is_last & (c == 1))
    far = (far_copies(0, (1,), (1, 2)), far_copies(1, (0, 1), (0, 1, 2)))
    got = {}

    def up1(l, piece):
        z_forward(l, piece, True, True)

    def up2(l, piece):
        z_forward(l, piece, True, False)

    def down1(l, piece, part=None):
        z_forward(l, piece, False, True, part)

    def down2(l, piece):
        z_forward(l, piece, False, False)

    def nothing():
        pass

    run_e1, ready_e1 = collect_transposed(1, 0, eb.at[1])
    run_n0, ready_n0 = collect_transposed(0, 1, nm)
    run_n1, ready_n1 = collect_transposed(1, 1, nm)

    def send_e1():
        @on1
        def _():
            ready_e1()
            far[1][0][0].start()

    def send_n0():
        @on0
        def _():
            ready_n0()
            far[0][0][1].start()

    def gap():
        run_n0()

        @pl.when(is_first)
        def _():
            send_n0()

        load_e.wait()
        run_e1()

        @pl.when(is_last)
        def _():
            send_e1()

    def gap_rs():
        @pl.when(is_last)
        def _():
            send_n0()

        @pl.when(inside)
        def _():
            @on0
            def _():
                ready_n0()

        @pl.when(s < n_seq - 1)
        def _():
            @on1
            def _():
                ready_e1()

    put, finish_gather = gather_rows(hb.at[1])
    finish_q = forward(0, nothing, gap)
    rs_part = project_branch(0)
    ready_u0 = scale_branch(0, finish_q)
    gap_rs()
    finish_branch(0, rs_part, put)
    finish_gather()

    def gap():
        @on1
        def _():
            ready_n1()

        @end1
        def _():
            far[1][0][1].start()

    put, finish_out = deliver(1)
    finish_q1 = forward(1, run_n1, gap)

    def gap_dot():
        got["rs1"] = project_branch(1)
        ready_u1 = scale_branch(1, finish_q1)

        @on1
        def _():
            ready_u1()

        @on1
        def _():
            z_first(0)

    def gap_chain(ready):
        @on1
        def _():
            ready()

        @first1
        def _():
            far[1][1][1].start()

    def gap_join():
        @last1
        def _():
            far[1][1][0].start()
            far[1][1][1].start()

        finish_branch(1, got["rs1"], put)

        @on1
        def _():
            up1(1, 0)

    def gap_rs(ready):
        got["bc1"] = bc_start(1)

        @on1
        def _():
            ready()

        @end1
        def _():
            far[1][1][2].start()

        @on1
        def _():
            up1(1, 1)
            down1(1, 0)

    rows = backward(1, gap_dot, gap_chain, nothing, gap_join, gap_rs)
    put, finish_gather = gather_rows(eb.at[0])
    for q in range(parts_rs):
        put(q, rows[:, q * RW : (q + 1) * RW].astype(BF16))
    small1 = small_start(1)
    ready_bc1 = bc_mid(1, got["bc1"])
    bc_to1, bc_g1 = bc_copies(1), bc_gather_copies(1)

    @on1
    def _():
        down1(1, 1)
        up1(1, 2)
        up2(1, 0)
        down1(1, 2, 0)

    finish_gather()

    run_e0, ready_e0 = collect_transposed(0, 0, eb.at[0])

    def gap_dot():
        run_e0()

        @on1
        def _():
            down2(1, 0)
            small_heads(1, small1)

        @on0
        def _():
            ready_u0()
            ready_e0()
            z_first(0)
            z_last(0, 0)

    def gap_chain(ready):
        @on1
        def _():
            up2(1, 1)
            small_seqs(small1)

        @on0
        def _():
            z_last(0, 1)
            ready()

        @first0
        def _():
            far[0][1][1].start()

    def gap_after():
        @on1
        def _():
            down1(1, 2, 1)

    def gap_join():
        @on0
        def _():
            z_last(0, 2)

        @last0
        def _():
            far[0][1][1].start()

        @on0
        def _():
            up1(0, 0)

    def gap_rs(ready):
        got["bc0"] = bc_start(0)

        @on0
        def _():
            ready()

        @end0
        def _():
            far[0][1][2].start()

        @on0
        def _():
            up1(0, 1)

        @on1
        def _():
            down2(1, 1)
            up2(1, 2)
            bc_out_start(ready_bc1, bc_to1)
            z_final(1, 0)

    rows = backward(0, gap_dot, gap_chain, gap_after, gap_join, gap_rs)
    put, finish_in = deliver(0)
    for q in range(parts_rs):
        put(q, rows[:, q * RW : (q + 1) * RW])
    small0 = small_start(0)
    ready_bc0 = bc_mid(0, got["bc0"])
    bc_to0, bc_g0 = bc_copies(0), bc_gather_copies(0)

    @on1
    def _():
        small_finish(small1)
        bc_sum(bc_to1, bc_g1)
        z_final(1, 1)
        down2(1, 2)
        bc_finish(bc_g1)
        z_final(1, 2)

    @on0
    def _():
        bc_out_start(ready_bc0, bc_to0)
        down1(0, 0)
        up1(0, 2)
        small_heads(0, small0)
        up2(0, 0)
        down1(0, 1)
        down2(0, 0)
        up2(0, 1)
        down1(0, 2)
        z_final(0, 0)
        small_seqs(small0)
        down2(0, 1)
        bc_sum(bc_to0, bc_g0)
        z_final(0, 1)
        up2(0, 2)
        down2(0, 2)
        small_finish(small0)
        bc_finish(bc_g0)
        z_final(0, 2)

    if DB % LANES == 0:
        z_saved(0)
    z_saved(2)
    finish_out()
    finish_in()
    save = links.local(ends, ends_out)
    save.start()
    save.wait()

    @pl.when(inside)
    def _():
        for i in range(n_seq - 1):
            z_sent(1, i)
            z_sent(2, i)

    @pl.when(is_first | (is_last & (c == 0)))
    def _():
        for i in range(n_seq - 1):
            z_sent(0, i)

    for l, copy in lt_sends:

        @pl.when(c != l)
        def _():
            copy.wait_send()

    for slot in range(2):
        for copy in rs_copies[slot]:
            copy.wait_send()
    links.drain()


def run_layers(tokens, cotangent, w_xz, w_bc, w_dt, w_out, in_gain, in_conv_x, in_conv_bc, in_head, in_out):
    n_seq, n_head = lax.axis_size("seq"), lax.axis_size("head")
    _, T, D = tokens.shape
    I = w_xz.shape[2]
    N = w_bc.shape[1] // 2
    heads = in_head.shape[2]
    XB = I + 2 * N
    G = 2 * I + 2 * N + LANES
    Q = T // n_head
    DB = D // n_seq
    BR = 2 * N // n_head + (heads + 15) // 16 * 16
    sems = 160 + 4 * (n_seq + n_head)
    S = jax.ShapeDtypeStruct
    V = pltpu.VMEM
    dma = pltpu.SemaphoreType.DMA
    vm = pl.BlockSpec(memory_space=pltpu.VMEM)
    hbm = pl.BlockSpec(memory_space=pl.ANY)
    scratch = [
        V((2, 2, D, I), BF16), V((2, D, 2 * N), BF16), V((2, LANES, D), BF16), V((2, I, D), BF16),
        V((2, 8, D), F32), V((2, T, D), BF16), V((2, T, D), BF16), V((T, D), BF16),
        V((2, T + EDGE, XB), BF16), V((2, T, I), F32), V((2, T, XB), F32),
        V((T, I), F32), V((T, I), F32), V((2, T, I), F32),
        V((2, T, LANES), F32), V((2, T, LANES), F32), V((2, T, LANES), F32), V((2, LANES, T), F32),
        V((2, N, T), BF16), V((2, N, T), BF16), V((2, T, N), BF16), V((2, T, N), BF16),
        V((2, N, I), F32), V((2, N, I), F32), V((T, I), BF16), V((T, I), BF16),
        V((2, T, LANES), F32),
        V((T, I), F32), V((T, I), F32), V((T, I), BF16), V((T, I), BF16),
        V((N, I), F32), V((N, I), F32), V((T + EDGE, XB), F32),
        V((T, T), F32), V((2, T, G), BF16), V((2, T, I), BF16), V((2, 8, D), F32),
        V((4, 8, T), F32), V((4, n_head - 1, 8, T), F32),
        V((2, T, D), BF16), V((2, n_head - 1, Q, D), BF16),
        V((4, 6, N, I // 6), BF16), V((4, 6, N, I // 6), BF16),
        V((2, EDGE, XB), BF16), V((2, EDGE, XB), BF16),
        V((Q, D), F32), V((2, Q, D), F32), V((I, LANES), BF16), V((T, T), F32),
        V((2, 2, D, T), BF16), V((D, T), BF16), V((3, 2, T, I), BF16),
        V((2, n_seq - 1, DB, I), BF16), V((2, DB, I), BF16), V((DB, I), F32), V((I, DB), F32),
        V((2, DB, T), BF16), V((2, T, I), BF16),
        V((2, n_head - 1, 2 * N // n_head, T), BF16), V((2, 2 * N, T), BF16), V((2, BR, T), BF16),
        V((2, BR, T), BF16), V((n_seq - 1, BR, DB), BF16), V((n_seq - 1, BR, DB), BF16),
        V((n_head, 2 * N // n_head, DB), F32),
        V((8, D), F32), V((8, D), F32), V((n_head - 1, 8, D), F32), V((8, D), F32),
        V((n_seq - 1, 8, D), F32),
        dma((24,)), dma((sems,)), dma((sems,)),
        dma((3 * (n_seq - 1),)), dma((3 * (n_seq + 1),)), dma((6,)),
    ]
    dims = (n_seq, n_head, T, D, I, N, heads)
    return pl.pallas_call(
        functools.partial(layer_kernel, dims),
        out_shape=(
            S((2, Q, D), F32), S((I, DB) if DB % LANES == 0 else (DB, I), F32), S((2, DB, I), F32),
            S((DB, 2 * N) if DB % LANES == 0 else (2 * N, DB), F32), S((heads, 1, DB), F32),
            S((1, D), F32), S((5, 1, I), F32), S((5, 1, 2 * N), F32), S((3, 1, heads), F32),
            S((1, I), F32),
            S((3, n_seq + 1, DB, I), BF16), S((2, 2, D, T), BF16), S((3, 2, T, I), BF16),
        ),
        in_specs=[hbm] * 6 + [vm] * 5,
        out_specs=(hbm, hbm, hbm, vm, vm, vm, vm, vm, vm, vm, hbm, hbm, hbm),
        scratch_shapes=scratch,
        compiler_params=pltpu.CompilerParams(
            collective_id=0, has_side_effects=True, vmem_limit_bytes=63 * 2**20
        ),
        name="layers",
    )(
        tokens, cotangent, w_xz, w_bc, w_dt, w_out, in_gain, in_conv_x, in_conv_bc, in_head, in_out
    )[:10]


def body(
    tokens, cotangent, norm_gain, w_xz, w_bc, w_dt, conv_x, conv_bc, head_params, out_gain, w_out
):
    heads = w_dt.shape[2]
    dt_rows = jnp.pad(w_dt[0].T, ((0, LANES - heads), (0, 0)))
    ends, gw_out, gw_xz, gw_bc, gw_dt, g_gain, g_conv_x, g_conv_bc, g_head, g_out = run_layers(
        tokens,
        cotangent,
        jnp.swapaxes(w_xz[0], 0, 1),
        w_bc[0],
        dt_rows,
        w_out[0],
        norm_gain,
        jnp.swapaxes(conv_x, 0, 1),
        jnp.swapaxes(conv_bc, 0, 1),
        jnp.swapaxes(head_params, 0, 1),
        out_gain,
    )
    if gw_bc.shape[1] != w_bc.shape[2]:
        gw_bc = gw_bc.T
        gw_out = gw_out.T
    return (
        ends[None],
        g_gain,
        jnp.swapaxes(gw_xz, 0, 1)[None],
        gw_bc[None],
        jnp.transpose(gw_dt, (1, 2, 0)),
        jnp.swapaxes(g_conv_x, 0, 1),
        jnp.swapaxes(g_conv_bc, 0, 1),
        jnp.swapaxes(g_head, 0, 1),
        g_out,
        gw_out[None],
    )


def solution(mesh):
    placed = (
        P(None, "seq", None),
        P(None, "seq", None),
        P("section", None),
        P("section", None, None, "head"),
        P("section", None, None),
        P("section", None, "head"),
        P("section", None, "head"),
        P("section", None, None),
        P("section", None, "head"),
        P("section", "head"),
        P("section", "head", None),
    )
    return jax.shard_map(
        body,
        mesh=mesh,
        in_specs=placed,
        out_specs=(
            P("section", None, ("seq", "head"), None),
            P("section", None),
            P("section", "seq", None, "head"),
            P("section", "seq", None),
            P("section", "seq", "head"),
            P("section", None, "head"),
            P("section", None, None),
            P("section", None, "head"),
            P("section", "head"),
            P("section", "head", "seq"),
        ),
        check_vma=False,
    )
```
